32 devices in a mesh: groups: 2 (over x), seq: 8 (over z, y), chan: 2 (over core).
Axes of the slice: x: 2, y: 2, z: 4, core: 2. Of those that a mesh axis runs over, the one named last changes fastest.
Arguments:
- query_proj: bfloat16 [16384, 256], P(('groups', 'seq'), 'chan'), parts along dimension 0, may hold values from -6 to 6
- key_proj: bfloat16 [16384, 256], P(('groups', 'seq'), 'chan'), parts along dimension 0, may hold values from -6 to 6
- value_proj: bfloat16 [16384, 256], P(('groups', 'seq'), 'chan'), parts along dimension 0, may hold values from -6 to 6
- long_filter: float32 [8192, 256], P('seq', 'chan'), may hold values from -4 to 4
- skip_bias: float32 [256], P('chan'), may hold values from -4 to 4
Outputs:
- gated_out: bfloat16 [16384, 256], P(('groups', 'seq'), 'chan'), parts along dimension 0
The draws below stay inside these ranges and needn't reach their ends.
There are 2 independent parts, one for each index of `groups`. The reference program is written for one: setup_inputs(seed, part) draws one part's arguments, and reference() takes and returns one part's arrays. A program takes and returns all parts, laid end to end along the dimension named above; an argument that names none is the same for every part. Nothing has to cross between parts.
All inputs are finite; a program needn't handle non-finite values.
Results may differ from the reference program's by a relative error of at most 0.001.
Values sent between devices are 32-bit elements; how exact they have to be, the bound alone decides.
No kernel may reach another device: no remote copies, remote signals or barrier semaphores. Data moves between devices by JAX's collectives and lax.ppermute only.
A program may use at most 64 MiB of HBM per device.

```python
import jax
import jax.numpy as jnp

CHAN = 256
SEQ = 8192


def envelope_energy(lifetimes):
    return jnp.expm1(-2.0 * SEQ / lifetimes) / jnp.expm1(-2.0 / lifetimes)


def draw_long_filter(key, part):
    key_rate = jax.random.fold_in(key, 11)
    key_noise = jax.random.fold_in(key, 12)
    key_slow = jax.random.fold_in(key, 13)
    key_share = jax.random.fold_in(key, 14)
    positions = jnp.arange(SEQ, dtype=jnp.float32)[:, None]
    lifetimes = jnp.exp(jax.random.uniform(key_rate, (CHAN,), jnp.float32, jnp.log(32.0), jnp.log(4.0 * SEQ)))
    noise_vals = jax.random.truncated_normal(key_noise, -4.0, 4.0, (SEQ, CHAN), jnp.float32)
    slow_share = jax.random.uniform(key_share, (CHAN,), jnp.float32, 0.1, 0.3)
    slow_life = jnp.exp(jax.random.uniform(key_slow, (CHAN,), jnp.float32, jnp.log(SEQ / 2.0), jnp.log(4.0 * SEQ)))
    fast_part = jnp.exp(-positions / lifetimes[None, :]) * jnp.sqrt((1.0 - slow_share) / envelope_energy(lifetimes))[None, :]
    slow_part = jnp.exp(-positions / slow_life[None, :]) * jnp.sqrt(slow_share / envelope_energy(slow_life))[None, :]
    return (noise_vals * (fast_part + slow_part)).astype(jnp.float32)


def steps_of(own_key, dims, cuts, smallest, top_value):
    factor_of = 1.0
    for dim, parts in cuts:
        steps = jax.random.uniform(jax.random.fold_in(jax.random.fold_in(own_key, 6), dim), (parts,), jnp.float32, smallest / len(cuts), top_value / len(cuts))
        factor_of = factor_of * jnp.repeat(jnp.exp(steps), dims[dim] // parts).reshape((-1,) + (1,) * (len(dims) - 1 - dim))
    return factor_of


def noise(key, extent, width, most, pieces=(), kind=jnp.bfloat16):
    array = width * jax.random.normal(key, extent, jnp.float32)
    if pieces:
        array = array * steps_of(key, extent, pieces, -0.22, 0.18)
    return jnp.clip(array, -most, most).astype(kind)


def setup_inputs(seed: int = 0, part: int = 0) -> dict:
    streams_of = jax.random.split(jax.random.key(seed), 6)
    own_keys = jax.random.split(jax.random.fold_in(streams_of[5], part), 6)
    query_proj = noise(own_keys[0], (SEQ, CHAN), 1.0, 6.0, ((0, 8), (1, 2)))
    key_proj = noise(own_keys[1], (SEQ, CHAN), 1.0, 6.0, ((0, 8), (1, 2)))
    value_proj = noise(own_keys[2], (SEQ, CHAN), 1.0, 6.0, ((0, 8), (1, 2)))
    long_filter = draw_long_filter(jax.random.fold_in(streams_of[5], 71), part)
    skip_bias = noise(streams_of[4], (CHAN,), 1.0, 4.0, ((0, 2),), jnp.float32)
    return {"query_proj": query_proj, "key_proj": key_proj, "value_proj": value_proj, "long_filter": long_filter, "skip_bias": skip_bias}


def reference(query_proj, key_proj, value_proj, long_filter, skip_bias):
    driver = key_proj.astype(jnp.float32) * value_proj.astype(jnp.float32)
    seq_len = driver.shape[0]
    padded_len = 2 * seq_len
    spectrum = jnp.fft.rfft(driver, n=padded_len, axis=0) * jnp.fft.rfft(long_filter, n=padded_len, axis=0)
    convolved = jnp.fft.irfft(spectrum, n=padded_len, axis=0)[:seq_len]
    gated = query_proj.astype(jnp.float32) * (convolved + skip_bias[None, :] * driver)
    return gated.astype(jnp.bfloat16)
```

```python
import functools

import jax
import jax.numpy as jnp
import ml_dtypes
import numpy as np
from jax import lax
from jax.experimental import pallas as pl
from jax.experimental.pallas import tpu as pltpu
from jax.sharding import PartitionSpec as P

LANES = 128
BF16 = jnp.bfloat16
F32 = jnp.float32
VMEM_LIMIT = 48 * 2**20


def split_np(table):
    high = table.astype(np.float32).astype(ml_dtypes.bfloat16)
    low = (table - high.astype(np.float64)).astype(np.float32).astype(ml_dtypes.bfloat16)
    return high, low


def make_tables(seq_len):
    outer = seq_len // LANES
    n_out, k_out = np.meshgrid(np.arange(outer), np.arange(outer), indexing="ij")
    head = np.exp(-2j * np.pi * (n_out * (4 * k_out + 1) % (4 * outer)) / (4 * outer))
    n_in = np.arange(LANES)
    twist = np.exp(-2j * np.pi * np.outer(4 * np.arange(outer) + 1, n_in) / (4 * seq_len))
    tail = np.exp(-2j * np.pi * (np.outer(n_in, n_in) % LANES) / LANES)

    def block(mat):
        return np.block([[mat.real, mat.imag], [-mat.imag, mat.real]])

    fwd_head = np.concatenate([head.real.T, head.imag.T], axis=0)
    high, low = split_np(fwd_head)
    head_tab = np.concatenate([high, high, low], axis=1)
    high, low = split_np(block(tail))
    tail_tab = np.concatenate([high, high, low], axis=0)
    high, low = split_np(block(tail.conj()))
    back_tail_tab = np.concatenate([high, high, low], axis=0)
    high, low = split_np(np.concatenate([head.real, head.imag], axis=1))
    back_head_tab = np.concatenate([high, high, low], axis=1)
    twist_tab = np.concatenate([twist.real, twist.imag], axis=1).astype(np.float32)
    return head_tab, twist_tab, tail_tab, back_tail_tab, back_head_tab


def halves(values):
    high = values.astype(BF16)
    return high, (values - high.astype(F32)).astype(BF16)


def by_rows(values):
    high, low = halves(values)
    return jnp.concatenate([high, low, high], axis=0)


def by_lanes(values):
    high, low = halves(values)
    return jnp.concatenate([high, low, high], axis=1)


def mat(left, right):
    return jnp.dot(left, right, preferred_element_type=F32)


def forward(signals, head, twist, tail):
    outer = signals[0].shape[0]
    mixed = mat(head, by_rows(jnp.concatenate(signals, axis=1)))
    cos, sin = twist[:, :LANES], twist[:, LANES:]
    rows = []
    for idx in range(len(signals)):
        real = mixed[:outer, idx * LANES : (idx + 1) * LANES]
        imag = mixed[outer:, idx * LANES : (idx + 1) * LANES]
        rows.append(jnp.concatenate([real * cos - imag * sin, real * sin + imag * cos], axis=1))
    return mat(by_lanes(jnp.concatenate(rows, axis=0)), tail)


def pack_kernel(rows, key_ref, value_ref, out_ref):
    for row in range(rows):
        span = pl.ds(row * LANES, LANES)
        driver = key_ref[span, :].astype(F32) * value_ref[span, :].astype(F32)
        out_ref[pl.ds(row, LANES, stride=rows), :] = driver.T


def pack_filter_kernel(rows, which_ref, filter_ref, out_ref, scratch):
    for row in range(rows):
        scratch[pl.ds(row, LANES, stride=rows), :] = filter_ref[pl.ds(row * LANES, LANES), :].T
    size = out_ref.shape[0]
    start = pl.multiple_of(which_ref[0] * size, size)
    out_ref[...] = scratch[pl.ds(start, size), :]


def filter_kernel(own, filter_ref, head_ref, twist_ref, tail_ref, out_ref):
    blocks, rows = filter_ref.shape[0], filter_ref.shape[2]
    signals = [filter_ref[:, chan].reshape(blocks * rows, LANES) for chan in range(own)]
    out_ref[...] = forward(signals, head_ref[...], twist_ref[...], tail_ref[...])


def conv_kernel(own, driver_ref, spec_ref, head_ref, twist_ref, tail_ref, back_tail_ref, back_head_ref, out_ref):
    groups, blocks, _, rows = driver_ref.shape[:4]
    outer = blocks * rows
    scale = 1.0 / (outer * LANES)
    signals = [
        driver_ref[group, :, chan].reshape(outer, LANES) for chan in range(own) for group in range(groups)
    ]
    spec = forward(signals, head_ref[...], twist_ref[...], tail_ref[...])
    prods = []
    for idx in range(len(signals)):
        own_spec = spec_ref[pl.ds(idx // groups * outer, outer), :]
        f_re, f_im = own_spec[:, :LANES], own_spec[:, LANES:]
        mine = spec[idx * outer : (idx + 1) * outer]
        d_re, d_im = mine[:, :LANES], mine[:, LANES:]
        prods.append(jnp.concatenate([d_re * f_re - d_im * f_im, d_re * f_im + d_im * f_re], axis=1))
    back = mat(by_lanes(jnp.concatenate(prods, axis=0)), back_tail_ref[...])
    cos, sin = twist_ref[:, :LANES] * scale, twist_ref[:, LANES:] * scale
    reals, imags = [], []
    for idx in range(len(signals)):
        mine = back[idx * outer : (idx + 1) * outer]
        real, imag = mine[:, :LANES], mine[:, LANES:]
        reals.append(real * cos + imag * sin)
        imags.append(imag * cos - real * sin)
    mixed = jnp.concatenate([jnp.concatenate(reals, axis=1), jnp.concatenate(imags, axis=1)], axis=0)
    result = mat(back_head_ref[...], by_rows(mixed))
    for idx in range(len(signals)):
        chan, group = divmod(idx, groups)
        out_ref[group, :, chan] = result[:, idx * LANES : (idx + 1) * LANES].reshape(blocks, rows, LANES)


def gate_kernel(rows, conv_ref, query_ref, key_ref, value_ref, bias_ref, out_ref):
    bias = bias_ref[...]
    for row in range(rows):
        span = pl.ds(row * LANES, LANES)
        driver = key_ref[span, :].astype(F32) * value_ref[span, :].astype(F32)
        convolved = conv_ref[pl.ds(row, LANES, stride=rows), :].T
        out_ref[span, :] = (query_ref[span, :].astype(F32) * (convolved + bias * driver)).astype(BF16)


VMEM = pl.BlockSpec(memory_space=pltpu.VMEM)
SMEM = pl.BlockSpec(memory_space=pltpu.SMEM)


def call(kernel, shape, dtype, specs, flops, moved, scratch=()):
    return pl.pallas_call(
        kernel,
        out_shape=jax.ShapeDtypeStruct(shape, dtype),
        in_specs=specs,
        out_specs=VMEM,
        scratch_shapes=scratch,
        compiler_params=pltpu.CompilerParams(vmem_limit_bytes=VMEM_LIMIT),
        cost_estimate=pl.CostEstimate(flops=flops, bytes_accessed=moved, transcendentals=0),
    )


def shards(groups, blocks, query_proj, key_proj, value_proj, long_filter, skip_bias):
    tokens, chans = key_proj.shape
    rows = tokens // LANES
    own = chans // (groups * blocks)
    outer = blocks * rows
    seq_len = blocks * tokens
    tables = make_tables(seq_len)
    head, twist, tail, back_tail, back_head = (jnp.asarray(table) for table in tables)
    size = tokens * chans * 4

    packed_filter = call(
        functools.partial(pack_filter_kernel, rows),
        (blocks * own * rows, LANES), F32, [SMEM, VMEM], 0, size * 2,
        [pltpu.VMEM((chans * rows, LANES), F32)],
    )(lax.axis_index("groups").reshape(1).astype(jnp.int32), long_filter)
    packed = call(functools.partial(pack_kernel, rows), (chans * rows, LANES), F32, [VMEM, VMEM], size // 4, size * 2)(
        key_proj, value_proj
    )
    moved_filter = lax.all_to_all(packed_filter, "seq", 0, 0, tiled=True)
    moved = lax.all_to_all(packed, ("groups", "seq"), 0, 0, tiled=True)
    macs = 2 * 3 * own * seq_len * (2 * outer + 4 * LANES)
    spec = call(
        functools.partial(filter_kernel, own), (own * outer, 2 * LANES), F32, [VMEM] * 4, macs, size
    )(moved_filter.reshape(blocks, own, rows, LANES), head, twist, tail)
    local = call(
        functools.partial(conv_kernel, own),
        (groups, blocks, own, rows, LANES), F32, [VMEM] * 7, 4 * macs, 3 * size,
    )(moved.reshape(groups, blocks, own, rows, LANES), spec, head, twist, tail, back_tail, back_head)
    convolved = lax.all_to_all(local.reshape(chans * rows, LANES), ("groups", "seq"), 0, 0, tiled=True)
    return call(functools.partial(gate_kernel, rows), (tokens, chans), BF16, [VMEM] * 5, size, 3 * size)(
        convolved, query_proj, key_proj, value_proj, skip_bias.reshape(1, chans)
    )


def solution(mesh):
    placed = (
        P(("groups", "seq"), "chan"),
        P(("groups", "seq"), "chan"),
        P(("groups", "seq"), "chan"),
        P("seq", "chan"),
        P("chan"),
    )
    body = functools.partial(shards, mesh.shape["groups"], mesh.shape["seq"])
    return jax.shard_map(
        body, mesh=mesh, in_specs=placed, out_specs=P(("groups", "seq"), "chan"), check_vma=False
    )
```

```python
import functools

import jax
import jax.numpy as jnp
import ml_dtypes
import numpy as np
from jax import lax
from jax.experimental import pallas as pl
from jax.experimental.pallas import tpu as pltpu
from jax.sharding import PartitionSpec as P

LANES = 128
BF16 = jnp.bfloat16
F32 = jnp.float32
VMEM_LIMIT = 48 * 2**20


def split_np(table):
    high = table.astype(np.float32).astype(ml_dtypes.bfloat16)
    low = (table - high.astype(np.float64)).astype(np.float32).astype(ml_dtypes.bfloat16)
    return high, low


def make_tables(seq_len):
    outer = seq_len // LANES
    n_out, k_out = np.meshgrid(np.arange(outer), np.arange(outer), indexing="ij")
    head = np.exp(-2j * np.pi * (n_out * (4 * k_out + 1) % (4 * outer)) / (4 * outer))
    n_in = np.arange(LANES)
    twist = np.exp(-2j * np.pi * np.outer(4 * np.arange(outer) + 1, n_in) / (4 * seq_len))
    tail = np.exp(-2j * np.pi * (np.outer(n_in, n_in) % LANES) / LANES)

    def block(mat):
        return np.block([[mat.real, mat.imag], [-mat.imag, mat.real]])

    fwd_head = np.concatenate([head.real.T, head.imag.T], axis=0)
    high, low = split_np(fwd_head)
    head_tab = np.concatenate([high, high, low], axis=1)
    high, low = split_np(block(tail))
    tail_tab = np.concatenate([high, high, low], axis=0)
    high, low = split_np(block(tail.conj()))
    back_tail_tab = np.concatenate([high, high, low], axis=0)
    high, low = split_np(np.concatenate([head.real, head.imag], axis=1))
    back_head_tab = np.concatenate([high, high, low], axis=1)
    twist_tab = np.concatenate([twist.real, twist.imag], axis=1).astype(np.float32)
    return head_tab, twist_tab, tail_tab, back_tail_tab, back_head_tab


def halves(values):
    high = values.astype(BF16)
    return high, (values - high.astype(F32)).astype(BF16)


def by_rows(values):
    high, low = halves(values)
    return jnp.concatenate([high, low, high], axis=0)


def by_lanes(values):
    high, low = halves(values)
    return jnp.concatenate([high, low, high], axis=1)


def mat(left, right):
    return jnp.dot(left, right, preferred_element_type=F32)


def forward(signals, head, twist, tail):
    outer = signals[0].shape[0]
    mixed = mat(head, by_rows(jnp.concatenate(signals, axis=1)))
    cos, sin = twist[:, :LANES], twist[:, LANES:]
    rows = []
    for idx in range(len(signals)):
        real = mixed[:outer, idx * LANES : (idx + 1) * LANES]
        imag = mixed[outer:, idx * LANES : (idx + 1) * LANES]
        rows.append(jnp.concatenate([real * cos - imag * sin, real * sin + imag * cos], axis=1))
    return mat(by_lanes(jnp.concatenate(rows, axis=0)), tail)


def pack_kernel(rows, own, share, which_ref, key_ref, value_ref, filter_ref, out_ref, turned):
    for row in range(rows):
        span = pl.ds(row * LANES, LANES)
        turned[0, pl.ds(row, LANES, stride=rows), :] = (
            key_ref[span, :].astype(F32) * value_ref[span, :].astype(F32)
        ).T
        turned[1, pl.ds(row, LANES, stride=rows), :] = filter_ref[span, :].T
    first = which_ref[0] * (share * rows if share < own else 0)
    for peer in range(out_ref.shape[0]):
        start = peer * own * rows
        out_ref[peer, : own * rows] = turned[0, pl.ds(start, own * rows), :]
        taken = pl.ds(pl.multiple_of(start + first, rows), share * rows)
        out_ref[peer, own * rows :] = turned[1, taken, :]


def conv_kernel(rows, own, share, moved_ref, head_ref, twist_ref, tail_ref, back_tail_ref, back_head_ref, out_ref):
    groups, blocks = moved_ref.shape[:2]
    outer = blocks * rows
    scale = 1.0 / (outer * LANES)

    def signal(group, place):
        return moved_ref[group, :, place * rows : (place + 1) * rows].reshape(outer, LANES)

    signals = [signal(chan // share, own + chan % share) for chan in range(own)]
    signals += [signal(group, chan) for chan in range(own) for group in range(groups)]
    spec = forward(signals, head_ref[...], twist_ref[...], tail_ref[...])
    pieces = [spec[idx * outer : (idx + 1) * outer] for idx in range(len(signals))]
    prods = []
    for idx, mine in enumerate(pieces[own:]):
        other = pieces[idx // groups]
        f_re, f_im = other[:, :LANES], other[:, LANES:]
        d_re, d_im = mine[:, :LANES], mine[:, LANES:]
        prods.append(jnp.concatenate([d_re * f_re - d_im * f_im, d_re * f_im + d_im * f_re], axis=1))
    back = mat(by_lanes(jnp.concatenate(prods, axis=0)), back_tail_ref[...])
    cos, sin = twist_ref[:, :LANES] * scale, twist_ref[:, LANES:] * scale
    reals, imags = [], []
    for idx in range(len(prods)):
        mine = back[idx * outer : (idx + 1) * outer]
        real, imag = mine[:, :LANES], mine[:, LANES:]
        reals.append(real * cos + imag * sin)
        imags.append(imag * cos - real * sin)
    mixed = jnp.concatenate([jnp.concatenate(reals, axis=1), jnp.concatenate(imags, axis=1)], axis=0)
    result = mat(back_head_ref[...], by_rows(mixed))
    for idx in range(len(prods)):
        chan, group = divmod(idx, groups)
        out_ref[group, :, chan] = result[:, idx * LANES : (idx + 1) * LANES].reshape(blocks, rows, LANES)


def gate_kernel(rows, conv_ref, query_ref, key_ref, value_ref, bias_ref, out_ref):
    bias = bias_ref[...]
    for row in range(rows):
        span = pl.ds(row * LANES, LANES)
        driver = key_ref[span, :].astype(F32) * value_ref[span, :].astype(F32)
        convolved = conv_ref[pl.ds(row, LANES, stride=rows), :].T
        out_ref[span, :] = (query_ref[span, :].astype(F32) * (convolved + bias * driver)).astype(BF16)


VMEM = pl.BlockSpec(memory_space=pltpu.VMEM)
SMEM = pl.BlockSpec(memory_space=pltpu.SMEM)


def call(kernel, shape, dtype, specs, flops, moved, scratch=()):
    return pl.pallas_call(
        kernel,
        out_shape=jax.ShapeDtypeStruct(shape, dtype),
        in_specs=specs,
        out_specs=VMEM,
        scratch_shapes=scratch,
        compiler_params=pltpu.CompilerParams(vmem_limit_bytes=VMEM_LIMIT),
        cost_estimate=pl.CostEstimate(flops=flops, bytes_accessed=moved, transcendentals=0),
    )


def shards(groups, blocks, query_proj, key_proj, value_proj, long_filter, skip_bias):
    tokens, chans = key_proj.shape
    rows = tokens // LANES
    own = chans // (groups * blocks)
    outer = blocks * rows
    seq_len = blocks * tokens
    tables = make_tables(seq_len)
    head, twist, tail, back_tail, back_head = (jnp.asarray(table) for table in tables)
    size = tokens * chans * 4

    share = own // groups if own % groups == 0 else own
    packed = call(
        functools.partial(pack_kernel, rows, own, share),
        (groups * blocks, (own + share) * rows, LANES), F32, [SMEM, VMEM, VMEM, VMEM], size // 4, size * 4,
        [pltpu.VMEM((2, chans * rows, LANES), F32)],
    )(lax.axis_index("groups").reshape(1).astype(jnp.int32), key_proj, value_proj, long_filter)
    moved = lax.all_to_all(packed, ("groups", "seq"), 0, 0, tiled=True)
    macs = 2 * 3 * own * seq_len * (2 * outer + 4 * LANES)
    local = call(
        functools.partial(conv_kernel, rows, own, share),
        (groups, blocks, own, rows, LANES), F32, [VMEM] * 6, 5 * macs, 3 * size,
    )(moved.reshape(groups, blocks, (own + share) * rows, LANES), head, twist, tail, back_tail, back_head)
    convolved = lax.all_to_all(local.reshape(chans * rows, LANES), ("groups", "seq"), 0, 0, tiled=True)
    return call(functools.partial(gate_kernel, rows), (tokens, chans), BF16, [VMEM] * 5, size, 3 * size)(
        convolved, query_proj, key_proj, value_proj, skip_bias.reshape(1, chans)
    )


def solution(mesh):
    placed = (
        P(("groups", "seq"), "chan"),
        P(("groups", "seq"), "chan"),
        P(("groups", "seq"), "chan"),
        P("seq", "chan"),
        P("chan"),
    )
    body = functools.partial(shards, mesh.shape["groups"], mesh.shape["seq"])
    return jax.shard_map(
        body, mesh=mesh, in_specs=placed, out_specs=P(("groups", "seq"), "chan"), check_vma=False
    )
```

```python
import functools

import jax
import jax.numpy as jnp
import ml_dtypes
import numpy as np
from jax import lax
from jax.experimental import pallas as pl
from jax.experimental.pallas import tpu as pltpu
from jax.sharding import PartitionSpec as P

LANES = 128
BF16 = jnp.bfloat16
F32 = jnp.float32
VMEM_LIMIT = 48 * 2**20


def split_np(table):
    high = table.astype(np.float32).astype(ml_dtypes.bfloat16)
    low = (table - high.astype(np.float64)).astype(np.float32).astype(ml_dtypes.bfloat16)
    return high, low


def make_tables(seq_len):
    outer = seq_len // LANES
    n_out, k_out = np.meshgrid(np.arange(outer), np.arange(outer), indexing="ij")
    head = np.exp(-2j * np.pi * (n_out * (4 * k_out + 1) % (4 * outer)) / (4 * outer))
    n_in = np.arange(LANES)
    twist = np.exp(-2j * np.pi * np.outer(4 * np.arange(outer) + 1, n_in) / (4 * seq_len))
    tail = np.exp(-2j * np.pi * (np.outer(n_in, n_in) % LANES) / LANES)

    def block(mat):
        return np.block([[mat.real, mat.imag], [-mat.imag, mat.real]])

    fwd_head = np.concatenate([head.real.T, head.imag.T], axis=0)
    high, low = split_np(fwd_head)
    head_tab = np.concatenate([high, high, low], axis=1)
    high, low = split_np(block(tail))
    tail_tab = np.concatenate([high, high, low], axis=0)
    high, low = split_np(block(tail.conj()))
    back_tail_tab = np.concatenate([high, high, low], axis=0)
    high, low = split_np(np.concatenate([head.real, head.imag], axis=1))
    back_head_tab = np.concatenate([high, high, low], axis=1)
    twist_tab = np.concatenate([twist.real, twist.imag], axis=1).astype(np.float32)
    return head_tab, twist_tab, tail_tab, back_tail_tab, back_head_tab


def halves(values):
    high = values.astype(BF16)
    return high, (values - high.astype(F32)).astype(BF16)


def by_rows(values):
    high, low = halves(values)
    return jnp.concatenate([high, low, high], axis=0)


def by_lanes(values):
    high, low = halves(values)
    return jnp.concatenate([high, low, high], axis=1)


def mat(left, right):
    return jnp.dot(left, right, preferred_element_type=F32)


def forward(signals, head, twist, tail):
    outer = signals[0].shape[0]
    mixed = mat(head, by_rows(jnp.concatenate(signals, axis=1)))
    cos, sin = twist[:, :LANES], twist[:, LANES:]
    rows = []
    for idx in range(len(signals)):
        real = mixed[:outer, idx * LANES : (idx + 1) * LANES]
        imag = mixed[outer:, idx * LANES : (idx + 1) * LANES]
        rows.append(jnp.concatenate([real * cos - imag * sin, real * sin + imag * cos], axis=1))
    return mat(by_lanes(jnp.concatenate(rows, axis=0)), tail)


def pack_kernel(rows, own, share, which_ref, *refs):
    sources, bias_ref, out_ref, bias_out = refs[:3], refs[3], refs[4], refs[5]
    held, turned, sems = refs[6:9], refs[9], refs[10]

    def fetch(place, row):
        span = pl.ds(row * LANES, LANES)
        return pltpu.make_async_copy(sources[place].at[span], held[place].at[span], sems.at[place, row])

    for row in range(rows):
        for place in range(3):
            fetch(place, row).start()
    bias_out[...] = bias_ref[...]
    for row in range(rows):
        span = pl.ds(row * LANES, LANES)
        fetch(0, row).wait()
        fetch(1, row).wait()
        driver = held[0][span, :].astype(F32) * held[1][span, :].astype(F32)
        turned[0, pl.ds(row, LANES, stride=rows), :] = driver.T
        fetch(2, row).wait()
        turned[1, pl.ds(row, LANES, stride=rows), :] = held[2][span, :].T
    first = which_ref[0] * (share * rows if share < own else 0)
    for peer in range(out_ref.shape[0]):
        start = peer * own * rows
        out_ref[peer, : own * rows] = turned[0, pl.ds(start, own * rows), :]
        taken = pl.ds(pl.multiple_of(start + first, rows), share * rows)
        out_ref[peer, own * rows :] = turned[1, taken, :]


def conv_kernel(rows, own, share, moved_ref, head_ref, twist_ref, tail_ref, back_tail_ref, back_head_ref, out_ref):
    groups, blocks = moved_ref.shape[:2]
    outer = blocks * rows
    scale = 1.0 / (outer * LANES)

    def signal(group, place):
        return moved_ref[group, :, place * rows : (place + 1) * rows].reshape(outer, LANES)

    signals = [signal(chan // share, own + chan % share) for chan in range(own)]
    signals += [signal(group, chan) for chan in range(own) for group in range(groups)]
    spec = forward(signals, head_ref[...], twist_ref[...], tail_ref[...])
    pieces = [spec[idx * outer : (idx + 1) * outer] for idx in range(len(signals))]
    prods = []
    for idx, mine in enumerate(pieces[own:]):
        other = pieces[idx // groups]
        f_re, f_im = other[:, :LANES], other[:, LANES:]
        d_re, d_im = mine[:, :LANES], mine[:, LANES:]
        prods.append(jnp.concatenate([d_re * f_re - d_im * f_im, d_re * f_im + d_im * f_re], axis=1))
    back = mat(by_lanes(jnp.concatenate(prods, axis=0)), back_tail_ref[...])
    cos, sin = twist_ref[:, :LANES] * scale, twist_ref[:, LANES:] * scale
    reals, imags = [], []
    for idx in range(len(prods)):
        mine = back[idx * outer : (idx + 1) * outer]
        real, imag = mine[:, :LANES], mine[:, LANES:]
        reals.append(real * cos + imag * sin)
        imags.append(imag * cos - real * sin)
    mixed = jnp.concatenate([jnp.concatenate(reals, axis=1), jnp.concatenate(imags, axis=1)], axis=0)
    result = mat(back_head_ref[...], by_rows(mixed))
    for idx in range(len(prods)):
        chan, group = divmod(idx, groups)
        out_ref[group, :, chan] = result[:, idx * LANES : (idx + 1) * LANES].reshape(blocks, rows, LANES)


def gate_kernel(rows, conv_ref, query_ref, key_ref, value_ref, bias_ref, out_ref):
    bias = bias_ref[...]
    for row in range(rows):
        span = pl.ds(row * LANES, LANES)
        driver = key_ref[span, :].astype(F32) * value_ref[span, :].astype(F32)
        convolved = conv_ref[pl.ds(row, LANES, stride=rows), :].T
        out_ref[span, :] = (query_ref[span, :].astype(F32) * (convolved + bias * driver)).astype(BF16)


VMEM = pl.BlockSpec(memory_space=pltpu.VMEM)
ANY = pl.BlockSpec(memory_space=pl.ANY)
SMEM = pl.BlockSpec(memory_space=pltpu.SMEM)


def call(kernel, outs, specs, flops, moved, scratch=()):
    return pl.pallas_call(
        kernel,
        out_shape=[jax.ShapeDtypeStruct(*out) for out in outs],
        in_specs=specs,
        out_specs=[VMEM] * len(outs),
        scratch_shapes=scratch,
        compiler_params=pltpu.CompilerParams(vmem_limit_bytes=VMEM_LIMIT),
        cost_estimate=pl.CostEstimate(flops=flops, bytes_accessed=moved, transcendentals=0),
    )


def shards(groups, blocks, query_proj, key_proj, value_proj, long_filter, skip_bias):
    tokens, chans = key_proj.shape
    rows = tokens // LANES
    own = chans // (groups * blocks)
    outer = blocks * rows
    seq_len = blocks * tokens
    tables = make_tables(seq_len)
    head, twist, tail, back_tail, back_head = (jnp.asarray(table) for table in tables)
    size = tokens * chans * 4

    share = own // groups if own % groups == 0 else own
    packed, bias = call(
        functools.partial(pack_kernel, rows, own, share),
        [((groups * blocks, (own + share) * rows, LANES), F32), ((1, chans), F32)],
        [SMEM, ANY, ANY, ANY, VMEM], size // 4, size * 4,
        [pltpu.VMEM((tokens, chans), BF16), pltpu.VMEM((tokens, chans), BF16), pltpu.VMEM((tokens, chans), F32),
         pltpu.VMEM((2, chans * rows, LANES), F32), pltpu.SemaphoreType.DMA((3, rows))],
    )(lax.axis_index("groups").reshape(1).astype(jnp.int32), key_proj, value_proj, long_filter,
      skip_bias.reshape(1, chans))
    moved = lax.all_to_all(packed, ("groups", "seq"), 0, 0, tiled=True)
    macs = 2 * 3 * own * seq_len * (2 * outer + 4 * LANES)
    local = call(
        functools.partial(conv_kernel, rows, own, share),
        [((groups, blocks, own, rows, LANES), F32)], [VMEM] * 6, 5 * macs, 3 * size,
    )(moved.reshape(groups, blocks, (own + share) * rows, LANES), head, twist, tail, back_tail, back_head)[0]
    convolved = lax.all_to_all(local.reshape(chans * rows, LANES), ("groups", "seq"), 0, 0, tiled=True)
    return call(functools.partial(gate_kernel, rows), [((tokens, chans), BF16)], [VMEM] * 5, size, 3 * size)(
        convolved, query_proj, key_proj, value_proj, bias
    )[0]


def solution(mesh):
    placed = (
        P(("groups", "seq"), "chan"),
        P(("groups", "seq"), "chan"),
        P(("groups", "seq"), "chan"),
        P("seq", "chan"),
        P("chan"),
    )
    body = functools.partial(shards, mesh.shape["groups"], mesh.shape["seq"])
    return jax.shard_map(
        body, mesh=mesh, in_specs=placed, out_specs=P(("groups", "seq"), "chan"), check_vma=False
    )
```

```python
import functools

import jax
import jax.numpy as jnp
import ml_dtypes
import numpy as np
from jax import lax
from jax.experimental import pallas as pl
from jax.experimental.pallas import tpu as pltpu
from jax.sharding import PartitionSpec as P

LANES = 128
BF16 = jnp.bfloat16
F32 = jnp.float32
VMEM_LIMIT = 48 * 2**20


def split_np(table):
    high = table.astype(np.float32).astype(ml_dtypes.bfloat16)
    low = (table - high.astype(np.float64)).astype(np.float32).astype(ml_dtypes.bfloat16)
    return high, low


def make_tables(seq_len):
    outer = seq_len // LANES
    n_out, k_out = np.meshgrid(np.arange(outer), np.arange(outer), indexing="ij")
    head = np.exp(-2j * np.pi * (n_out * (4 * k_out + 1) % (4 * outer)) / (4 * outer))
    n_in = np.arange(LANES)
    twist = np.exp(-2j * np.pi * np.outer(4 * np.arange(outer) + 1, n_in) / (4 * seq_len))
    tail = np.exp(-2j * np.pi * (np.outer(n_in, n_in) % LANES) / LANES)

    def block(mat):
        return np.block([[mat.real, mat.imag], [-mat.imag, mat.real]])

    fwd_head = np.concatenate([head.real.T, head.imag.T], axis=0)
    high, low = split_np(fwd_head)
    head_tab = np.concatenate([high, high, low], axis=1)
    high, low = split_np(block(tail))
    tail_tab = np.concatenate([high, high, low], axis=0)
    high, low = split_np(block(tail.conj()))
    back_tail_tab = np.concatenate([high, high, low], axis=0)
    high, low = split_np(np.concatenate([head.real, head.imag], axis=1))
    back_head_tab = np.concatenate([high, high, low], axis=1)
    twist_tab = np.concatenate([twist.real, twist.imag], axis=1).astype(np.float32)
    return head_tab, twist_tab, tail_tab, back_tail_tab, back_head_tab


def halves(values):
    high = values.astype(BF16)
    return high, (values - high.astype(F32)).astype(BF16)


def by_rows(values):
    high, low = halves(values)
    return jnp.concatenate([high, low, high], axis=0)


def by_lanes(values):
    high, low = halves(values)
    return jnp.concatenate([high, low, high], axis=1)


def mat(left, right):
    return jnp.dot(left, right, preferred_element_type=F32)


def forward(signals, head, twist, tail):
    outer = signals[0].shape[0]
    mixed = mat(head, by_rows(jnp.concatenate(signals, axis=1)))
    cos, sin = twist[:, :LANES], twist[:, LANES:]
    rows = []
    for idx in range(len(signals)):
        real = mixed[:outer, idx * LANES : (idx + 1) * LANES]
        imag = mixed[outer:, idx * LANES : (idx + 1) * LANES]
        rows.append(jnp.concatenate([real * cos - imag * sin, real * sin + imag * cos], axis=1))
    return mat(by_lanes(jnp.concatenate(rows, axis=0)), tail)


def pack_kernel(rows, own, share, which_ref, *refs):
    sources, bias_ref, out_ref, bias_out = refs[:3], refs[3], refs[4], refs[5]
    held, turned, sems, bias_sem = refs[6:9], refs[9], refs[10], refs[11]
    bias_copy = pltpu.make_async_copy(bias_ref, bias_out, bias_sem)

    def fetch(place, row):
        span = pl.ds(row * LANES, LANES)
        return pltpu.make_async_copy(sources[place].at[span], held[place].at[span], sems.at[place, row])

    for row in range(rows):
        for place in range(3):
            fetch(place, row).start()
    bias_copy.start()
    for row in range(rows):
        span = pl.ds(row * LANES, LANES)
        fetch(0, row).wait()
        fetch(1, row).wait()
        driver = held[0][span, :].astype(F32) * held[1][span, :].astype(F32)
        turned[0, pl.ds(row, LANES, stride=rows), :] = driver.T
        fetch(2, row).wait()
        turned[1, pl.ds(row, LANES, stride=rows), :] = held[2][span, :].T
    first = which_ref[0] * (share * rows if share < own else 0)
    for peer in range(out_ref.shape[0]):
        start = peer * own * rows
        out_ref[peer, : own * rows] = turned[0, pl.ds(start, own * rows), :]
        taken = pl.ds(pl.multiple_of(start + first, rows), share * rows)
        out_ref[peer, own * rows :] = turned[1, taken, :]
    bias_copy.wait()


def conv_kernel(rows, own, share, moved_ref, head_ref, twist_ref, tail_ref, back_tail_ref, back_head_ref, out_ref):
    groups, blocks = moved_ref.shape[:2]
    outer = blocks * rows
    scale = 1.0 / (outer * LANES)

    def signal(group, place):
        return moved_ref[group, :, place * rows : (place + 1) * rows].reshape(outer, LANES)

    signals = [signal(chan // share, own + chan % share) for chan in range(own)]
    signals += [signal(group, chan) for chan in range(own) for group in range(groups)]
    spec = forward(signals, head_ref[...], twist_ref[...], tail_ref[...])
    pieces = [spec[idx * outer : (idx + 1) * outer] for idx in range(len(signals))]
    prods = []
    for idx, mine in enumerate(pieces[own:]):
        other = pieces[idx // groups]
        f_re, f_im = other[:, :LANES], other[:, LANES:]
        d_re, d_im = mine[:, :LANES], mine[:, LANES:]
        prods.append(jnp.concatenate([d_re * f_re - d_im * f_im, d_re * f_im + d_im * f_re], axis=1))
    back = mat(by_lanes(jnp.concatenate(prods, axis=0)), back_tail_ref[...])
    cos, sin = twist_ref[:, :LANES] * scale, twist_ref[:, LANES:] * scale
    reals, imags = [], []
    for idx in range(len(prods)):
        mine = back[idx * outer : (idx + 1) * outer]
        real, imag = mine[:, :LANES], mine[:, LANES:]
        reals.append(real * cos + imag * sin)
        imags.append(imag * cos - real * sin)
    mixed = jnp.concatenate([jnp.concatenate(reals, axis=1), jnp.concatenate(imags, axis=1)], axis=0)
    result = mat(back_head_ref[...], by_rows(mixed))
    for idx in range(len(prods)):
        chan, group = divmod(idx, groups)
        out_ref[group, :, chan] = result[:, idx * LANES : (idx + 1) * LANES].reshape(blocks, rows, LANES)


def gate_kernel(rows, conv_ref, query_ref, key_ref, value_ref, bias_ref, out_ref):
    bias = bias_ref[...]
    for row in range(rows):
        span = pl.ds(row * LANES, LANES)
        driver = key_ref[span, :].astype(F32) * value_ref[span, :].astype(F32)
        convolved = conv_ref[pl.ds(row, LANES, stride=rows), :].T
        out_ref[span, :] = (query_ref[span, :].astype(F32) * (convolved + bias * driver)).astype(BF16)


VMEM = pl.BlockSpec(memory_space=pltpu.VMEM)
HBM = pl.BlockSpec(memory_space=pltpu.HBM)
SMEM = pl.BlockSpec(memory_space=pltpu.SMEM)


def call(kernel, outs, specs, flops, moved, scratch=()):
    return pl.pallas_call(
        kernel,
        out_shape=[jax.ShapeDtypeStruct(*out) for out in outs],
        in_specs=specs,
        out_specs=[VMEM] * len(outs),
        scratch_shapes=scratch,
        compiler_params=pltpu.CompilerParams(vmem_limit_bytes=VMEM_LIMIT),
        cost_estimate=pl.CostEstimate(flops=flops, bytes_accessed=moved, transcendentals=0),
    )


def shards(groups, blocks, query_proj, key_proj, value_proj, long_filter, skip_bias):
    tokens, chans = key_proj.shape
    rows = tokens // LANES
    own = chans // (groups * blocks)
    outer = blocks * rows
    seq_len = blocks * tokens
    tables = make_tables(seq_len)
    head, twist, tail, back_tail, back_head = (jnp.asarray(table) for table in tables)
    size = tokens * chans * 4

    share = own // groups if own % groups == 0 else own
    packed, bias = call(
        functools.partial(pack_kernel, rows, own, share),
        [((groups * blocks, (own + share) * rows, LANES), F32), ((1, chans), F32)],
        [SMEM, HBM, HBM, HBM, HBM], size // 4, size * 4,
        [pltpu.VMEM((tokens, chans), BF16), pltpu.VMEM((tokens, chans), BF16), pltpu.VMEM((tokens, chans), F32),
         pltpu.VMEM((2, chans * rows, LANES), F32), pltpu.SemaphoreType.DMA((3, rows)),
         pltpu.SemaphoreType.DMA],
    )(lax.axis_index("groups").reshape(1).astype(jnp.int32), *(
        pltpu.with_memory_space_constraint(source, pltpu.HBM)
        for source in (key_proj, value_proj, long_filter, skip_bias.reshape(1, chans))
    ))
    moved = lax.all_to_all(packed, ("groups", "seq"), 0, 0, tiled=True)
    macs = 2 * 3 * own * seq_len * (2 * outer + 4 * LANES)
    local = call(
        functools.partial(conv_kernel, rows, own, share),
        [((groups, blocks, own, rows, LANES), F32)], [VMEM] * 6, 5 * macs, 3 * size,
    )(moved.reshape(groups, blocks, (own + share) * rows, LANES), head, twist, tail, back_tail, back_head)[0]
    convolved = lax.all_to_all(local.reshape(chans * rows, LANES), ("groups", "seq"), 0, 0, tiled=True)
    return call(functools.partial(gate_kernel, rows), [((tokens, chans), BF16)], [VMEM] * 5, size, 3 * size)(
        convolved, query_proj, key_proj, value_proj, bias
    )[0]


def solution(mesh):
    placed = (
        P(("groups", "seq"), "chan"),
        P(("groups", "seq"), "chan"),
        P(("groups", "seq"), "chan"),
        P("seq", "chan"),
        P("chan"),
    )
    body = functools.partial(shards, mesh.shape["groups"], mesh.shape["seq"])
    return jax.shard_map(
        body, mesh=mesh, in_specs=placed, out_specs=P(("groups", "seq"), "chan"), check_vma=False
    )
```

```python
import functools

import jax
import jax.numpy as jnp
import ml_dtypes
import numpy as np
from jax import lax
from jax.experimental import pallas as pl
from jax.experimental.pallas import tpu as pltpu
from jax.sharding import PartitionSpec as P

LANES = 128
BF16 = jnp.bfloat16
F32 = jnp.float32
VMEM_LIMIT = 48 * 2**20


def split_np(table):
    high = table.astype(np.float32).astype(ml_dtypes.bfloat16)
    low = (table - high.astype(np.float64)).astype(np.float32).astype(ml_dtypes.bfloat16)
    return high, low


def make_tables(seq_len):
    outer = seq_len // LANES
    n_out, k_out = np.meshgrid(np.arange(outer), np.arange(outer), indexing="ij")
    head = np.exp(-2j * np.pi * (n_out * (4 * k_out + 1) % (4 * outer)) / (4 * outer))
    n_in = np.arange(LANES)
    twist = np.exp(-2j * np.pi * np.outer(4 * np.arange(outer) + 1, n_in) / (4 * seq_len))
    tail = np.exp(-2j * np.pi * (np.outer(n_in, n_in) % LANES) / LANES)

    def block(mat):
        return np.block([[mat.real, mat.imag], [-mat.imag, mat.real]])

    fwd_head = np.concatenate([head.real.T, head.imag.T], axis=0)
    high, low = split_np(fwd_head)
    head_tab = np.concatenate([high, high, low], axis=1)
    high, low = split_np(block(tail))
    tail_tab = np.concatenate([high, high, low], axis=0)
    high, low = split_np(block(tail.conj()))
    back_tail_tab = np.concatenate([high, high, low], axis=0)
    high, low = split_np(np.concatenate([head.real, head.imag], axis=1))
    back_head_tab = np.concatenate([high, high, low], axis=1)
    twist_tab = np.concatenate([twist.real, twist.imag], axis=1).astype(np.float32)
    return head_tab, twist_tab, tail_tab, back_tail_tab, back_head_tab


def halves(values):
    high = values.astype(BF16)
    return high, (values - high.astype(F32)).astype(BF16)


def by_rows(values):
    high, low = halves(values)
    return jnp.concatenate([high, low, high], axis=0)


def by_lanes(values):
    high, low = halves(values)
    return jnp.concatenate([high, low, high], axis=1)


def mat(left, right):
    return jnp.dot(left, right, preferred_element_type=F32)


def forward(signals, head, twist, tail):
    outer = signals[0].shape[0]
    mixed = mat(head, by_rows(jnp.concatenate(signals, axis=1)))
    cos, sin = twist[:, :LANES], twist[:, LANES:]
    rows = []
    for idx in range(len(signals)):
        real = mixed[:outer, idx * LANES : (idx + 1) * LANES]
        imag = mixed[outer:, idx * LANES : (idx + 1) * LANES]
        rows.append(jnp.concatenate([real * cos - imag * sin, real * sin + imag * cos], axis=1))
    return mat(by_lanes(jnp.concatenate(rows, axis=0)), tail)


def partner(place, step, count):
    return place ^ step if count & (count - 1) == 0 else (place + count - step) % count


def receiver(place, step, count):
    return place ^ step if count & (count - 1) == 0 else (place + step) % count


def exchange(parts, axes):
    count = len(parts)
    return [parts[0]] + [
        lax.ppermute(parts[step], axes, [(place, receiver(place, step, count)) for place in range(count)])
        for step in range(1, count)
    ]


def pack_kernel(rows, own, share, count, where_ref, *refs):
    sources, bias_ref = refs[:3], refs[3]
    outs, bias_out = refs[4 : 4 + count], refs[4 + count]
    held, turned, sems, bias_sem = refs[5 + count : 8 + count], refs[-3], refs[-2], refs[-1]
    bias_copy = pltpu.make_async_copy(bias_ref, bias_out, bias_sem)
    fetches = [pltpu.make_async_copy(sources[idx], held[idx], sems.at[idx]) for idx in range(3)]
    for fetch in fetches:
        fetch.start()
    bias_copy.start()
    fetches[0].wait()
    fetches[1].wait()
    for row in range(rows):
        span = pl.ds(row * LANES, LANES)
        driver = held[0][span, :].astype(F32) * held[1][span, :].astype(F32)
        turned[0, pl.ds(row, LANES, stride=rows), :] = driver.T
    fetches[2].wait()
    for row in range(rows):
        span = pl.ds(row * LANES, LANES)
        turned[1, pl.ds(row, LANES, stride=rows), :] = held[2][span, :].T
    first = where_ref[1] * (share * rows if share < own else 0)
    for step in range(count):
        start = pl.multiple_of(receiver(where_ref[0], step, count) * (own * rows), own * rows)
        outs[step][: own * rows] = turned[0, pl.ds(start, own * rows), :]
        taken = pl.ds(pl.multiple_of(start + first, rows), share * rows)
        outs[step][own * rows :] = turned[1, taken, :]
    bias_copy.wait()


def conv_kernel(rows, own, share, groups, blocks, where_ref, *refs):
    count = groups * blocks
    arrived, outs = refs[:count], refs[count + 5 : 2 * count + 5]
    head_ref, twist_ref, tail_ref, back_tail_ref, back_head_ref = refs[count : count + 5]
    moved_ref, result_ref = refs[-2:]
    for step in range(count):
        moved_ref[partner(where_ref[0], step, count)] = arrived[step][...]
    outer = blocks * rows
    scale = 1.0 / (outer * LANES)

    def signal(group, place):
        return moved_ref[pl.ds(group * blocks, blocks), place * rows : (place + 1) * rows].reshape(outer, LANES)

    signals = [signal(chan // share, own + chan % share) for chan in range(own)]
    signals += [signal(group, chan) for chan in range(own) for group in range(groups)]
    spec = forward(signals, head_ref[...], twist_ref[...], tail_ref[...])
    pieces = [spec[idx * outer : (idx + 1) * outer] for idx in range(len(signals))]
    prods = []
    for idx, mine in enumerate(pieces[own:]):
        other = pieces[idx // groups]
        f_re, f_im = other[:, :LANES], other[:, LANES:]
        d_re, d_im = mine[:, :LANES], mine[:, LANES:]
        prods.append(jnp.concatenate([d_re * f_re - d_im * f_im, d_re * f_im + d_im * f_re], axis=1))
    back = mat(by_lanes(jnp.concatenate(prods, axis=0)), back_tail_ref[...])
    cos, sin = twist_ref[:, :LANES] * scale, twist_ref[:, LANES:] * scale
    reals, imags = [], []
    for idx in range(len(prods)):
        mine = back[idx * outer : (idx + 1) * outer]
        real, imag = mine[:, :LANES], mine[:, LANES:]
        reals.append(real * cos + imag * sin)
        imags.append(imag * cos - real * sin)
    mixed = jnp.concatenate([jnp.concatenate(reals, axis=1), jnp.concatenate(imags, axis=1)], axis=0)
    result = mat(back_head_ref[...], by_rows(mixed))
    for idx in range(len(prods)):
        chan, group = divmod(idx, groups)
        result_ref[pl.ds(group * blocks, blocks), chan * rows : (chan + 1) * rows] = result[
            :, idx * LANES : (idx + 1) * LANES
        ].reshape(blocks, rows, LANES)
    for step in range(count):
        outs[step][...] = result_ref[receiver(where_ref[0], step, count)]


def gate_kernel(rows, count, where_ref, *refs):
    arrived, (query_ref, key_ref, value_ref, bias_ref, out_ref, conv_ref) = refs[:count], refs[count:]
    size = arrived[0].shape[0]
    for step in range(count):
        start = pl.multiple_of(partner(where_ref[0], step, count) * size, size)
        conv_ref[pl.ds(start, size), :] = arrived[step][...]
    bias = bias_ref[...]
    for row in range(rows):
        span = pl.ds(row * LANES, LANES)
        driver = key_ref[span, :].astype(F32) * value_ref[span, :].astype(F32)
        convolved = conv_ref[pl.ds(row, LANES, stride=rows), :].T
        out_ref[span, :] = (query_ref[span, :].astype(F32) * (convolved + bias * driver)).astype(BF16)


VMEM = pl.BlockSpec(memory_space=pltpu.VMEM)
HBM = pl.BlockSpec(memory_space=pltpu.HBM)
SMEM = pl.BlockSpec(memory_space=pltpu.SMEM)


def call(kernel, outs, specs, flops, moved, scratch=()):
    return pl.pallas_call(
        kernel,
        out_shape=[jax.ShapeDtypeStruct(*out) for out in outs],
        in_specs=specs,
        out_specs=[VMEM] * len(outs),
        scratch_shapes=scratch,
        compiler_params=pltpu.CompilerParams(vmem_limit_bytes=VMEM_LIMIT),
        cost_estimate=pl.CostEstimate(flops=flops, bytes_accessed=moved, transcendentals=0),
    )


def shards(groups, blocks, query_proj, key_proj, value_proj, long_filter, skip_bias):
    tokens, chans = key_proj.shape
    rows = tokens // LANES
    own = chans // (groups * blocks)
    outer = blocks * rows
    seq_len = blocks * tokens
    tables = make_tables(seq_len)
    head, twist, tail, back_tail, back_head = (jnp.asarray(table) for table in tables)
    size = tokens * chans * 4

    share = own // groups if own % groups == 0 else own
    count, axes = groups * blocks, ("groups", "seq")
    where = jnp.stack([lax.axis_index(axes), lax.axis_index("groups")]).astype(jnp.int32)
    *packed, bias = call(
        functools.partial(pack_kernel, rows, own, share, count),
        [(((own + share) * rows, LANES), F32)] * count + [((1, chans), F32)],
        [SMEM, HBM, HBM, HBM, HBM], size // 4, size * 4,
        [pltpu.VMEM((tokens, chans), BF16), pltpu.VMEM((tokens, chans), BF16), pltpu.VMEM((tokens, chans), F32),
         pltpu.VMEM((2, chans * rows, LANES), F32), pltpu.SemaphoreType.DMA((3,)), pltpu.SemaphoreType.DMA],
    )(where, *(
        pltpu.with_memory_space_constraint(source, pltpu.HBM)
        for source in (key_proj, value_proj, long_filter, skip_bias.reshape(1, chans))
    ))
    moved = exchange(packed, axes)
    macs = 2 * 3 * own * seq_len * (2 * outer + 4 * LANES)
    local = call(
        functools.partial(conv_kernel, rows, own, share, groups, blocks),
        [((own * rows, LANES), F32)] * count, [SMEM] + [VMEM] * (count + 5), 5 * macs, 3 * size,
        [pltpu.VMEM((count, (own + share) * rows, LANES), F32), pltpu.VMEM((count, own * rows, LANES), F32)],
    )(where, *moved, head, twist, tail, back_tail, back_head)
    convolved = exchange(local, axes)
    return call(
        functools.partial(gate_kernel, rows, count),
        [((tokens, chans), BF16)], [SMEM] + [VMEM] * (count + 4), size, 3 * size,
        [pltpu.VMEM((chans * rows, LANES), F32)],
    )(where, *convolved, query_proj, key_proj, value_proj, bias)[0]


def solution(mesh):
    placed = (
        P(("groups", "seq"), "chan"),
        P(("groups", "seq"), "chan"),
        P(("groups", "seq"), "chan"),
        P("seq", "chan"),
        P("chan"),
    )
    body = functools.partial(shards, mesh.shape["groups"], mesh.shape["seq"])
    return jax.shard_map(
        body, mesh=mesh, in_specs=placed, out_specs=P(("groups", "seq"), "chan"), check_vma=False
    )
```

```python
import functools

import jax
import jax.numpy as jnp
import ml_dtypes
import numpy as np
from jax import lax
from jax.experimental import pallas as pl
from jax.experimental.pallas import tpu as pltpu
from jax.sharding import PartitionSpec as P

LANES = 128
BF16 = jnp.bfloat16
F32 = jnp.float32
VMEM_LIMIT = 48 * 2**20


def split_np(table):
    high = table.astype(np.float32).astype(ml_dtypes.bfloat16)
    low = (table - high.astype(np.float64)).astype(np.float32).astype(ml_dtypes.bfloat16)
    return high, low


def make_tables(seq_len):
    outer = seq_len // LANES
    n_out, k_out = np.meshgrid(np.arange(outer), np.arange(outer), indexing="ij")
    head = np.exp(-2j * np.pi * (n_out * (4 * k_out + 1) % (4 * outer)) / (4 * outer))
    n_in = np.arange(LANES)
    twist = np.exp(-2j * np.pi * np.outer(4 * np.arange(outer) + 1, n_in) / (4 * seq_len))
    tail = np.exp(-2j * np.pi * (np.outer(n_in, n_in) % LANES) / LANES)

    def block(mat):
        return np.block([[mat.real, mat.imag], [-mat.imag, mat.real]])

    fwd_head = np.concatenate([head.real.T, head.imag.T], axis=0)
    high, low = split_np(fwd_head)
    head_tab = np.concatenate([high, high, low], axis=1)
    high, low = split_np(block(tail))
    tail_tab = np.concatenate([high, high, low], axis=0)
    high, low = split_np(block(tail.conj()))
    back_tail_tab = np.concatenate([high, high, low], axis=0)
    high, low = split_np(np.concatenate([head.real, head.imag], axis=1))
    back_head_tab = np.concatenate([high, high, low], axis=1)
    twist_tab = np.concatenate([twist.real, twist.imag], axis=1).astype(np.float32)
    return head_tab, twist_tab, tail_tab, back_tail_tab, back_head_tab


def halves(values):
    high = values.astype(BF16)
    return high, (values - high.astype(F32)).astype(BF16)


def by_rows(values):
    high, low = halves(values)
    return jnp.concatenate([high, low, high], axis=0)


def by_lanes(values):
    high, low = halves(values)
    return jnp.concatenate([high, low, high], axis=1)


def mat(left, right):
    return jnp.dot(left, right, preferred_element_type=F32)


def forward(signals, head, twist, tail):
    outer = signals[0].shape[0]
    mixed = mat(head, by_rows(jnp.concatenate(signals, axis=1)))
    cos, sin = twist[:, :LANES], twist[:, LANES:]
    rows = []
    for idx in range(len(signals)):
        real = mixed[:outer, idx * LANES : (idx + 1) * LANES]
        imag = mixed[outer:, idx * LANES : (idx + 1) * LANES]
        rows.append(jnp.concatenate([real * cos - imag * sin, real * sin + imag * cos], axis=1))
    return mat(by_lanes(jnp.concatenate(rows, axis=0)), tail)


def pack_kernel(layout, with_driver, with_filter, where_ref, *refs):
    rows, own, part, groups = layout
    refs = list(refs)
    sources = [refs.pop(0) for _ in range(2 * with_driver + with_filter)]
    bias_ref = refs.pop(0) if with_driver else None
    out_ref = refs.pop(0)
    bias_out = refs.pop(0) if with_driver else None
    held = [refs.pop(0) for _ in sources]
    sems = refs.pop(0)
    fetches = []
    for idx, source in enumerate(sources):
        if idx == 2 * with_driver:
            first = where_ref[0] * (part * LANES if part < rows else 0)
            source = source.at[pl.ds(pl.multiple_of(first, part * LANES), part * LANES)]
        fetches.append(pltpu.make_async_copy(source, held[idx], sems.at[idx]))
    if with_driver:
        fetches.append(pltpu.make_async_copy(bias_ref, bias_out, sems.at[len(sources)]))
    for fetch in fetches:
        fetch.start()
    base = 0
    if with_driver:
        base = own * rows
        fetches[0].wait()
        fetches[1].wait()
        for row in range(rows):
            span = pl.ds(row * LANES, LANES)
            turned = (held[0][span, :].astype(F32) * held[1][span, :].astype(F32)).T
            for peer in range(out_ref.shape[0]):
                out_ref[peer, pl.ds(row, own, stride=rows), :] = turned[peer * own : (peer + 1) * own]
    if with_filter:
        fetches[2 * with_driver].wait()
        for row in range(part):
            turned = held[-1][pl.ds(row * LANES, LANES), :].T
            for peer in range(out_ref.shape[0]):
                out_ref[peer, pl.ds(base + row, own, stride=part), :] = turned[peer * own : (peer + 1) * own]
    if with_driver:
        fetches[-1].wait()


def driver_signals(layout, moved_ref):
    rows, own, part, groups = layout
    blocks = moved_ref.shape[0] // groups
    return [
        moved_ref[pl.ds(group * blocks, blocks), chan * rows : (chan + 1) * rows].reshape(blocks * rows, LANES)
        for chan in range(own)
        for group in range(groups)
    ]


def filter_signals(layout, base, moved_ref):
    rows, own, part, groups = layout
    blocks = moved_ref.shape[0] // groups
    signals = []
    for chan in range(own):
        start = base + chan * part
        pieces = [
            moved_ref[pl.ds(group * blocks, blocks), start : start + part]
            for group in range(groups if part < rows else 1)
        ]
        signals.append(jnp.concatenate(pieces, axis=1).reshape(blocks * rows, LANES))
    return signals


def filter_kernel(layout, moved_ref, head_ref, twist_ref, tail_ref, out_ref):
    signals = filter_signals(layout, 0, moved_ref)
    out_ref[...] = forward(signals, head_ref[...], twist_ref[...], tail_ref[...])


def conv_kernel(layout, joint, moved_ref, *refs):
    rows, own, part, groups = layout
    spec_ref = None if joint else refs[0]
    head_ref, twist_ref, tail_ref, back_tail_ref, back_head_ref, out_ref = refs[-6:]
    blocks = moved_ref.shape[0] // groups
    outer = blocks * rows
    scale = 1.0 / (outer * LANES)
    signals = filter_signals(layout, own * rows, moved_ref) if joint else []
    signals += driver_signals(layout, moved_ref)
    spec = forward(signals, head_ref[...], twist_ref[...], tail_ref[...])
    pieces = [spec[idx * outer : (idx + 1) * outer] for idx in range(len(signals))]
    if not joint:
        pieces = [spec_ref[pl.ds(chan * outer, outer), :] for chan in range(own)] + pieces
    prods = []
    for idx, mine in enumerate(pieces[own:]):
        other = pieces[idx // groups]
        f_re, f_im = other[:, :LANES], other[:, LANES:]
        d_re, d_im = mine[:, :LANES], mine[:, LANES:]
        prods.append(jnp.concatenate([d_re * f_re - d_im * f_im, d_re * f_im + d_im * f_re], axis=1))
    back = mat(by_lanes(jnp.concatenate(prods, axis=0)), back_tail_ref[...])
    cos, sin = twist_ref[:, :LANES] * scale, twist_ref[:, LANES:] * scale
    reals, imags = [], []
    for idx in range(len(prods)):
        mine = back[idx * outer : (idx + 1) * outer]
        real, imag = mine[:, :LANES], mine[:, LANES:]
        reals.append(real * cos + imag * sin)
        imags.append(imag * cos - real * sin)
    mixed = jnp.concatenate([jnp.concatenate(reals, axis=1), jnp.concatenate(imags, axis=1)], axis=0)
    result = mat(back_head_ref[...], by_rows(mixed))
    for idx in range(len(prods)):
        chan, group = divmod(idx, groups)
        out_ref[pl.ds(group * blocks, blocks), chan * rows : (chan + 1) * rows] = result[
            :, idx * LANES : (idx + 1) * LANES
        ].reshape(blocks, rows, LANES)


def gate_kernel(rows, conv_ref, query_ref, key_ref, value_ref, bias_ref, out_ref):
    bias = bias_ref[...]
    for row in range(rows):
        span = pl.ds(row * LANES, LANES)
        driver = key_ref[span, :].astype(F32) * value_ref[span, :].astype(F32)
        convolved = conv_ref[pl.ds(row, LANES, stride=rows), :].T
        out_ref[span, :] = (query_ref[span, :].astype(F32) * (convolved + bias * driver)).astype(BF16)


VMEM = pl.BlockSpec(memory_space=pltpu.VMEM)
HBM = pl.BlockSpec(memory_space=pltpu.HBM)
SMEM = pl.BlockSpec(memory_space=pltpu.SMEM)


def call(kernel, outs, specs, flops, moved, scratch=()):
    return pl.pallas_call(
        kernel,
        out_shape=[jax.ShapeDtypeStruct(*out) for out in outs],
        in_specs=specs,
        out_specs=[VMEM] * len(outs),
        scratch_shapes=scratch,
        compiler_params=pltpu.CompilerParams(vmem_limit_bytes=VMEM_LIMIT),
        cost_estimate=pl.CostEstimate(flops=flops, bytes_accessed=moved, transcendentals=0),
    )


def convolve(groups, blocks, joint, query_proj, key_proj, value_proj, long_filter, skip_bias):
    tokens, chans = key_proj.shape
    rows = tokens // LANES
    count, axes = groups * blocks, ("groups", "seq")
    own = chans // count
    outer = blocks * rows
    seq_len = blocks * tokens
    part = rows // groups
    if rows % groups or own * part % 8:
        part = rows
    layout = (rows, own, part, groups)
    head, twist, tail, back_tail, back_head = (jnp.asarray(table) for table in make_tables(seq_len))
    size = tokens * chans * 4
    macs = 2 * 3 * own * seq_len * (2 * outer + 4 * LANES)
    where = lax.axis_index("groups").reshape(1).astype(jnp.int32)

    def pack(with_driver, with_filter):
        height = own * (rows * with_driver + part * with_filter)
        sources = [key_proj, value_proj] * with_driver + [long_filter] * with_filter
        heights = [tokens, tokens] * with_driver + [part * LANES] * with_filter
        scratch = [pltpu.VMEM((tall, chans), source.dtype) for tall, source in zip(heights, sources)]
        sources += [skip_bias.reshape(1, chans)] * with_driver
        return call(
            functools.partial(pack_kernel, layout, with_driver, with_filter),
            [((count, height, LANES), F32)] + [((1, chans), F32)] * with_driver,
            [SMEM] + [HBM] * len(sources), size // 4, size * 3,
            scratch + [pltpu.SemaphoreType.DMA((len(sources),))],
        )(where, *(pltpu.with_memory_space_constraint(source, pltpu.HBM) for source in sources))

    def exchange(array):
        return lax.all_to_all(array, axes, 0, 0, tiled=True)

    spec = []
    if joint:
        packed, bias = pack(1, 1)
    else:
        moved_filter = exchange(pack(0, 1)[0])
        packed, bias = pack(1, 0)
        spec = call(
            functools.partial(filter_kernel, layout), [((own * outer, 2 * LANES), F32)], [VMEM] * 4, macs, size
        )(moved_filter, head, twist, tail)
    local = call(
        functools.partial(conv_kernel, layout, joint),
        [((count, own * rows, LANES), F32)], [VMEM] * (6 + len(spec)), 5 * macs, 3 * size,
    )(exchange(packed), *spec, head, twist, tail, back_tail, back_head)[0]
    convolved = exchange(local).reshape(chans * rows, LANES)
    return call(functools.partial(gate_kernel, rows), [((tokens, chans), BF16)], [VMEM] * 5, size, 3 * size)(
        convolved, query_proj, key_proj, value_proj, bias
    )[0]


def shards(groups, blocks, cores, *args):
    if cores == 1:
        return convolve(groups, blocks, True, *args)
    return lax.cond(
        lax.axis_index("chan") % 2 == 1,
        functools.partial(convolve, groups, blocks, True),
        functools.partial(convolve, groups, blocks, False),
        *args,
    )


def solution(mesh):
    placed = (
        P(("groups", "seq"), "chan"),
        P(("groups", "seq"), "chan"),
        P(("groups", "seq"), "chan"),
        P("seq", "chan"),
        P("chan"),
    )
    body = functools.partial(shards, *(mesh.shape[axis] for axis in ("groups", "seq", "chan")))
    return jax.shard_map(
        body, mesh=mesh, in_specs=placed, out_specs=P(("groups", "seq"), "chan"), check_vma=False
    )
```

```python
import functools

import jax
import jax.numpy as jnp
import ml_dtypes
import numpy as np
from jax import lax
from jax.experimental import pallas as pl
from jax.experimental.pallas import tpu as pltpu
from jax.sharding import PartitionSpec as P

LANES = 128
BF16 = jnp.bfloat16
F32 = jnp.float32
VMEM_LIMIT = 48 * 2**20


def split_np(table):
    high = table.astype(np.float32).astype(ml_dtypes.bfloat16)
    low = (table - high.astype(np.float64)).astype(np.float32).astype(ml_dtypes.bfloat16)
    return high, low


def make_tables(seq_len):
    outer = seq_len // LANES
    n_out, k_out = np.meshgrid(np.arange(outer), np.arange(outer), indexing="ij")
    head = np.exp(-2j * np.pi * (n_out * (4 * k_out + 1) % (4 * outer)) / (4 * outer))
    n_in = np.arange(LANES)
    twist = np.exp(-2j * np.pi * np.outer(4 * np.arange(outer) + 1, n_in) / (4 * seq_len))
    tail = np.exp(-2j * np.pi * (np.outer(n_in, n_in) % LANES) / LANES)

    def block(mat):
        return np.block([[mat.real, mat.imag], [-mat.imag, mat.real]])

    fwd_head = np.concatenate([head.real.T, head.imag.T], axis=0)
    high, low = split_np(fwd_head)
    head_tab = np.concatenate([high, high, low], axis=1)
    high, low = split_np(block(tail))
    tail_tab = np.concatenate([high, high, low], axis=0)
    high, low = split_np(block(tail.conj()))
    back_tail_tab = np.concatenate([high, high, low], axis=0)
    high, low = split_np(np.concatenate([head.real, head.imag], axis=1))
    back_head_tab = np.concatenate([high, high, low], axis=1)
    twist_tab = np.concatenate([twist.real, twist.imag], axis=1).astype(np.float32)
    return head_tab, twist_tab, tail_tab, back_tail_tab, back_head_tab


def halves(values):
    high = values.astype(BF16)
    return high, (values - high.astype(F32)).astype(BF16)


def by_rows(values):
    high, low = halves(values)
    return jnp.concatenate([high, low, high], axis=0)


def by_lanes(values):
    high, low = halves(values)
    return jnp.concatenate([high, low, high], axis=1)


def mat(left, right):
    return jnp.dot(left, right, preferred_element_type=F32)


def forward(signals, head, twist, tail):
    outer = signals[0].shape[0]
    mixed = mat(head, by_rows(jnp.concatenate(signals, axis=1)))
    cos, sin = twist[:, :LANES], twist[:, LANES:]
    rows = []
    for idx in range(len(signals)):
        real = mixed[:outer, idx * LANES : (idx + 1) * LANES]
        imag = mixed[outer:, idx * LANES : (idx + 1) * LANES]
        rows.append(jnp.concatenate([real * cos - imag * sin, real * sin + imag * cos], axis=1))
    return mat(by_lanes(jnp.concatenate(rows, axis=0)), tail)


def pack_kernel(layout, where_ref, key_ref, value_ref, filter_ref, bias_ref, out_ref, bias_out, key, value, taps, sems):
    rows, own, part, groups = layout
    first = where_ref[0] * (part * LANES if part < rows else 0)
    taken = filter_ref.at[pl.ds(pl.multiple_of(first, part * LANES), part * LANES)]
    pairs = ((key_ref, key), (value_ref, value), (taken, taps), (bias_ref, bias_out))
    fetches = [pltpu.make_async_copy(*pair, sems.at[idx]) for idx, pair in enumerate(pairs)]
    for fetch in fetches:
        fetch.start()
    fetches[0].wait()
    fetches[1].wait()
    for row in range(rows):
        span = pl.ds(row * LANES, LANES)
        turned = (key[span, :].astype(F32) * value[span, :].astype(F32)).T
        for peer in range(out_ref.shape[0]):
            out_ref[peer, pl.ds(row, own, stride=rows), :] = turned[peer * own : (peer + 1) * own]
    fetches[2].wait()
    for row in range(part):
        turned = taps[pl.ds(row * LANES, LANES), :].T
        for peer in range(out_ref.shape[0]):
            out_ref[peer, pl.ds(own * rows + row, own, stride=part), :] = turned[peer * own : (peer + 1) * own]
    fetches[3].wait()


def driver_signals(layout, moved_ref):
    rows, own, part, groups = layout
    blocks = moved_ref.shape[0] // groups
    return [
        moved_ref[pl.ds(group * blocks, blocks), chan * rows : (chan + 1) * rows].reshape(blocks * rows, LANES)
        for chan in range(own)
        for group in range(groups)
    ]


def filter_signals(layout, moved_ref):
    rows, own, part, groups = layout
    blocks = moved_ref.shape[0] // groups
    signals = []
    for chan in range(own):
        start = own * rows + chan * part
        pieces = [
            moved_ref[pl.ds(group * blocks, blocks), start : start + part]
            for group in range(groups if part < rows else 1)
        ]
        signals.append(jnp.concatenate(pieces, axis=1).reshape(blocks * rows, LANES))
    return signals


def conv_kernel(layout, moved_ref, head_ref, twist_ref, tail_ref, back_tail_ref, back_head_ref, out_ref):
    rows, own, part, groups = layout
    blocks = moved_ref.shape[0] // groups
    outer = blocks * rows
    scale = 1.0 / (outer * LANES)
    signals = filter_signals(layout, moved_ref) + driver_signals(layout, moved_ref)
    spec = forward(signals, head_ref[...], twist_ref[...], tail_ref[...])
    pieces = [spec[idx * outer : (idx + 1) * outer] for idx in range(len(signals))]
    prods = []
    for idx, mine in enumerate(pieces[own:]):
        other = pieces[idx // groups]
        f_re, f_im = other[:, :LANES], other[:, LANES:]
        d_re, d_im = mine[:, :LANES], mine[:, LANES:]
        prods.append(jnp.concatenate([d_re * f_re - d_im * f_im, d_re * f_im + d_im * f_re], axis=1))
    back = mat(by_lanes(jnp.concatenate(prods, axis=0)), back_tail_ref[...])
    cos, sin = twist_ref[:, :LANES] * scale, twist_ref[:, LANES:] * scale
    reals, imags = [], []
    for idx in range(len(prods)):
        mine = back[idx * outer : (idx + 1) * outer]
        real, imag = mine[:, :LANES], mine[:, LANES:]
        reals.append(real * cos + imag * sin)
        imags.append(imag * cos - real * sin)
    mixed = jnp.concatenate([jnp.concatenate(reals, axis=1), jnp.concatenate(imags, axis=1)], axis=0)
    result = mat(back_head_ref[...], by_rows(mixed))
    for idx in range(len(prods)):
        chan, group = divmod(idx, groups)
        out_ref[pl.ds(group * blocks, blocks), chan * rows : (chan + 1) * rows] = result[
            :, idx * LANES : (idx + 1) * LANES
        ].reshape(blocks, rows, LANES)


def gate_kernel(rows, conv_ref, query_ref, key_ref, value_ref, bias_ref, out_ref):
    bias = bias_ref[...]
    for row in range(rows):
        span = pl.ds(row * LANES, LANES)
        driver = key_ref[span, :].astype(F32) * value_ref[span, :].astype(F32)
        convolved = conv_ref[pl.ds(row, LANES, stride=rows), :].T
        out_ref[span, :] = (query_ref[span, :].astype(F32) * (convolved + bias * driver)).astype(BF16)


VMEM = pl.BlockSpec(memory_space=pltpu.VMEM)
HBM = pl.BlockSpec(memory_space=pltpu.HBM)
SMEM = pl.BlockSpec(memory_space=pltpu.SMEM)


def call(kernel, outs, specs, flops, moved, scratch=()):
    return pl.pallas_call(
        kernel,
        out_shape=[jax.ShapeDtypeStruct(*out) for out in outs],
        in_specs=specs,
        out_specs=[VMEM] * len(outs),
        scratch_shapes=scratch,
        compiler_params=pltpu.CompilerParams(vmem_limit_bytes=VMEM_LIMIT),
        cost_estimate=pl.CostEstimate(flops=flops, bytes_accessed=moved, transcendentals=0),
    )


def shards(groups, blocks, query_proj, key_proj, value_proj, long_filter, skip_bias):
    tokens, chans = key_proj.shape
    rows = tokens // LANES
    count, axes = groups * blocks, ("groups", "seq")
    own = chans // count
    outer = blocks * rows
    seq_len = blocks * tokens
    part = rows // groups
    if rows % groups or own * part % 8:
        part = rows
    layout = (rows, own, part, groups)
    head, twist, tail, back_tail, back_head = (jnp.asarray(table) for table in make_tables(seq_len))
    size = tokens * chans * 4
    macs = 2 * 3 * own * seq_len * (2 * outer + 4 * LANES)
    where = lax.axis_index("groups").reshape(1).astype(jnp.int32)

    def exchange(array):
        return lax.all_to_all(array, axes, 0, 0, tiled=True)

    sources = (key_proj, value_proj, long_filter, skip_bias.reshape(1, chans))
    packed, bias = call(
        functools.partial(pack_kernel, layout),
        [((count, own * (rows + part), LANES), F32), ((1, chans), F32)],
        [SMEM] + [HBM] * 4, size // 4, size * 3,
        [pltpu.VMEM((tokens, chans), BF16), pltpu.VMEM((tokens, chans), BF16), pltpu.VMEM((part * LANES, chans), F32),
         pltpu.SemaphoreType.DMA((4,))],
    )(where, *(pltpu.with_memory_space_constraint(source, pltpu.HBM) for source in sources))
    local = call(
        functools.partial(conv_kernel, layout),
        [((count, own * rows, LANES), F32)], [VMEM] * 6, 5 * macs, 3 * size,
    )(exchange(packed), head, twist, tail, back_tail, back_head)[0]
    convolved = exchange(local).reshape(chans * rows, LANES)
    return call(functools.partial(gate_kernel, rows), [((tokens, chans), BF16)], [VMEM] * 5, size, 3 * size)(
        convolved, query_proj, key_proj, value_proj, bias
    )[0]


def solution(mesh):
    placed = (
        P(("groups", "seq"), "chan"),
        P(("groups", "seq"), "chan"),
        P(("groups", "seq"), "chan"),
        P("seq", "chan"),
        P("chan"),
    )
    body = functools.partial(shards, mesh.shape["groups"], mesh.shape["seq"])
    return jax.shard_map(
        body, mesh=mesh, in_specs=placed, out_specs=P(("groups", "seq"), "chan"), check_vma=False
    )
```

```python
import functools

import jax
import jax.numpy as jnp
import ml_dtypes
import numpy as np
from jax import lax
from jax.experimental import pallas as pl
from jax.experimental.pallas import tpu as pltpu
from jax.sharding import PartitionSpec as P

LANES = 128
BF16 = jnp.bfloat16
F32 = jnp.float32
VMEM_LIMIT = 48 * 2**20


def split_np(table):
    high = table.astype(np.float32).astype(ml_dtypes.bfloat16)
    low = (table - high.astype(np.float64)).astype(np.float32).astype(ml_dtypes.bfloat16)
    return high, low


def make_tables(seq_len):
    outer = seq_len // LANES
    n_out, k_out = np.meshgrid(np.arange(outer), np.arange(outer), indexing="ij")
    head = np.exp(-2j * np.pi * (n_out * (4 * k_out + 1) % (4 * outer)) / (4 * outer))
    n_in = np.arange(LANES)
    twist = np.exp(-2j * np.pi * np.outer(4 * np.arange(outer) + 1, n_in) / (4 * seq_len))
    tail = np.exp(-2j * np.pi * (np.outer(n_in, n_in) % LANES) / LANES)

    def block(mat):
        return np.block([[mat.real, mat.imag], [-mat.imag, mat.real]])

    fwd_head = np.concatenate([head.real.T, head.imag.T], axis=0)
    high, low = split_np(fwd_head)
    head_tab = np.concatenate([high, high, low], axis=1)
    high, low = split_np(block(tail))
    tail_tab = np.concatenate([high, high, low], axis=0)
    high, low = split_np(block(tail.conj()))
    back_tail_tab = np.concatenate([high, high, low], axis=0)
    high, low = split_np(np.concatenate([head.real, head.imag], axis=1))
    back_head_tab = np.block([[high, high], [low, np.zeros_like(low)]])
    twist_tab = np.concatenate([twist.real, twist.imag], axis=1).astype(np.float32)
    return head_tab, twist_tab, tail_tab, back_tail_tab, back_head_tab


def halves(values):
    high = values.astype(BF16)
    return high, (values - high.astype(F32)).astype(BF16)


def by_rows(values):
    high, low = halves(values)
    return jnp.concatenate([high, low, high], axis=0)


def by_lanes(values):
    high, low = halves(values)
    return jnp.concatenate([high, low, high], axis=1)


def mat(left, right):
    return jnp.dot(left, right, preferred_element_type=F32)


def head_stage(signals, head, twist):
    outer = signals[0].shape[0]
    mixed = mat(head, by_rows(jnp.concatenate(signals, axis=1)))
    cos, sin = twist[:, :LANES], twist[:, LANES:]
    rows = []
    for idx in range(len(signals)):
        real = mixed[:outer, idx * LANES : (idx + 1) * LANES]
        imag = mixed[outer:, idx * LANES : (idx + 1) * LANES]
        rows.append(jnp.concatenate([real * cos - imag * sin, real * sin + imag * cos], axis=1))
    return jnp.concatenate(rows, axis=0)


def product_stage(spec, outer, groups):
    pieces = [spec[idx * outer : (idx + 1) * outer] for idx in range(spec.shape[0] // outer)]
    own = len(pieces) // (groups + 1)
    prods = []
    for idx, mine in enumerate(pieces[own:]):
        other = pieces[idx // groups]
        f_re, f_im = other[:, :LANES], other[:, LANES:]
        d_re, d_im = mine[:, :LANES], mine[:, LANES:]
        prods.append(jnp.concatenate([d_re * f_re - d_im * f_im, d_re * f_im + d_im * f_re], axis=1))
    return jnp.concatenate(prods, axis=0)


def back_stage(back, cos, sin):
    outer = cos.shape[0]
    reals, imags = [], []
    for idx in range(back.shape[0] // outer):
        mine = back[idx * outer : (idx + 1) * outer]
        real, imag = mine[:, :LANES], mine[:, LANES:]
        reals.append(real * cos + imag * sin)
        imags.append(imag * cos - real * sin)
    return jnp.concatenate([jnp.concatenate(reals, axis=1), jnp.concatenate(imags, axis=1)], axis=0)


def pack_kernel(layout, where_ref, key_ref, value_ref, filter_ref, bias_ref, out_ref, bias_out, key, value, taps, sems):
    rows, own, part, groups = layout
    first = where_ref[0] * (part * LANES if part < rows else 0)
    taken = filter_ref.at[pl.ds(pl.multiple_of(first, part * LANES), part * LANES)]
    pairs = ((key_ref, key), (value_ref, value), (taken, taps), (bias_ref, bias_out))
    fetches = [pltpu.make_async_copy(*pair, sems.at[idx]) for idx, pair in enumerate(pairs)]
    for fetch in fetches:
        fetch.start()
    fetches[0].wait()
    fetches[1].wait()
    for row in range(rows):
        span = pl.ds(row * LANES, LANES)
        turned = (key[span, :].astype(F32) * value[span, :].astype(F32)).T
        for peer in range(out_ref.shape[0]):
            out_ref[peer, pl.ds(row, own, stride=rows), :] = turned[peer * own : (peer + 1) * own]
    fetches[2].wait()
    for row in range(part):
        turned = taps[pl.ds(row * LANES, LANES), :].T
        for peer in range(out_ref.shape[0]):
            out_ref[peer, pl.ds(own * rows + row, own, stride=part), :] = turned[peer * own : (peer + 1) * own]
    fetches[3].wait()


def driver_signals(layout, moved_ref, chans):
    rows, own, part, groups = layout
    blocks = moved_ref.shape[0] // groups
    return [
        moved_ref[pl.ds(group * blocks, blocks), chan * rows : (chan + 1) * rows].reshape(blocks * rows, LANES)
        for chan in chans
        for group in range(groups)
    ]


def filter_signals(layout, moved_ref, chans):
    rows, own, part, groups = layout
    blocks = moved_ref.shape[0] // groups
    signals = []
    for chan in chans:
        start = own * rows + chan * part
        pieces = [
            moved_ref[pl.ds(group * blocks, blocks), start : start + part]
            for group in range(groups if part < rows else 1)
        ]
        signals.append(jnp.concatenate(pieces, axis=1).reshape(blocks * rows, LANES))
    return signals


def conv_kernel(layout, pieces, moved_ref, head_ref, twist_ref, tail_ref, back_tail_ref, back_head_ref, out_ref):
    rows, own, part, groups = layout
    blocks = moved_ref.shape[0] // groups
    outer = blocks * rows
    scale = 1.0 / (outer * LANES)
    cos, sin = twist_ref[:, :LANES] * scale, twist_ref[:, LANES:] * scale
    sets = [range(piece * own // pieces, (piece + 1) * own // pieces) for piece in range(pieces)]
    mixed = [
        head_stage(
            filter_signals(layout, moved_ref, chans) + driver_signals(layout, moved_ref, chans),
            head_ref[...],
            twist_ref[...],
        )
        for chans in sets
    ]
    specs = [mat(by_lanes(values), tail_ref[...]) for values in mixed]
    prods = [product_stage(spec, outer, groups) for spec in specs]
    backs = [mat(by_lanes(values), back_tail_ref[...]) for values in prods]
    turned = [back_stage(back, cos, sin) for back in backs]
    results = [mat(back_head_ref[...], jnp.concatenate(halves(values), axis=0)) for values in turned]
    for chans, result in zip(sets, results):
        result = result[:outer] + result[outer:]
        for idx in range(len(chans) * groups):
            chan, group = divmod(idx, groups)
            start = (chans[0] + chan) * rows
            out_ref[pl.ds(group * blocks, blocks), start : start + rows] = result[
                :, idx * LANES : (idx + 1) * LANES
            ].reshape(blocks, rows, LANES)


def gate_kernel(rows, conv_ref, query_ref, key_ref, value_ref, bias_ref, out_ref):
    bias = bias_ref[...]
    for row in range(rows):
        span = pl.ds(row * LANES, LANES)
        driver = key_ref[span, :].astype(F32) * value_ref[span, :].astype(F32)
        convolved = conv_ref[pl.ds(row, LANES, stride=rows), :].T
        out_ref[span, :] = (query_ref[span, :].astype(F32) * (convolved + bias * driver)).astype(BF16)


VMEM = pl.BlockSpec(memory_space=pltpu.VMEM)
HBM = pl.BlockSpec(memory_space=pltpu.HBM)
SMEM = pl.BlockSpec(memory_space=pltpu.SMEM)


def call(kernel, outs, specs, flops, moved, scratch=()):
    return pl.pallas_call(
        kernel,
        out_shape=[jax.ShapeDtypeStruct(*out) for out in outs],
        in_specs=specs,
        out_specs=[VMEM] * len(outs),
        scratch_shapes=scratch,
        compiler_params=pltpu.CompilerParams(vmem_limit_bytes=VMEM_LIMIT),
        cost_estimate=pl.CostEstimate(flops=flops, bytes_accessed=moved, transcendentals=0),
    )


def shards(groups, blocks, query_proj, key_proj, value_proj, long_filter, skip_bias):
    tokens, chans = key_proj.shape
    rows = tokens // LANES
    count, axes = groups * blocks, ("groups", "seq")
    own = chans // count
    outer = blocks * rows
    seq_len = blocks * tokens
    part = rows // groups
    if rows % groups or own * part % 8:
        part = rows
    layout = (rows, own, part, groups)
    head, twist, tail, back_tail, back_head = (jnp.asarray(table) for table in make_tables(seq_len))
    size = tokens * chans * 4
    macs = 2 * 3 * own * seq_len * (2 * outer + 4 * LANES)
    where = lax.axis_index("groups").reshape(1).astype(jnp.int32)

    def exchange(array):
        return lax.all_to_all(array, axes, 0, 0, tiled=True)

    sources = (key_proj, value_proj, long_filter, skip_bias.reshape(1, chans))
    packed, bias = call(
        functools.partial(pack_kernel, layout),
        [((count, own * (rows + part), LANES), F32), ((1, chans), F32)],
        [SMEM] + [HBM] * 4, size // 4, size * 3,
        [pltpu.VMEM((tokens, chans), BF16), pltpu.VMEM((tokens, chans), BF16), pltpu.VMEM((part * LANES, chans), F32),
         pltpu.SemaphoreType.DMA((4,))],
    )(where, *(pltpu.with_memory_space_constraint(source, pltpu.HBM) for source in sources))
    local = call(
        functools.partial(conv_kernel, layout, min(own, 2)),
        [((count, own * rows, LANES), F32)], [VMEM] * 6, 5 * macs, 3 * size,
    )(exchange(packed), head, twist, tail, back_tail, back_head)[0]
    convolved = exchange(local).reshape(chans * rows, LANES)
    return call(functools.partial(gate_kernel, rows), [((tokens, chans), BF16)], [VMEM] * 5, size, 3 * size)(
        convolved, query_proj, key_proj, value_proj, bias
    )[0]


def solution(mesh):
    placed = (
        P(("groups", "seq"), "chan"),
        P(("groups", "seq"), "chan"),
        P(("groups", "seq"), "chan"),
        P("seq", "chan"),
        P("chan"),
    )
    body = functools.partial(shards, mesh.shape["groups"], mesh.shape["seq"])
    return jax.shard_map(
        body, mesh=mesh, in_specs=placed, out_specs=P(("groups", "seq"), "chan"), check_vma=False
    )
```

```python
import functools

import jax
import jax.numpy as jnp
import ml_dtypes
import numpy as np
from jax import lax
from jax.experimental import pallas as pl
from jax.experimental.pallas import tpu as pltpu
from jax.sharding import PartitionSpec as P

LANES = 128
BF16 = jnp.bfloat16
F32 = jnp.float32
VMEM_LIMIT = 48 * 2**20


def split_np(table):
    high = table.astype(np.float32).astype(ml_dtypes.bfloat16)
    low = (table - high.astype(np.float64)).astype(np.float32).astype(ml_dtypes.bfloat16)
    return high, low


def make_tables(seq_len):
    outer = seq_len // LANES
    n_out, k_out = np.meshgrid(np.arange(outer), np.arange(outer), indexing="ij")
    head = np.exp(-2j * np.pi * (n_out * (4 * k_out + 1) % (4 * outer)) / (4 * outer))
    n_in = np.arange(LANES)
    twist = np.exp(-2j * np.pi * np.outer(4 * np.arange(outer) + 1, n_in) / (4 * seq_len))
    tail = np.exp(-2j * np.pi * (np.outer(n_in, n_in) % LANES) / LANES)

    def block(mat):
        return np.block([[mat.real, mat.imag], [-mat.imag, mat.real]])

    fwd_head = np.concatenate([head.real.T, head.imag.T], axis=0)
    high, low = split_np(fwd_head)
    head_tab = np.concatenate([high, high, low], axis=1)
    high, low = split_np(block(tail))
    tail_tab = np.concatenate([high, high, low], axis=0)
    high, low = split_np(block(tail.conj()))
    back_tail_tab = np.concatenate([high, high, low], axis=0)
    high, low = split_np(np.concatenate([head.real, head.imag], axis=1))
    back_head_tab = np.block([[high, high], [low, np.zeros_like(low)]])
    twist_tab = np.concatenate([twist.real, twist.imag], axis=1).astype(np.float32)
    return head_tab, twist_tab, tail_tab, back_tail_tab, back_head_tab


def halves(values):
    high = values.astype(BF16)
    return high, (values - high.astype(F32)).astype(BF16)


def by_rows(values):
    high, low = halves(values)
    return jnp.concatenate([high, low, high], axis=0)


def by_lanes(values):
    high, low = halves(values)
    return jnp.concatenate([high, low, high], axis=1)


def mat(left, right):
    return jnp.dot(left, right, preferred_element_type=F32)


def head_stage(signals, head, twist):
    outer = signals[0].shape[0]
    mixed = mat(head, by_rows(jnp.concatenate(signals, axis=1)))
    cos, sin = twist[:, :LANES], twist[:, LANES:]
    rows = []
    for idx in range(len(signals)):
        real = mixed[:outer, idx * LANES : (idx + 1) * LANES]
        imag = mixed[outer:, idx * LANES : (idx + 1) * LANES]
        rows.append(jnp.concatenate([real * cos - imag * sin, real * sin + imag * cos], axis=1))
    return jnp.concatenate(rows, axis=0)


def product_stage(spec, outer, groups):
    pieces = [spec[idx * outer : (idx + 1) * outer] for idx in range(spec.shape[0] // outer)]
    own = len(pieces) // (groups + 1)
    prods = []
    for idx, mine in enumerate(pieces[own:]):
        other = pieces[idx // groups]
        f_re, f_im = other[:, :LANES], other[:, LANES:]
        d_re, d_im = mine[:, :LANES], mine[:, LANES:]
        prods.append(jnp.concatenate([d_re * f_re - d_im * f_im, d_re * f_im + d_im * f_re], axis=1))
    return jnp.concatenate(prods, axis=0)


def back_stage(back, cos, sin):
    outer = cos.shape[0]
    reals, imags = [], []
    for idx in range(back.shape[0] // outer):
        mine = back[idx * outer : (idx + 1) * outer]
        real, imag = mine[:, :LANES], mine[:, LANES:]
        reals.append(real * cos + imag * sin)
        imags.append(imag * cos - real * sin)
    return jnp.concatenate([jnp.concatenate(reals, axis=1), jnp.concatenate(imags, axis=1)], axis=0)


def pack_kernel(layout, where_ref, key_ref, value_ref, filter_ref, bias_ref, out_ref, bias_out, key, value, taps, sems):
    rows, own, part, groups = layout
    first = where_ref[0] * (part * LANES if part < rows else 0)
    taken = filter_ref.at[pl.ds(pl.multiple_of(first, part * LANES), part * LANES)]
    pairs = ((key_ref, key), (value_ref, value), (taken, taps), (bias_ref, bias_out))
    fetches = [pltpu.make_async_copy(*pair, sems.at[idx]) for idx, pair in enumerate(pairs)]
    for fetch in fetches:
        fetch.start()
    fetches[0].wait()
    fetches[1].wait()
    for row in range(rows):
        span = pl.ds(row * LANES, LANES)
        turned = (key[span, :].astype(F32) * value[span, :].astype(F32)).T
        for peer in range(out_ref.shape[0]):
            out_ref[peer, pl.ds(row, own, stride=rows), :] = turned[peer * own : (peer + 1) * own]
    fetches[2].wait()
    for row in range(part):
        turned = taps[pl.ds(row * LANES, LANES), :].T
        for peer in range(out_ref.shape[0]):
            out_ref[peer, pl.ds(own * rows + row, own, stride=part), :] = turned[peer * own : (peer + 1) * own]
    fetches[3].wait()


def arrived(layout, staged, moved_ref, group, start, height):
    rows, own, part, groups = layout
    if staged:
        start += group * own * (rows + part)
        return moved_ref[:, start : start + height]
    blocks = moved_ref.shape[0] // groups
    return moved_ref[pl.ds(group * blocks, blocks), start : start + height]


def driver_signals(layout, staged, moved_ref, chans):
    rows, own, part, groups = layout
    parts = [
        arrived(layout, staged, moved_ref, group, chan * rows, rows) for chan in chans for group in range(groups)
    ]
    return [values.reshape(values.shape[0] * rows, LANES) for values in parts]


def filter_signals(layout, staged, moved_ref, chans):
    rows, own, part, groups = layout
    signals = []
    for chan in chans:
        pieces = [
            arrived(layout, staged, moved_ref, group, own * rows + chan * part, part)
            for group in range(groups if part < rows else 1)
        ]
        signals.append(jnp.concatenate(pieces, axis=1).reshape(pieces[0].shape[0] * rows, LANES))
    return signals


def conv_kernel(layout, staged, pieces, moved_ref, head_ref, twist_ref, tail_ref, back_tail_ref, back_head_ref, out_ref):
    rows, own, part, groups = layout
    blocks = out_ref.shape[0] // groups
    outer = blocks * rows
    scale = 1.0 / (outer * LANES)
    cos, sin = twist_ref[:, :LANES] * scale, twist_ref[:, LANES:] * scale
    sets = [range(piece * own // pieces, (piece + 1) * own // pieces) for piece in range(pieces)]
    mixed = [
        head_stage(
            filter_signals(layout, staged, moved_ref, chans) + driver_signals(layout, staged, moved_ref, chans),
            head_ref[...],
            twist_ref[...],
        )
        for chans in sets
    ]
    specs = [mat(by_lanes(values), tail_ref[...]) for values in mixed]
    prods = [product_stage(spec, outer, groups) for spec in specs]
    backs = [mat(by_lanes(values), back_tail_ref[...]) for values in prods]
    turned = [back_stage(back, cos, sin) for back in backs]
    results = [mat(back_head_ref[...], jnp.concatenate(halves(values), axis=0)) for values in turned]
    for chans, result in zip(sets, results):
        result = result[:outer] + result[outer:]
        for idx in range(len(chans) * groups):
            chan, group = divmod(idx, groups)
            start = (chans[0] + chan) * rows
            out_ref[pl.ds(group * blocks, blocks), start : start + rows] = result[
                :, idx * LANES : (idx + 1) * LANES
            ].reshape(blocks, rows, LANES)


def gate_kernel(rows, conv_ref, query_ref, key_ref, value_ref, bias_ref, out_ref):
    bias = bias_ref[...]
    for row in range(rows):
        span = pl.ds(row * LANES, LANES)
        driver = key_ref[span, :].astype(F32) * value_ref[span, :].astype(F32)
        convolved = conv_ref[pl.ds(row, LANES, stride=rows), :].T
        out_ref[span, :] = (query_ref[span, :].astype(F32) * (convolved + bias * driver)).astype(BF16)


VMEM = pl.BlockSpec(memory_space=pltpu.VMEM)
HBM = pl.BlockSpec(memory_space=pltpu.HBM)
SMEM = pl.BlockSpec(memory_space=pltpu.SMEM)


def call(kernel, outs, specs, flops, moved, scratch=()):
    return pl.pallas_call(
        kernel,
        out_shape=[jax.ShapeDtypeStruct(*out) for out in outs],
        in_specs=specs,
        out_specs=[VMEM] * len(outs),
        scratch_shapes=scratch,
        compiler_params=pltpu.CompilerParams(vmem_limit_bytes=VMEM_LIMIT),
        cost_estimate=pl.CostEstimate(flops=flops, bytes_accessed=moved, transcendentals=0),
    )


def convolve(groups, blocks, staged, query_proj, key_proj, value_proj, long_filter, skip_bias):
    tokens, chans = key_proj.shape
    rows = tokens // LANES
    count, axes = groups * blocks, ("groups", "seq")
    own = chans // count
    outer = blocks * rows
    seq_len = blocks * tokens
    part = rows // groups
    if rows % groups or own * part % 8:
        part = rows
    layout = (rows, own, part, groups)
    head, twist, tail, back_tail, back_head = (jnp.asarray(table) for table in make_tables(seq_len))
    size = tokens * chans * 4
    macs = 2 * 3 * own * seq_len * (2 * outer + 4 * LANES)
    where = lax.axis_index("groups").reshape(1).astype(jnp.int32)

    def exchange(array):
        return lax.all_to_all(array, axes, 0, 0, tiled=True)

    sources = (key_proj, value_proj, long_filter, skip_bias.reshape(1, chans))
    packed, bias = call(
        functools.partial(pack_kernel, layout),
        [((count, own * (rows + part), LANES), F32), ((1, chans), F32)],
        [SMEM] + [HBM] * 4, size // 4, size * 3,
        [pltpu.VMEM((tokens, chans), BF16), pltpu.VMEM((tokens, chans), BF16), pltpu.VMEM((part * LANES, chans), F32),
         pltpu.SemaphoreType.DMA((4,))],
    )(where, *(pltpu.with_memory_space_constraint(source, pltpu.HBM) for source in sources))
    if staged:
        mine = lax.axis_index("groups")
        height = own * (rows + part)
        by_group = packed.reshape(2, blocks, height, LANES)
        first = mine == 0
        kept = jnp.where(first, by_group[0], by_group[1])
        other = lax.ppermute(jnp.where(first, by_group[1], by_group[0]), "groups", [(0, 1), (1, 0)])
        pair = jnp.concatenate([jnp.where(first, kept, other), jnp.where(first, other, kept)], axis=1)
        moved = lax.all_to_all(pair, "seq", 0, 0, tiled=True)
    else:
        moved = exchange(packed)
    local = call(
        functools.partial(conv_kernel, layout, staged, min(own, 2)),
        [((count, own * rows, LANES), F32)], [VMEM] * 6, 5 * macs, 3 * size,
    )(moved, head, twist, tail, back_tail, back_head)[0]
    convolved = exchange(local).reshape(chans * rows, LANES)
    return call(functools.partial(gate_kernel, rows), [((tokens, chans), BF16)], [VMEM] * 5, size, 3 * size)(
        convolved, query_proj, key_proj, value_proj, bias
    )[0]


def shards(groups, blocks, cores, *args):
    if cores == 1 or groups != 2:
        return convolve(groups, blocks, False, *args)
    return lax.cond(
        lax.axis_index("chan") % 2 == 1,
        functools.partial(convolve, groups, blocks, False),
        functools.partial(convolve, groups, blocks, True),
        *args,
    )


def solution(mesh):
    placed = (
        P(("groups", "seq"), "chan"),
        P(("groups", "seq"), "chan"),
        P(("groups", "seq"), "chan"),
        P("seq", "chan"),
        P("chan"),
    )
    body = functools.partial(shards, *(mesh.shape[axis] for axis in ("groups", "seq", "chan")))
    return jax.shard_map(
        body, mesh=mesh, in_specs=placed, out_specs=P(("groups", "seq"), "chan"), check_vma=False
    )
```

```python
import functools

import jax
import jax.numpy as jnp
import ml_dtypes
import numpy as np
from jax import lax
from jax.experimental import pallas as pl
from jax.experimental.pallas import tpu as pltpu
from jax.sharding import PartitionSpec as P

LANES = 128
BF16 = jnp.bfloat16
F32 = jnp.float32
VMEM_LIMIT = 48 * 2**20


def split_np(table):
    high = table.astype(np.float32).astype(ml_dtypes.bfloat16)
    low = (table - high.astype(np.float64)).astype(np.float32).astype(ml_dtypes.bfloat16)
    return high, low


def make_tables(seq_len):
    outer = seq_len // LANES
    n_out, k_out = np.meshgrid(np.arange(outer), np.arange(outer), indexing="ij")
    head = np.exp(-2j * np.pi * (n_out * (4 * k_out + 1) % (4 * outer)) / (4 * outer))
    n_in = np.arange(LANES)
    twist = np.exp(-2j * np.pi * np.outer(4 * np.arange(outer) + 1, n_in) / (4 * seq_len))
    tail = np.exp(-2j * np.pi * (np.outer(n_in, n_in) % LANES) / LANES)

    def block(mat):
        return np.block([[mat.real, mat.imag], [-mat.imag, mat.real]])

    fwd_head = np.concatenate([head.real.T, head.imag.T], axis=0)
    high, low = split_np(fwd_head)
    head_tab = np.concatenate([high, high, low], axis=1)
    high, low = split_np(block(tail))
    tail_tab = np.concatenate([high, high, low], axis=0)
    high, low = split_np(block(tail.conj()))
    back_tail_tab = np.concatenate([high, high, low], axis=0)
    high, low = split_np(np.concatenate([head.real, head.imag], axis=1))
    back_head_tab = np.block([[high, high], [low, np.zeros_like(low)]])
    twist_tab = np.concatenate([twist.real, twist.imag], axis=1).astype(np.float32)
    return head_tab, twist_tab, tail_tab, back_tail_tab, back_head_tab


def halves(values):
    high = values.astype(BF16)
    return high, (values - high.astype(F32)).astype(BF16)


def by_rows(values):
    high, low = halves(values)
    return jnp.concatenate([high, low, high], axis=0)


def by_lanes(values):
    high, low = halves(values)
    return jnp.concatenate([high, low, high], axis=1)


def mat(left, right):
    return jnp.dot(left, right, preferred_element_type=F32)


def head_stage(signals, head, twist):
    outer = signals[0].shape[0]
    mixed = mat(head, by_rows(jnp.concatenate(signals, axis=1)))
    cos, sin = twist[:, :LANES], twist[:, LANES:]
    rows = []
    for idx in range(len(signals)):
        real = mixed[:outer, idx * LANES : (idx + 1) * LANES]
        imag = mixed[outer:, idx * LANES : (idx + 1) * LANES]
        rows.append(jnp.concatenate([real * cos - imag * sin, real * sin + imag * cos], axis=1))
    return jnp.concatenate(rows, axis=0)


def product_stage(spec, outer, groups):
    pieces = [spec[idx * outer : (idx + 1) * outer] for idx in range(spec.shape[0] // outer)]
    own = len(pieces) // (groups + 1)
    prods = []
    for idx, mine in enumerate(pieces[own:]):
        other = pieces[idx // groups]
        f_re, f_im = other[:, :LANES], other[:, LANES:]
        d_re, d_im = mine[:, :LANES], mine[:, LANES:]
        prods.append(jnp.concatenate([d_re * f_re - d_im * f_im, d_re * f_im + d_im * f_re], axis=1))
    return jnp.concatenate(prods, axis=0)


def back_stage(back, cos, sin):
    outer = cos.shape[0]
    reals, imags = [], []
    for idx in range(back.shape[0] // outer):
        mine = back[idx * outer : (idx + 1) * outer]
        real, imag = mine[:, :LANES], mine[:, LANES:]
        reals.append(real * cos + imag * sin)
        imags.append(imag * cos - real * sin)
    return jnp.concatenate([jnp.concatenate(reals, axis=1), jnp.concatenate(imags, axis=1)], axis=0)


def pack_kernel(layout, staged, where_ref, key_ref, value_ref, filter_ref, bias_ref, *refs):
    rows, own, part, groups = layout
    refs = list(refs)
    out_ref = refs.pop(0)
    filter_out = refs.pop(0) if staged else None
    bias_out, key, value, taps, turned_ref, sems = refs
    first = where_ref[0] * (part * LANES if part < rows else 0)
    taken = filter_ref.at[pl.ds(pl.multiple_of(first, part * LANES), part * LANES)]
    pairs = ((key_ref, key), (value_ref, value), (taken, taps), (bias_ref, bias_out))
    fetches = [pltpu.make_async_copy(*pair, sems.at[idx]) for idx, pair in enumerate(pairs)]
    for fetch in fetches:
        fetch.start()
    fetches[0].wait()
    fetches[1].wait()
    for row in range(rows):
        span = pl.ds(row * LANES, LANES)
        turned = (key[span, :].astype(F32) * value[span, :].astype(F32)).T
        for peer in range(out_ref.shape[0]):
            out_ref[peer, pl.ds(row, own, stride=rows), :] = turned[peer * own : (peer + 1) * own]
    fetches[2].wait()
    for row in range(part):
        turned = taps[pl.ds(row * LANES, LANES), :].T
        if staged:
            turned_ref[row] = turned
            for peer in range(filter_out.shape[0]):
                start = pl.multiple_of((where_ref[0] * filter_out.shape[0] + peer) * own, own)
                filter_out[peer, pl.ds(row, own, stride=part), :] = turned_ref[row, pl.ds(start, own), :]
        else:
            for peer in range(out_ref.shape[0]):
                out_ref[peer, pl.ds(own * rows + row, own, stride=part), :] = turned[peer * own : (peer + 1) * own]
    fetches[3].wait()


def arrived(layout, staged, moved_ref, group, start, height):
    rows, own, part, groups = layout
    if staged:
        start += group * own * rows
        return moved_ref[:, start : start + height]
    blocks = moved_ref.shape[0] // groups
    return moved_ref[pl.ds(group * blocks, blocks), start : start + height]


def driver_signals(layout, staged, moved_ref, chans):
    rows, own, part, groups = layout
    parts = [
        arrived(layout, staged, moved_ref, group, chan * rows, rows) for chan in chans for group in range(groups)
    ]
    return [values.reshape(values.shape[0] * rows, LANES) for values in parts]


def filter_signals(layout, staged, moved_ref, chans):
    rows, own, part, groups = layout
    first = own * rows * (groups if staged else 1)
    signals = []
    for chan in chans:
        pieces = [
            arrived(layout, staged, moved_ref, group, first + chan * part, part)
            for group in range(groups if part < rows else 1)
        ]
        signals.append(jnp.concatenate(pieces, axis=1).reshape(pieces[0].shape[0] * rows, LANES))
    return signals


def conv_kernel(layout, staged, pieces, moved_ref, head_ref, twist_ref, tail_ref, back_tail_ref, back_head_ref, out_ref):
    rows, own, part, groups = layout
    blocks = out_ref.shape[0] // groups
    outer = blocks * rows
    scale = 1.0 / (outer * LANES)
    cos, sin = twist_ref[:, :LANES] * scale, twist_ref[:, LANES:] * scale
    sets = [range(piece * own // pieces, (piece + 1) * own // pieces) for piece in range(pieces)]
    mixed = [
        head_stage(
            filter_signals(layout, staged, moved_ref, chans) + driver_signals(layout, staged, moved_ref, chans),
            head_ref[...],
            twist_ref[...],
        )
        for chans in sets
    ]
    specs = [mat(by_lanes(values), tail_ref[...]) for values in mixed]
    prods = [product_stage(spec, outer, groups) for spec in specs]
    backs = [mat(by_lanes(values), back_tail_ref[...]) for values in prods]
    turned = [back_stage(back, cos, sin) for back in backs]
    results = [mat(back_head_ref[...], jnp.concatenate(halves(values), axis=0)) for values in turned]
    for chans, result in zip(sets, results):
        result = result[:outer] + result[outer:]
        for idx in range(len(chans) * groups):
            chan, group = divmod(idx, groups)
            start = (chans[0] + chan) * rows
            out_ref[pl.ds(group * blocks, blocks), start : start + rows] = result[
                :, idx * LANES : (idx + 1) * LANES
            ].reshape(blocks, rows, LANES)


def gate_kernel(rows, conv_ref, query_ref, key_ref, value_ref, bias_ref, out_ref):
    bias = bias_ref[...]
    for row in range(rows):
        span = pl.ds(row * LANES, LANES)
        driver = key_ref[span, :].astype(F32) * value_ref[span, :].astype(F32)
        convolved = conv_ref[pl.ds(row, LANES, stride=rows), :].T
        out_ref[span, :] = (query_ref[span, :].astype(F32) * (convolved + bias * driver)).astype(BF16)


VMEM = pl.BlockSpec(memory_space=pltpu.VMEM)
HBM = pl.BlockSpec(memory_space=pltpu.HBM)
SMEM = pl.BlockSpec(memory_space=pltpu.SMEM)


def call(kernel, outs, specs, flops, moved, scratch=()):
    return pl.pallas_call(
        kernel,
        out_shape=[jax.ShapeDtypeStruct(*out) for out in outs],
        in_specs=specs,
        out_specs=[VMEM] * len(outs),
        scratch_shapes=scratch,
        compiler_params=pltpu.CompilerParams(vmem_limit_bytes=VMEM_LIMIT),
        cost_estimate=pl.CostEstimate(flops=flops, bytes_accessed=moved, transcendentals=0),
    )


def convolve(groups, blocks, staged, query_proj, key_proj, value_proj, long_filter, skip_bias):
    tokens, chans = key_proj.shape
    rows = tokens // LANES
    count, axes = groups * blocks, ("groups", "seq")
    own = chans // count
    outer = blocks * rows
    seq_len = blocks * tokens
    part = rows // groups
    if staged or rows % groups or own * part % 8:
        part = rows
    layout = (rows, own, part, groups)
    head, twist, tail, back_tail, back_head = (jnp.asarray(table) for table in make_tables(seq_len))
    size = tokens * chans * 4
    macs = 2 * 3 * own * seq_len * (2 * outer + 4 * LANES)
    where = lax.axis_index("groups").reshape(1).astype(jnp.int32)

    def exchange(array):
        return lax.all_to_all(array, axes, 0, 0, tiled=True)

    sources = (key_proj, value_proj, long_filter, skip_bias.reshape(1, chans))
    if staged:
        outs = [((count, own * rows, LANES), F32), ((blocks, own * rows, LANES), F32)]
    else:
        outs = [((count, own * (rows + part), LANES), F32)]
    packed, *filter_blocks, bias = call(
        functools.partial(pack_kernel, layout, staged), outs + [((1, chans), F32)],
        [SMEM] + [HBM] * 4, size // 4, size * 3,
        [pltpu.VMEM((tokens, chans), BF16), pltpu.VMEM((tokens, chans), BF16), pltpu.VMEM((part * LANES, chans), F32),
         pltpu.VMEM((part, chans, LANES), F32), pltpu.SemaphoreType.DMA((4,))],
    )(where, *(pltpu.with_memory_space_constraint(source, pltpu.HBM) for source in sources))
    if staged:
        mine = lax.axis_index("groups")
        by_group = packed.reshape(2, blocks, own * rows, LANES)
        first = mine == 0
        kept = jnp.where(first, by_group[0], by_group[1])
        other = lax.ppermute(jnp.where(first, by_group[1], by_group[0]), "groups", [(0, 1), (1, 0)])
        pair = [jnp.where(first, kept, other), jnp.where(first, other, kept)]
        pair = jnp.concatenate(pair + filter_blocks, axis=1)
        moved = lax.all_to_all(pair, "seq", 0, 0, tiled=True)
    else:
        moved = exchange(packed)
    local = call(
        functools.partial(conv_kernel, layout, staged, min(own, 2)),
        [((count, own * rows, LANES), F32)], [VMEM] * 6, 5 * macs, 3 * size,
    )(moved, head, twist, tail, back_tail, back_head)[0]
    convolved = exchange(local).reshape(chans * rows, LANES)
    return call(functools.partial(gate_kernel, rows), [((tokens, chans), BF16)], [VMEM] * 5, size, 3 * size)(
        convolved, query_proj, key_proj, value_proj, bias
    )[0]


def shards(groups, blocks, cores, *args):
    if cores == 1 or groups != 2:
        return convolve(groups, blocks, False, *args)
    return lax.cond(
        lax.axis_index("chan") % 2 == 1,
        functools.partial(convolve, groups, blocks, False),
        functools.partial(convolve, groups, blocks, True),
        *args,
    )


def solution(mesh):
    placed = (
        P(("groups", "seq"), "chan"),
        P(("groups", "seq"), "chan"),
        P(("groups", "seq"), "chan"),
        P("seq", "chan"),
        P("chan"),
    )
    body = functools.partial(shards, *(mesh.shape[axis] for axis in ("groups", "seq", "chan")))
    return jax.shard_map(
        body, mesh=mesh, in_specs=placed, out_specs=P(("groups", "seq"), "chan"), check_vma=False
    )
```

```python
import functools

import jax
import jax.numpy as jnp
import ml_dtypes
import numpy as np
from jax import lax
from jax.experimental import pallas as pl
from jax.experimental.pallas import tpu as pltpu
from jax.sharding import PartitionSpec as P

LANES = 128
BF16 = jnp.bfloat16
F32 = jnp.float32
VMEM_LIMIT = 48 * 2**20


def split_np(table):
    high = table.astype(np.float32).astype(ml_dtypes.bfloat16)
    low = (table - high.astype(np.float64)).astype(np.float32).astype(ml_dtypes.bfloat16)
    return high, low


def make_tables(seq_len):
    outer = seq_len // LANES
    n_out, k_out = np.meshgrid(np.arange(outer), np.arange(outer), indexing="ij")
    head = np.exp(-2j * np.pi * (n_out * (4 * k_out + 1) % (4 * outer)) / (4 * outer))
    n_in = np.arange(LANES)
    twist = np.exp(-2j * np.pi * np.outer(4 * np.arange(outer) + 1, n_in) / (4 * seq_len))
    tail = np.exp(-2j * np.pi * (np.outer(n_in, n_in) % LANES) / LANES)

    def block(mat):
        return np.block([[mat.real, mat.imag], [-mat.imag, mat.real]])

    fwd_head = np.concatenate([head.real.T, head.imag.T], axis=0)
    high, low = split_np(fwd_head)
    head_tab = np.concatenate([high, high, low], axis=1)
    high, low = split_np(block(tail))
    tail_tab = np.concatenate([high, high, low], axis=0)
    high, low = split_np(block(tail.conj()))
    back_tail_tab = np.concatenate([high, high, low], axis=0)
    high, low = split_np(np.concatenate([head.real, head.imag], axis=1))
    back_head_tab = np.block([[high, high], [low, np.zeros_like(low)]])
    twist_tab = np.concatenate([twist.real, twist.imag], axis=1).astype(np.float32)
    return head_tab, twist_tab, tail_tab, back_tail_tab, back_head_tab


def halves(values):
    high = values.astype(BF16)
    return high, (values - high.astype(F32)).astype(BF16)


def by_rows(values):
    high, low = halves(values)
    return jnp.concatenate([high, low, high], axis=0)


def by_lanes(values):
    high, low = halves(values)
    return jnp.concatenate([high, low, high], axis=1)


def mat(left, right):
    return jnp.dot(left, right, preferred_element_type=F32)


def head_stage(signals, head, twist):
    outer = signals[0].shape[0]
    mixed = mat(head, by_rows(jnp.concatenate(signals, axis=1)))
    cos, sin = twist[:, :LANES], twist[:, LANES:]
    rows = []
    for idx in range(len(signals)):
        real = mixed[:outer, idx * LANES : (idx + 1) * LANES]
        imag = mixed[outer:, idx * LANES : (idx + 1) * LANES]
        rows.append(jnp.concatenate([real * cos - imag * sin, real * sin + imag * cos], axis=1))
    return jnp.concatenate(rows, axis=0)


def product_stage(spec, outer, groups):
    pieces = [spec[idx * outer : (idx + 1) * outer] for idx in range(spec.shape[0] // outer)]
    own = len(pieces) // (groups + 1)
    prods = []
    for idx, mine in enumerate(pieces[own:]):
        other = pieces[idx // groups]
        f_re, f_im = other[:, :LANES], other[:, LANES:]
        d_re, d_im = mine[:, :LANES], mine[:, LANES:]
        prods.append(jnp.concatenate([d_re * f_re - d_im * f_im, d_re * f_im + d_im * f_re], axis=1))
    return jnp.concatenate(prods, axis=0)


def back_stage(back, cos, sin):
    outer = cos.shape[0]
    reals, imags = [], []
    for idx in range(back.shape[0] // outer):
        mine = back[idx * outer : (idx + 1) * outer]
        real, imag = mine[:, :LANES], mine[:, LANES:]
        reals.append(real * cos + imag * sin)
        imags.append(imag * cos - real * sin)
    return jnp.concatenate([jnp.concatenate(reals, axis=1), jnp.concatenate(imags, axis=1)], axis=0)


def place_of(halved, groups, blocks, peer):
    group, block = divmod(peer, blocks)
    side, inner = divmod(block, blocks // 2)
    return side * (groups * blocks // 2) + group * (blocks // 2) + inner if halved else peer


def chans_of(halved, groups, blocks, peer):
    group, block = divmod(peer, blocks)
    side, inner = divmod(block, blocks // 2)
    return (group * (blocks // 2) + inner) * 2 + side if halved else peer


def pack_kernel(layout, halved_in, halved_out, where_ref, key_ref, value_ref, filter_ref, bias_ref, out_ref, bias_out, key, value, taps, sems):
    rows, own, part, groups = layout
    count = out_ref.shape[0]
    homes = [
        (
            place_of(halved_in, groups, count // groups, peer),
            chans_of(halved_out, groups, count // groups, peer) * own,
        )
        for peer in range(count)
    ]
    first = where_ref[0] * (part * LANES if part < rows else 0)
    taken = filter_ref.at[pl.ds(pl.multiple_of(first, part * LANES), part * LANES)]
    pairs = ((key_ref, key), (value_ref, value), (taken, taps), (bias_ref, bias_out))
    fetches = [pltpu.make_async_copy(*pair, sems.at[idx]) for idx, pair in enumerate(pairs)]
    for fetch in fetches:
        fetch.start()
    fetches[0].wait()
    fetches[1].wait()
    for row in range(rows):
        span = pl.ds(row * LANES, LANES)
        turned = (key[span, :].astype(F32) * value[span, :].astype(F32)).T
        for place, chan in homes:
            out_ref[place, pl.ds(row, own, stride=rows), :] = turned[chan : chan + own]
    fetches[2].wait()
    for row in range(part):
        turned = taps[pl.ds(row * LANES, LANES), :].T
        for place, chan in homes:
            out_ref[place, pl.ds(own * rows + row, own, stride=part), :] = turned[chan : chan + own]
    fetches[3].wait()


def arrived(layout, halved, moved_ref, group, start, height):
    rows, own, part, groups = layout
    span = pl.ds(group * (moved_ref.shape[0] // groups), moved_ref.shape[0] // groups)
    if not halved:
        return moved_ref[span, start : start + height]
    second = start + own * (rows + part)
    return jnp.concatenate(
        [moved_ref[span, start : start + height], moved_ref[span, second : second + height]], axis=0
    )


def driver_signals(layout, halved, moved_ref, chans):
    rows, own, part, groups = layout
    parts = [
        arrived(layout, halved, moved_ref, group, chan * rows, rows) for chan in chans for group in range(groups)
    ]
    return [values.reshape(values.shape[0] * rows, LANES) for values in parts]


def filter_signals(layout, halved, moved_ref, chans):
    rows, own, part, groups = layout
    signals = []
    for chan in chans:
        pieces = [
            arrived(layout, halved, moved_ref, group, own * rows + chan * part, part)
            for group in range(groups if part < rows else 1)
        ]
        signals.append(jnp.concatenate(pieces, axis=1).reshape(pieces[0].shape[0] * rows, LANES))
    return signals


def conv_kernel(layout, halved, halved_out, pieces, moved_ref, head_ref, twist_ref, tail_ref, back_tail_ref, back_head_ref, out_ref):
    rows, own, part, groups = layout
    blocks = out_ref.shape[0] // groups
    outer = blocks * rows
    scale = 1.0 / (outer * LANES)
    cos, sin = twist_ref[:, :LANES] * scale, twist_ref[:, LANES:] * scale
    sets = [range(piece * own // pieces, (piece + 1) * own // pieces) for piece in range(pieces)]
    mixed = [
        head_stage(
            filter_signals(layout, halved, moved_ref, chans) + driver_signals(layout, halved, moved_ref, chans),
            head_ref[...],
            twist_ref[...],
        )
        for chans in sets
    ]
    specs = [mat(by_lanes(values), tail_ref[...]) for values in mixed]
    prods = [product_stage(spec, outer, groups) for spec in specs]
    backs = [mat(by_lanes(values), back_tail_ref[...]) for values in prods]
    turned = [back_stage(back, cos, sin) for back in backs]
    results = [mat(back_head_ref[...], jnp.concatenate(halves(values), axis=0)) for values in turned]
    for chans, result in zip(sets, results):
        result = result[:outer] + result[outer:]
        for idx in range(len(chans) * groups):
            chan, group = divmod(idx, groups)
            start = (chans[0] + chan) * rows
            values = result[:, idx * LANES : (idx + 1) * LANES].reshape(blocks, rows, LANES)
            if halved_out:
                inner = blocks // 2
                for side in range(2):
                    place = side * groups * inner + group * inner
                    out_ref[place : place + inner, start : start + rows] = values[side * inner : (side + 1) * inner]
            else:
                out_ref[group * blocks : (group + 1) * blocks, start : start + rows] = values


def gate_kernel(rows, conv_ref, query_ref, key_ref, value_ref, bias_ref, out_ref):
    bias = bias_ref[...]
    for row in range(rows):
        span = pl.ds(row * LANES, LANES)
        driver = key_ref[span, :].astype(F32) * value_ref[span, :].astype(F32)
        convolved = conv_ref[pl.ds(row, LANES, stride=rows), :].T
        out_ref[span, :] = (query_ref[span, :].astype(F32) * (convolved + bias * driver)).astype(BF16)


VMEM = pl.BlockSpec(memory_space=pltpu.VMEM)
HBM = pl.BlockSpec(memory_space=pltpu.HBM)
SMEM = pl.BlockSpec(memory_space=pltpu.SMEM)


def call(kernel, outs, specs, flops, moved, scratch=()):
    return pl.pallas_call(
        kernel,
        out_shape=[jax.ShapeDtypeStruct(*out) for out in outs],
        in_specs=specs,
        out_specs=[VMEM] * len(outs),
        scratch_shapes=scratch,
        compiler_params=pltpu.CompilerParams(vmem_limit_bytes=VMEM_LIMIT),
        cost_estimate=pl.CostEstimate(flops=flops, bytes_accessed=moved, transcendentals=0),
    )


def convolve(groups, blocks, halved_in, halved_out, query_proj, key_proj, value_proj, long_filter, skip_bias):
    tokens, chans = key_proj.shape
    rows = tokens // LANES
    count, axes = groups * blocks, ("groups", "seq")
    own = chans // count
    outer = blocks * rows
    seq_len = blocks * tokens
    part = rows // groups
    if rows % groups or own * part % 8:
        part = rows
    layout = (rows, own, part, groups)
    head, twist, tail, back_tail, back_head = (jnp.asarray(table) for table in make_tables(seq_len))
    size = tokens * chans * 4
    macs = 2 * 3 * own * seq_len * (2 * outer + 4 * LANES)
    where = lax.axis_index("groups").reshape(1).astype(jnp.int32)

    def exchange(array, halved):
        if not halved:
            return lax.all_to_all(array, axes, 0, 0, tiled=True)
        inner = blocks // 2
        low = lax.axis_index("seq") < inner
        by_side = array.reshape(2, count // 2, array.shape[1], LANES)
        kept = jnp.where(low, by_side[0], by_side[1])
        swap = [(block, (block + inner) % blocks) for block in range(blocks)]
        other = lax.ppermute(jnp.where(low, by_side[1], by_side[0]), "seq", swap)
        pair = jnp.concatenate([jnp.where(low, kept, other), jnp.where(low, other, kept)], axis=1)
        sides = [
            [group * blocks + side * inner + block for group in range(groups) for block in range(inner)]
            for side in range(2)
        ]
        return lax.all_to_all(pair, axes, 0, 0, axis_index_groups=sides, tiled=True)

    sources = (key_proj, value_proj, long_filter, skip_bias.reshape(1, chans))
    packed, bias = call(
        functools.partial(pack_kernel, layout, halved_in, halved_out),
        [((count, own * (rows + part), LANES), F32), ((1, chans), F32)],
        [SMEM] + [HBM] * 4, size // 4, size * 3,
        [pltpu.VMEM((tokens, chans), BF16), pltpu.VMEM((tokens, chans), BF16), pltpu.VMEM((part * LANES, chans), F32),
         pltpu.SemaphoreType.DMA((4,))],
    )(where, *(pltpu.with_memory_space_constraint(source, pltpu.HBM) for source in sources))
    moved = exchange(packed, halved_in)
    local = call(
        functools.partial(conv_kernel, layout, halved_in, halved_out, min(own, 2)),
        [((count, own * rows, LANES), F32)], [VMEM] * 6, 5 * macs, 3 * size,
    )(moved, head, twist, tail, back_tail, back_head)[0]
    convolved = exchange(local, halved_out).reshape(chans * rows, LANES)
    return call(functools.partial(gate_kernel, rows), [((tokens, chans), BF16)], [VMEM] * 5, size, 3 * size)(
        convolved, query_proj, key_proj, value_proj, bias
    )[0]


def shards(groups, blocks, cores, *args):
    if cores == 1 or blocks % 2:
        return convolve(groups, blocks, False, False, *args)
    return lax.cond(
        lax.axis_index("chan") % 2 == 1,
        functools.partial(convolve, groups, blocks, False, False),
        functools.partial(convolve, groups, blocks, True, False),
        *args,
    )


def solution(mesh):
    placed = (
        P(("groups", "seq"), "chan"),
        P(("groups", "seq"), "chan"),
        P(("groups", "seq"), "chan"),
        P("seq", "chan"),
        P("chan"),
    )
    body = functools.partial(shards, *(mesh.shape[axis] for axis in ("groups", "seq", "chan")))
    return jax.shard_map(
        body, mesh=mesh, in_specs=placed, out_specs=P(("groups", "seq"), "chan"), check_vma=False
    )
```

```python
import functools

import jax
import jax.numpy as jnp
import ml_dtypes
import numpy as np
from jax import lax
from jax.experimental import pallas as pl
from jax.experimental.pallas import tpu as pltpu
from jax.sharding import PartitionSpec as P

LANES = 128
BF16 = jnp.bfloat16
F32 = jnp.float32
VMEM_LIMIT = 48 * 2**20


def split_np(table):
    high = table.astype(np.float32).astype(ml_dtypes.bfloat16)
    low = (table - high.astype(np.float64)).astype(np.float32).astype(ml_dtypes.bfloat16)
    return high, low


def make_tables(seq_len):
    outer = seq_len // LANES
    n_out, k_out = np.meshgrid(np.arange(outer), np.arange(outer), indexing="ij")
    head = np.exp(-2j * np.pi * (n_out * (4 * k_out + 1) % (4 * outer)) / (4 * outer))
    n_in = np.arange(LANES)
    twist = np.exp(-2j * np.pi * np.outer(4 * np.arange(outer) + 1, n_in) / (4 * seq_len))
    tail = np.exp(-2j * np.pi * (np.outer(n_in, n_in) % LANES) / LANES)

    def block(mat):
        return np.block([[mat.real, mat.imag], [-mat.imag, mat.real]])

    fwd_head = np.concatenate([head.real.T, head.imag.T], axis=0)
    high, low = split_np(fwd_head)
    head_tab = np.concatenate([high, high, low], axis=1)
    high, low = split_np(block(tail))
    tail_tab = np.concatenate([high, high, low], axis=0)
    high, low = split_np(block(tail.conj()))
    back_tail_tab = np.concatenate([high, high, low], axis=0)
    high, low = split_np(np.concatenate([head.real, head.imag], axis=1))
    back_head_tab = np.block([[high, high], [low, np.zeros_like(low)]])
    twist_tab = np.concatenate([twist.real, twist.imag], axis=1).astype(np.float32)
    return head_tab, twist_tab, tail_tab, back_tail_tab, back_head_tab


def halves(values):
    high = values.astype(BF16)
    return high, (values - high.astype(F32)).astype(BF16)


def by_rows(values):
    high, low = halves(values)
    return jnp.concatenate([high, low, high], axis=0)


def by_lanes(values):
    high, low = halves(values)
    return jnp.concatenate([high, low, high], axis=1)


def mat(left, right):
    return jnp.dot(left, right, preferred_element_type=F32)


def head_stage(signals, head, twist):
    outer = signals[0].shape[0]
    mixed = mat(head, by_rows(jnp.concatenate(signals, axis=1)))
    cos, sin = twist[:, :LANES], twist[:, LANES:]
    rows = []
    for idx in range(len(signals)):
        real = mixed[:outer, idx * LANES : (idx + 1) * LANES]
        imag = mixed[outer:, idx * LANES : (idx + 1) * LANES]
        rows.append(jnp.concatenate([real * cos - imag * sin, real * sin + imag * cos], axis=1))
    return jnp.concatenate(rows, axis=0)


def product_stage(spec, outer, groups):
    pieces = [spec[idx * outer : (idx + 1) * outer] for idx in range(spec.shape[0] // outer)]
    own = len(pieces) // (groups + 1)
    prods = []
    for idx, mine in enumerate(pieces[own:]):
        other = pieces[idx // groups]
        f_re, f_im = other[:, :LANES], other[:, LANES:]
        d_re, d_im = mine[:, :LANES], mine[:, LANES:]
        prods.append(jnp.concatenate([d_re * f_re - d_im * f_im, d_re * f_im + d_im * f_re], axis=1))
    return jnp.concatenate(prods, axis=0)


def back_stage(back, cos, sin):
    outer = cos.shape[0]
    reals, imags = [], []
    for idx in range(back.shape[0] // outer):
        mine = back[idx * outer : (idx + 1) * outer]
        real, imag = mine[:, :LANES], mine[:, LANES:]
        reals.append(real * cos + imag * sin)
        imags.append(imag * cos - real * sin)
    return jnp.concatenate([jnp.concatenate(reals, axis=1), jnp.concatenate(imags, axis=1)], axis=0)


def place_of(halved, groups, blocks, peer):
    group, block = divmod(peer, blocks)
    side, inner = divmod(block, blocks // 2)
    return (group * (blocks // 2) + inner) * 2 + side if halved else peer


def pack_kernel(layout, halved, where_ref, key_ref, value_ref, filter_ref, bias_ref, out_ref, bias_out, key, value, taps, sems):
    rows, own, part, groups = layout
    count = out_ref.shape[0]
    homes = [(place_of(halved, groups, count // groups, peer), peer * own) for peer in range(count)]
    first = where_ref[0] * (part * LANES if part < rows else 0)
    taken = filter_ref.at[pl.ds(pl.multiple_of(first, part * LANES), part * LANES)]
    pairs = ((key_ref, key), (value_ref, value), (taken, taps), (bias_ref, bias_out))
    fetches = [pltpu.make_async_copy(*pair, sems.at[idx]) for idx, pair in enumerate(pairs)]
    for fetch in fetches:
        fetch.start()
    fetches[0].wait()
    fetches[1].wait()
    for row in range(rows):
        span = pl.ds(row * LANES, LANES)
        turned = (key[span, :].astype(F32) * value[span, :].astype(F32)).T
        for place, chan in homes:
            out_ref[place, pl.ds(row, own, stride=rows), :] = turned[chan : chan + own]
    fetches[2].wait()
    for row in range(part):
        turned = taps[pl.ds(row * LANES, LANES), :].T
        for place, chan in homes:
            out_ref[place, pl.ds(own * rows + row, own, stride=part), :] = turned[chan : chan + own]
    fetches[3].wait()


def arrived(layout, halved, moved_ref, group, start, height):
    rows, own, part, groups = layout
    span = pl.ds(group * (moved_ref.shape[0] // groups), moved_ref.shape[0] // groups)
    if not halved:
        return moved_ref[span, start : start + height]
    second = start + own * (rows + part)
    return jnp.concatenate(
        [moved_ref[span, start : start + height], moved_ref[span, second : second + height]], axis=0
    )


def driver_signals(layout, halved, moved_ref, chans):
    rows, own, part, groups = layout
    parts = [
        arrived(layout, halved, moved_ref, group, chan * rows, rows) for chan in chans for group in range(groups)
    ]
    return [values.reshape(values.shape[0] * rows, LANES) for values in parts]


def filter_signals(layout, halved, moved_ref, chans):
    rows, own, part, groups = layout
    signals = []
    for chan in chans:
        pieces = [
            arrived(layout, halved, moved_ref, group, own * rows + chan * part, part)
            for group in range(groups if part < rows else 1)
        ]
        signals.append(jnp.concatenate(pieces, axis=1).reshape(pieces[0].shape[0] * rows, LANES))
    return signals


def conv_kernel(layout, halved, pieces, moved_ref, head_ref, twist_ref, tail_ref, back_tail_ref, back_head_ref, out_ref):
    rows, own, part, groups = layout
    blocks = out_ref.shape[0] // groups
    outer = blocks * rows
    scale = 1.0 / (outer * LANES)
    cos, sin = twist_ref[:, :LANES] * scale, twist_ref[:, LANES:] * scale
    sets = [range(piece * own // pieces, (piece + 1) * own // pieces) for piece in range(pieces)]
    mixed = [
        head_stage(
            filter_signals(layout, halved, moved_ref, chans) + driver_signals(layout, halved, moved_ref, chans),
            head_ref[...],
            twist_ref[...],
        )
        for chans in sets
    ]
    specs = [mat(by_lanes(values), tail_ref[...]) for values in mixed]
    prods = [product_stage(spec, outer, groups) for spec in specs]
    backs = [mat(by_lanes(values), back_tail_ref[...]) for values in prods]
    turned = [back_stage(back, cos, sin) for back in backs]
    results = [mat(back_head_ref[...], jnp.concatenate(halves(values), axis=0)) for values in turned]
    for chans, result in zip(sets, results):
        result = result[:outer] + result[outer:]
        for idx in range(len(chans) * groups):
            chan, group = divmod(idx, groups)
            start = (chans[0] + chan) * rows
            values = result[:, idx * LANES : (idx + 1) * LANES].reshape(blocks, rows, LANES)
            out_ref[group * blocks : (group + 1) * blocks, start : start + rows] = values


def gate_kernel(rows, conv_ref, query_ref, key_ref, value_ref, bias_ref, out_ref):
    bias = bias_ref[...]
    for row in range(rows):
        span = pl.ds(row * LANES, LANES)
        driver = key_ref[span, :].astype(F32) * value_ref[span, :].astype(F32)
        convolved = conv_ref[pl.ds(row, LANES, stride=rows), :].T
        out_ref[span, :] = (query_ref[span, :].astype(F32) * (convolved + bias * driver)).astype(BF16)


VMEM = pl.BlockSpec(memory_space=pltpu.VMEM)
HBM = pl.BlockSpec(memory_space=pltpu.HBM)
SMEM = pl.BlockSpec(memory_space=pltpu.SMEM)


def call(kernel, outs, specs, flops, moved, scratch=()):
    return pl.pallas_call(
        kernel,
        out_shape=[jax.ShapeDtypeStruct(*out) for out in outs],
        in_specs=specs,
        out_specs=[VMEM] * len(outs),
        scratch_shapes=scratch,
        compiler_params=pltpu.CompilerParams(vmem_limit_bytes=VMEM_LIMIT),
        cost_estimate=pl.CostEstimate(flops=flops, bytes_accessed=moved, transcendentals=0),
    )


def convolve(groups, blocks, halved, query_proj, key_proj, value_proj, long_filter, skip_bias):
    tokens, chans = key_proj.shape
    rows = tokens // LANES
    count, axes = groups * blocks, ("groups", "seq")
    own = chans // count
    outer = blocks * rows
    seq_len = blocks * tokens
    part = rows // groups
    if rows % groups or own * part % 8:
        part = rows
    layout = (rows, own, part, groups)
    head, twist, tail, back_tail, back_head = (jnp.asarray(table) for table in make_tables(seq_len))
    size = tokens * chans * 4
    macs = 2 * 3 * own * seq_len * (2 * outer + 4 * LANES)
    where = lax.axis_index("groups").reshape(1).astype(jnp.int32)

    def exchange(array):
        return lax.all_to_all(array, axes, 0, 0, tiled=True)

    def exchange_halved(array):
        inner, height = blocks // 2, array.shape[1]
        sides = [
            [group * blocks + side * inner + block for group in range(groups) for block in range(inner)]
            for side in range(2)
        ]
        inside = lax.all_to_all(
            array.reshape(count // 2, 2 * height, LANES), axes, 0, 0, axis_index_groups=sides, tiled=True
        )
        low = lax.axis_index("seq") < inner
        to_low, to_high = inside[:, :height], inside[:, height:]
        kept = jnp.where(low, to_low, to_high)
        swap = [(block, (block + inner) % blocks) for block in range(blocks)]
        other = lax.ppermute(jnp.where(low, to_high, to_low), "seq", swap)
        return jnp.concatenate([jnp.where(low, kept, other), jnp.where(low, other, kept)], axis=1)

    sources = (key_proj, value_proj, long_filter, skip_bias.reshape(1, chans))
    packed, bias = call(
        functools.partial(pack_kernel, layout, halved),
        [((count, own * (rows + part), LANES), F32), ((1, chans), F32)],
        [SMEM] + [HBM] * 4, size // 4, size * 3,
        [pltpu.VMEM((tokens, chans), BF16), pltpu.VMEM((tokens, chans), BF16), pltpu.VMEM((part * LANES, chans), F32),
         pltpu.SemaphoreType.DMA((4,))],
    )(where, *(pltpu.with_memory_space_constraint(source, pltpu.HBM) for source in sources))
    moved = (exchange_halved if halved else exchange)(packed)
    local = call(
        functools.partial(conv_kernel, layout, halved, min(own, 2)),
        [((count, own * rows, LANES), F32)], [VMEM] * 6, 5 * macs, 3 * size,
    )(moved, head, twist, tail, back_tail, back_head)[0]
    convolved = exchange(local).reshape(chans * rows, LANES)
    return call(functools.partial(gate_kernel, rows), [((tokens, chans), BF16)], [VMEM] * 5, size, 3 * size)(
        convolved, query_proj, key_proj, value_proj, bias
    )[0]


def shards(groups, blocks, cores, *args):
    if cores == 1 or blocks % 2:
        return convolve(groups, blocks, False, *args)
    return lax.cond(
        lax.axis_index("chan") % 2 == 1,
        functools.partial(convolve, groups, blocks, False),
        functools.partial(convolve, groups, blocks, True),
        *args,
    )


def solution(mesh):
    placed = (
        P(("groups", "seq"), "chan"),
        P(("groups", "seq"), "chan"),
        P(("groups", "seq"), "chan"),
        P("seq", "chan"),
        P("chan"),
    )
    body = functools.partial(shards, *(mesh.shape[axis] for axis in ("groups", "seq", "chan")))
    return jax.shard_map(
        body, mesh=mesh, in_specs=placed, out_specs=P(("groups", "seq"), "chan"), check_vma=False
    )
```

```python
import functools

import jax
import jax.numpy as jnp
import ml_dtypes
import numpy as np
from jax import lax
from jax.experimental import pallas as pl
from jax.experimental.pallas import tpu as pltpu
from jax.sharding import PartitionSpec as P

LANES = 128
BF16 = jnp.bfloat16
F32 = jnp.float32
VMEM_LIMIT = 48 * 2**20


def split_np(table):
    high = table.astype(np.float32).astype(ml_dtypes.bfloat16)
    low = (table - high.astype(np.float64)).astype(np.float32).astype(ml_dtypes.bfloat16)
    return high, low


def make_tables(seq_len):
    outer = seq_len // LANES
    n_out, k_out = np.meshgrid(np.arange(outer), np.arange(outer), indexing="ij")
    head = np.exp(-2j * np.pi * (n_out * (4 * k_out + 1) % (4 * outer)) / (4 * outer))
    n_in = np.arange(LANES)
    twist = np.exp(-2j * np.pi * np.outer(4 * np.arange(outer) + 1, n_in) / (4 * seq_len))
    tail = np.exp(-2j * np.pi * (np.outer(n_in, n_in) % LANES) / LANES)

    def block(mat):
        return np.block([[mat.real, mat.imag], [-mat.imag, mat.real]])

    fwd_head = np.concatenate([head.real.T, head.imag.T], axis=0)
    high, low = split_np(fwd_head)
    head_tab = np.concatenate([high, high, low], axis=1)
    high, low = split_np(block(tail))
    tail_tab = np.concatenate([high, high, low], axis=0)
    high, low = split_np(block(tail.conj()))
    back_tail_tab = np.concatenate([high, high, low], axis=0)
    high, low = split_np(np.concatenate([head.real, head.imag], axis=1))
    back_head_tab = np.block([[high, high], [low, np.zeros_like(low)]])
    twist_tab = np.concatenate([twist.real, twist.imag], axis=1).astype(np.float32)
    return head_tab, twist_tab, tail_tab, back_tail_tab, back_head_tab


def halves(values):
    high = values.astype(BF16)
    return high, (values - high.astype(F32)).astype(BF16)


def by_rows(values):
    high, low = halves(values)
    return jnp.concatenate([high, low, high], axis=0)


def by_lanes(values):
    high, low = halves(values)
    return jnp.concatenate([high, low, high], axis=1)


def mat(left, right):
    return jnp.dot(left, right, preferred_element_type=F32)


def head_stage(signals, head, twist):
    outer = signals[0].shape[0]
    mixed = mat(head, by_rows(jnp.concatenate(signals, axis=1)))
    cos, sin = twist[:, :LANES], twist[:, LANES:]
    rows = []
    for idx in range(len(signals)):
        real = mixed[:outer, idx * LANES : (idx + 1) * LANES]
        imag = mixed[outer:, idx * LANES : (idx + 1) * LANES]
        rows.append(jnp.concatenate([real * cos - imag * sin, real * sin + imag * cos], axis=1))
    return jnp.concatenate(rows, axis=0)


def product_stage(spec, outer, groups):
    pieces = [spec[idx * outer : (idx + 1) * outer] for idx in range(spec.shape[0] // outer)]
    own = len(pieces) // (groups + 1)
    prods = []
    for idx, mine in enumerate(pieces[own:]):
        other = pieces[idx // groups]
        f_re, f_im = other[:, :LANES], other[:, LANES:]
        d_re, d_im = mine[:, :LANES], mine[:, LANES:]
        prods.append(jnp.concatenate([d_re * f_re - d_im * f_im, d_re * f_im + d_im * f_re], axis=1))
    return jnp.concatenate(prods, axis=0)


def back_stage(back, cos, sin):
    outer = cos.shape[0]
    reals, imags = [], []
    for idx in range(back.shape[0] // outer):
        mine = back[idx * outer : (idx + 1) * outer]
        real, imag = mine[:, :LANES], mine[:, LANES:]
        reals.append(real * cos + imag * sin)
        imags.append(imag * cos - real * sin)
    return jnp.concatenate([jnp.concatenate(reals, axis=1), jnp.concatenate(imags, axis=1)], axis=0)


def pack_kernel(layout, where_ref, key_ref, value_ref, filter_ref, bias_ref, out_ref, bias_out, key, value, taps, sems):
    rows, own, part, groups = layout
    first = where_ref[0] * (part * LANES if part < rows else 0)
    taken = filter_ref.at[pl.ds(pl.multiple_of(first, part * LANES), part * LANES)]
    pairs = ((key_ref, key), (value_ref, value), (taken, taps), (bias_ref, bias_out))
    fetches = [pltpu.make_async_copy(*pair, sems.at[idx]) for idx, pair in enumerate(pairs)]
    for fetch in fetches:
        fetch.start()
    fetches[0].wait()
    fetches[1].wait()
    for row in range(rows):
        span = pl.ds(row * LANES, LANES)
        turned = (key[span, :].astype(F32) * value[span, :].astype(F32)).T
        for peer in range(out_ref.shape[0]):
            out_ref[peer, pl.ds(row, own, stride=rows), :] = turned[peer * own : (peer + 1) * own]
    fetches[2].wait()
    for row in range(part):
        turned = taps[pl.ds(row * LANES, LANES), :].T
        for peer in range(out_ref.shape[0]):
            out_ref[peer, pl.ds(own * rows + row, own, stride=part), :] = turned[peer * own : (peer + 1) * own]
    fetches[3].wait()


def arrived(layout, staged, moved_ref, group, start, height):
    rows, own, part, groups = layout
    if staged:
        start += group * own * (rows + part)
        return moved_ref[:, start : start + height]
    blocks = moved_ref.shape[0] // groups
    return moved_ref[pl.ds(group * blocks, blocks), start : start + height]


def driver_signals(layout, staged, moved_ref, chans):
    rows, own, part, groups = layout
    parts = [
        arrived(layout, staged, moved_ref, group, chan * rows, rows) for chan in chans for group in range(groups)
    ]
    return [values.reshape(values.shape[0] * rows, LANES) for values in parts]


def filter_signals(layout, staged, moved_ref, chans):
    rows, own, part, groups = layout
    signals = []
    for chan in chans:
        pieces = [
            arrived(layout, staged, moved_ref, group, own * rows + chan * part, part)
            for group in range(groups if part < rows else 1)
        ]
        signals.append(jnp.concatenate(pieces, axis=1).reshape(pieces[0].shape[0] * rows, LANES))
    return signals


def conv_kernel(layout, staged, pieces, moved_ref, head_ref, twist_ref, tail_ref, back_tail_ref, back_head_ref, out_ref):
    rows, own, part, groups = layout
    blocks = out_ref.shape[0] // groups
    outer = blocks * rows
    scale = 1.0 / (outer * LANES)
    cos, sin = twist_ref[:, :LANES] * scale, twist_ref[:, LANES:] * scale
    sets = [range(piece * own // pieces, (piece + 1) * own // pieces) for piece in range(pieces)]
    mixed = [
        head_stage(
            filter_signals(layout, staged, moved_ref, chans) + driver_signals(layout, staged, moved_ref, chans),
            head_ref[...],
            twist_ref[...],
        )
        for chans in sets
    ]
    specs = [mat(by_lanes(values), tail_ref[...]) for values in mixed]
    prods = [product_stage(spec, outer, groups) for spec in specs]
    backs = [mat(by_lanes(values), back_tail_ref[...]) for values in prods]
    turned = [back_stage(back, cos, sin) for back in backs]
    results = [mat(back_head_ref[...], jnp.concatenate(halves(values), axis=0)) for values in turned]
    for chans, result in zip(sets, results):
        result = result[:outer] + result[outer:]
        for idx in range(len(chans) * groups):
            chan, group = divmod(idx, groups)
            start = (chans[0] + chan) * rows
            out_ref[pl.ds(group * blocks, blocks), start : start + rows] = result[
                :, idx * LANES : (idx + 1) * LANES
            ].reshape(blocks, rows, LANES)


def gate_kernel(rows, conv_ref, query_ref, key_ref, value_ref, bias_ref, out_ref, gated, sems):
    bias = bias_ref[...]
    half = rows * LANES // 2
    stores = [
        pltpu.make_async_copy(gated.at[pl.ds(idx * half, half)], out_ref.at[pl.ds(idx * half, half)], sems.at[idx])
        for idx in range(2)
    ]
    for row in range(rows):
        span = pl.ds(row * LANES, LANES)
        driver = key_ref[span, :].astype(F32) * value_ref[span, :].astype(F32)
        convolved = conv_ref[pl.ds(row, LANES, stride=rows), :].T
        gated[span, :] = (query_ref[span, :].astype(F32) * (convolved + bias * driver)).astype(BF16)
        if (row + 1) * LANES == half:
            stores[0].start()
    if rows % 2:
        stores[0].start()
    stores[1].start()
    for store in stores:
        store.wait()


VMEM = pl.BlockSpec(memory_space=pltpu.VMEM)
HBM = pl.BlockSpec(memory_space=pltpu.HBM)
SMEM = pl.BlockSpec(memory_space=pltpu.SMEM)


def call(kernel, outs, specs, flops, moved, scratch=()):
    return pl.pallas_call(
        kernel,
        out_shape=[jax.ShapeDtypeStruct(*out) for out in outs],
        in_specs=specs,
        out_specs=[VMEM] * len(outs),
        scratch_shapes=scratch,
        compiler_params=pltpu.CompilerParams(vmem_limit_bytes=VMEM_LIMIT),
        cost_estimate=pl.CostEstimate(flops=flops, bytes_accessed=moved, transcendentals=0),
    )


def convolve(groups, blocks, staged, query_proj, key_proj, value_proj, long_filter, skip_bias):
    tokens, chans = key_proj.shape
    rows = tokens // LANES
    count, axes = groups * blocks, ("groups", "seq")
    own = chans // count
    outer = blocks * rows
    seq_len = blocks * tokens
    part = rows // groups
    if rows % groups or own * part % 8:
        part = rows
    layout = (rows, own, part, groups)
    head, twist, tail, back_tail, back_head = (jnp.asarray(table) for table in make_tables(seq_len))
    size = tokens * chans * 4
    macs = 2 * 3 * own * seq_len * (2 * outer + 4 * LANES)
    where = lax.axis_index("groups").reshape(1).astype(jnp.int32)

    def exchange(array):
        return lax.all_to_all(array, axes, 0, 0, tiled=True)

    sources = (key_proj, value_proj, long_filter, skip_bias.reshape(1, chans))
    packed, bias = call(
        functools.partial(pack_kernel, layout),
        [((count, own * (rows + part), LANES), F32), ((1, chans), F32)],
        [SMEM] + [HBM] * 4, size // 4, size * 3,
        [pltpu.VMEM((tokens, chans), BF16), pltpu.VMEM((tokens, chans), BF16), pltpu.VMEM((part * LANES, chans), F32),
         pltpu.SemaphoreType.DMA((4,))],
    )(where, *(pltpu.with_memory_space_constraint(source, pltpu.HBM) for source in sources))
    if staged:
        mine = lax.axis_index("groups")
        height = own * (rows + part)
        by_group = packed.reshape(2, blocks, height, LANES)
        first = mine == 0
        kept = jnp.where(first, by_group[0], by_group[1])
        other = lax.ppermute(jnp.where(first, by_group[1], by_group[0]), "groups", [(0, 1), (1, 0)])
        pair = jnp.concatenate([jnp.where(first, kept, other), jnp.where(first, other, kept)], axis=1)
        moved = lax.all_to_all(pair, "seq", 0, 0, tiled=True)
    else:
        moved = exchange(packed)
    local = call(
        functools.partial(conv_kernel, layout, staged, min(own, 4)),
        [((count, own * rows, LANES), F32)], [VMEM] * 6, 5 * macs, 3 * size,
    )(moved, head, twist, tail, back_tail, back_head)[0]
    convolved = exchange(local).reshape(chans * rows, LANES)
    return pl.pallas_call(
        functools.partial(gate_kernel, rows),
        out_shape=pltpu.HBM((tokens, chans), BF16),
        in_specs=[VMEM] * 5,
        out_specs=HBM,
        scratch_shapes=[pltpu.VMEM((tokens, chans), BF16), pltpu.SemaphoreType.DMA((2,))],
        compiler_params=pltpu.CompilerParams(vmem_limit_bytes=VMEM_LIMIT),
        cost_estimate=pl.CostEstimate(flops=size, bytes_accessed=3 * size, transcendentals=0),
    )(convolved, query_proj, key_proj, value_proj, bias)


def shards(groups, blocks, cores, *args):
    if cores == 1 or groups != 2:
        return convolve(groups, blocks, False, *args)
    return lax.cond(
        lax.axis_index("chan") % 2 == 0,
        functools.partial(convolve, groups, blocks, False),
        functools.partial(convolve, groups, blocks, True),
        *args,
    )


def solution(mesh):
    placed = (
        P(("groups", "seq"), "chan"),
        P(("groups", "seq"), "chan"),
        P(("groups", "seq"), "chan"),
        P("seq", "chan"),
        P("chan"),
    )
    body = functools.partial(shards, *(mesh.shape[axis] for axis in ("groups", "seq", "chan")))
    return jax.shard_map(
        body, mesh=mesh, in_specs=placed, out_specs=P(("groups", "seq"), "chan"), check_vma=False
    )
```

```python
import functools

import jax
import jax.numpy as jnp
import ml_dtypes
import numpy as np
from jax import lax
from jax.experimental import pallas as pl
from jax.experimental.pallas import tpu as pltpu
from jax.sharding import PartitionSpec as P

LANES = 128
BF16 = jnp.bfloat16
F32 = jnp.float32
VMEM_LIMIT = 48 * 2**20


def split_np(table):
    high = table.astype(np.float32).astype(ml_dtypes.bfloat16)
    low = (table - high.astype(np.float64)).astype(np.float32).astype(ml_dtypes.bfloat16)
    return high, low


def make_tables(seq_len):
    outer = seq_len // LANES
    n_out, k_out = np.meshgrid(np.arange(outer), np.arange(outer), indexing="ij")
    head = np.exp(-2j * np.pi * (n_out * (4 * k_out + 1) % (4 * outer)) / (4 * outer))
    n_in = np.arange(LANES)
    twist = np.exp(-2j * np.pi * np.outer(4 * np.arange(outer) + 1, n_in) / (4 * seq_len))
    tail = np.exp(-2j * np.pi * (np.outer(n_in, n_in) % LANES) / LANES)

    def block(mat):
        return np.block([[mat.real, mat.imag], [-mat.imag, mat.real]])

    fwd_head = np.concatenate([head.real.T, head.imag.T], axis=0)
    high, low = split_np(fwd_head)
    head_tab = np.concatenate([high, high, low], axis=1)
    high, low = split_np(block(tail))
    tail_tab = np.concatenate([high, high, low], axis=0)
    high, low = split_np(block(tail.conj()))
    back_tail_tab = np.concatenate([high, high, low], axis=0)
    high, low = split_np(np.concatenate([head.real, head.imag], axis=1))
    back_head_tab = np.block([[high, high], [low, np.zeros_like(low)]])
    twist_tab = np.concatenate([twist.real, twist.imag], axis=1).astype(np.float32)
    return head_tab, twist_tab, tail_tab, back_tail_tab, back_head_tab


def halves(values):
    high = values.astype(BF16)
    return high, (values - high.astype(F32)).astype(BF16)


def by_rows(values):
    high, low = halves(values)
    return jnp.concatenate([high, low, high], axis=0)


def by_lanes(values):
    high, low = halves(values)
    return jnp.concatenate([high, low, high], axis=1)


def mat(left, right):
    return jnp.dot(left, right, preferred_element_type=F32)


def head_stage(signals, head, twist):
    outer = signals[0].shape[0]
    mixed = mat(head, by_rows(jnp.concatenate(signals, axis=1)))
    cos, sin = twist[:, :LANES], twist[:, LANES:]
    rows = []
    for idx in range(len(signals)):
        real = mixed[:outer, idx * LANES : (idx + 1) * LANES]
        imag = mixed[outer:, idx * LANES : (idx + 1) * LANES]
        rows.append(jnp.concatenate([real * cos - imag * sin, real * sin + imag * cos], axis=1))
    return jnp.concatenate(rows, axis=0)


def product_stage(spec, outer, groups):
    pieces = [spec[idx * outer : (idx + 1) * outer] for idx in range(spec.shape[0] // outer)]
    own = len(pieces) // (groups + 1)
    prods = []
    for idx, mine in enumerate(pieces[own:]):
        other = pieces[idx // groups]
        f_re, f_im = other[:, :LANES], other[:, LANES:]
        d_re, d_im = mine[:, :LANES], mine[:, LANES:]
        prods.append(jnp.concatenate([d_re * f_re - d_im * f_im, d_re * f_im + d_im * f_re], axis=1))
    return jnp.concatenate(prods, axis=0)


def back_stage(back, cos, sin):
    outer = cos.shape[0]
    reals, imags = [], []
    for idx in range(back.shape[0] // outer):
        mine = back[idx * outer : (idx + 1) * outer]
        real, imag = mine[:, :LANES], mine[:, LANES:]
        reals.append(real * cos + imag * sin)
        imags.append(imag * cos - real * sin)
    return jnp.concatenate([jnp.concatenate(reals, axis=1), jnp.concatenate(imags, axis=1)], axis=0)


def pack_kernel(layout, where_ref, key_ref, value_ref, filter_ref, bias_ref, out_ref, bias_out, key, value, taps, sems):
    rows, own, part, groups = layout
    first = where_ref[0] * (part * LANES if part < rows else 0)
    taken = filter_ref.at[pl.ds(pl.multiple_of(first, part * LANES), part * LANES)]
    cuts = 2 if rows % 2 == 0 else 1
    spans = [pl.ds(cut * rows // cuts * LANES, rows // cuts * LANES) for cut in range(cuts)]
    pairs = [(source.at[span], held.at[span]) for span in spans for source, held in ((key_ref, key), (value_ref, value))]
    pairs += [(taken, taps), (bias_ref, bias_out)]
    fetches = [pltpu.make_async_copy(*pair, sems.at[idx]) for idx, pair in enumerate(pairs)]
    for fetch in fetches:
        fetch.start()
    for row in range(rows):
        if row % (rows // cuts) == 0:
            for fetch in fetches[row // (rows // cuts) * 2 :][:2]:
                fetch.wait()
        span = pl.ds(row * LANES, LANES)
        turned = (key[span, :].astype(F32) * value[span, :].astype(F32)).T
        for peer in range(out_ref.shape[0]):
            out_ref[peer, pl.ds(row, own, stride=rows), :] = turned[peer * own : (peer + 1) * own]
    fetches[-2].wait()
    for row in range(part):
        turned = taps[pl.ds(row * LANES, LANES), :].T
        for peer in range(out_ref.shape[0]):
            out_ref[peer, pl.ds(own * rows + row, own, stride=part), :] = turned[peer * own : (peer + 1) * own]
    fetches[-1].wait()


def arrived(layout, staged, moved_ref, group, start, height):
    rows, own, part, groups = layout
    if staged:
        start += group * own * (rows + part)
        return moved_ref[:, start : start + height]
    blocks = moved_ref.shape[0] // groups
    return moved_ref[pl.ds(group * blocks, blocks), start : start + height]


def driver_signals(layout, staged, moved_ref, chans):
    rows, own, part, groups = layout
    parts = [
        arrived(layout, staged, moved_ref, group, chan * rows, rows) for chan in chans for group in range(groups)
    ]
    return [values.reshape(values.shape[0] * rows, LANES) for values in parts]


def filter_signals(layout, staged, moved_ref, chans):
    rows, own, part, groups = layout
    signals = []
    for chan in chans:
        pieces = [
            arrived(layout, staged, moved_ref, group, own * rows + chan * part, part)
            for group in range(groups if part < rows else 1)
        ]
        signals.append(jnp.concatenate(pieces, axis=1).reshape(pieces[0].shape[0] * rows, LANES))
    return signals


def conv_kernel(layout, staged, pieces, moved_ref, head_ref, twist_ref, tail_ref, back_tail_ref, back_head_ref, out_ref):
    rows, own, part, groups = layout
    blocks = out_ref.shape[0] // groups
    outer = blocks * rows
    scale = 1.0 / (outer * LANES)
    cos, sin = twist_ref[:, :LANES] * scale, twist_ref[:, LANES:] * scale
    sets = [range(piece * own // pieces, (piece + 1) * own // pieces) for piece in range(pieces)]
    mixed = [
        head_stage(
            filter_signals(layout, staged, moved_ref, chans) + driver_signals(layout, staged, moved_ref, chans),
            head_ref[...],
            twist_ref[...],
        )
        for chans in sets
    ]
    specs = [mat(by_lanes(values), tail_ref[...]) for values in mixed]
    prods = [product_stage(spec, outer, groups) for spec in specs]
    backs = [mat(by_lanes(values), back_tail_ref[...]) for values in prods]
    turned = [back_stage(back, cos, sin) for back in backs]
    results = [mat(back_head_ref[...], jnp.concatenate(halves(values), axis=0)) for values in turned]
    for chans, result in zip(sets, results):
        result = result[:outer] + result[outer:]
        for idx in range(len(chans) * groups):
            chan, group = divmod(idx, groups)
            start = (chans[0] + chan) * rows
            out_ref[pl.ds(group * blocks, blocks), start : start + rows] = result[
                :, idx * LANES : (idx + 1) * LANES
            ].reshape(blocks, rows, LANES)


def gate_kernel(rows, conv_ref, query_ref, key_ref, value_ref, bias_ref, out_ref, gated, sems):
    bias = bias_ref[...]
    half = rows * LANES // 2
    stores = [
        pltpu.make_async_copy(gated.at[pl.ds(idx * half, half)], out_ref.at[pl.ds(idx * half, half)], sems.at[idx])
        for idx in range(2)
    ]
    for row in range(rows):
        span = pl.ds(row * LANES, LANES)
        driver = key_ref[span, :].astype(F32) * value_ref[span, :].astype(F32)
        convolved = conv_ref[pl.ds(row, LANES, stride=rows), :].T
        gated[span, :] = (query_ref[span, :].astype(F32) * (convolved + bias * driver)).astype(BF16)
        if (row + 1) * LANES == half:
            stores[0].start()
    if rows % 2:
        stores[0].start()
    stores[1].start()
    for store in stores:
        store.wait()


VMEM = pl.BlockSpec(memory_space=pltpu.VMEM)
HBM = pl.BlockSpec(memory_space=pltpu.HBM)
SMEM = pl.BlockSpec(memory_space=pltpu.SMEM)


def call(kernel, outs, specs, flops, moved, scratch=()):
    return pl.pallas_call(
        kernel,
        out_shape=[jax.ShapeDtypeStruct(*out) for out in outs],
        in_specs=specs,
        out_specs=[VMEM] * len(outs),
        scratch_shapes=scratch,
        compiler_params=pltpu.CompilerParams(vmem_limit_bytes=VMEM_LIMIT),
        cost_estimate=pl.CostEstimate(flops=flops, bytes_accessed=moved, transcendentals=0),
    )


def convolve(groups, blocks, staged, query_proj, key_proj, value_proj, long_filter, skip_bias):
    tokens, chans = key_proj.shape
    rows = tokens // LANES
    count, axes = groups * blocks, ("groups", "seq")
    own = chans // count
    outer = blocks * rows
    seq_len = blocks * tokens
    part = rows // groups
    if rows % groups or own * part % 8:
        part = rows
    layout = (rows, own, part, groups)
    head, twist, tail, back_tail, back_head = (jnp.asarray(table) for table in make_tables(seq_len))
    size = tokens * chans * 4
    macs = 2 * 3 * own * seq_len * (2 * outer + 4 * LANES)
    where = lax.axis_index("groups").reshape(1).astype(jnp.int32)

    def exchange(array):
        return lax.all_to_all(array, axes, 0, 0, tiled=True)

    sources = (key_proj, value_proj, long_filter, skip_bias.reshape(1, chans))
    packed, bias = call(
        functools.partial(pack_kernel, layout),
        [((count, own * (rows + part), LANES), F32), ((1, chans), F32)],
        [SMEM] + [HBM] * 4, size // 4, size * 3,
        [pltpu.VMEM((tokens, chans), BF16), pltpu.VMEM((tokens, chans), BF16), pltpu.VMEM((part * LANES, chans), F32),
         pltpu.SemaphoreType.DMA((6,))],
    )(where, *(pltpu.with_memory_space_constraint(source, pltpu.HBM) for source in sources))
    if staged:
        mine = lax.axis_index("groups")
        height = own * (rows + part)
        by_group = packed.reshape(2, blocks, height, LANES)
        first = mine == 0
        kept = jnp.where(first, by_group[0], by_group[1])
        other = lax.ppermute(jnp.where(first, by_group[1], by_group[0]), "groups", [(0, 1), (1, 0)])
        pair = jnp.concatenate([jnp.where(first, kept, other), jnp.where(first, other, kept)], axis=1)
        moved = lax.all_to_all(pair, "seq", 0, 0, tiled=True)
    else:
        moved = exchange(packed)
    local = call(
        functools.partial(conv_kernel, layout, staged, min(own, 4)),
        [((count, own * rows, LANES), F32)], [VMEM] * 6, 5 * macs, 3 * size,
    )(moved, head, twist, tail, back_tail, back_head)[0]
    convolved = exchange(local).reshape(chans * rows, LANES)
    return pl.pallas_call(
        functools.partial(gate_kernel, rows),
        out_shape=pltpu.HBM((tokens, chans), BF16),
        in_specs=[VMEM] * 5,
        out_specs=HBM,
        scratch_shapes=[pltpu.VMEM((tokens, chans), BF16), pltpu.SemaphoreType.DMA((2,))],
        compiler_params=pltpu.CompilerParams(vmem_limit_bytes=VMEM_LIMIT),
        cost_estimate=pl.CostEstimate(flops=size, bytes_accessed=3 * size, transcendentals=0),
    )(convolved, query_proj, key_proj, value_proj, bias)


def shards(groups, blocks, cores, *args):
    if cores == 1 or groups != 2:
        return convolve(groups, blocks, False, *args)
    return lax.cond(
        lax.axis_index("chan") % 2 == 1,
        functools.partial(convolve, groups, blocks, False),
        functools.partial(convolve, groups, blocks, True),
        *args,
    )


def solution(mesh):
    placed = (
        P(("groups", "seq"), "chan"),
        P(("groups", "seq"), "chan"),
        P(("groups", "seq"), "chan"),
        P("seq", "chan"),
        P("chan"),
    )
    body = functools.partial(shards, *(mesh.shape[axis] for axis in ("groups", "seq", "chan")))
    return jax.shard_map(
        body, mesh=mesh, in_specs=placed, out_specs=P(("groups", "seq"), "chan"), check_vma=False
    )
```

```python
import functools

import jax
import jax.numpy as jnp
import ml_dtypes
import numpy as np
from jax import lax
from jax.experimental import pallas as pl
from jax.experimental.pallas import tpu as pltpu
from jax.sharding import PartitionSpec as P

LANES = 128
BF16 = jnp.bfloat16
F32 = jnp.float32
VMEM_LIMIT = 48 * 2**20


def split_np(table):
    high = table.astype(np.float32).astype(ml_dtypes.bfloat16)
    low = (table - high.astype(np.float64)).astype(np.float32).astype(ml_dtypes.bfloat16)
    return high, low


def make_tables(seq_len):
    outer = seq_len // LANES
    n_out, k_out = np.meshgrid(np.arange(outer), np.arange(outer), indexing="ij")
    head = np.exp(-2j * np.pi * (n_out * (4 * k_out + 1) % (4 * outer)) / (4 * outer))
    n_in = np.arange(LANES)
    twist = np.exp(-2j * np.pi * np.outer(4 * np.arange(outer) + 1, n_in) / (4 * seq_len))
    tail = np.exp(-2j * np.pi * (np.outer(n_in, n_in) % LANES) / LANES)

    def block(mat):
        return np.block([[mat.real, mat.imag], [-mat.imag, mat.real]])

    fwd_head = np.concatenate([head.real.T, head.imag.T], axis=0)
    high, low = split_np(fwd_head)
    head_tab = np.concatenate([high, high, low], axis=1)
    high, low = split_np(block(tail))
    tail_tab = np.concatenate([high, high, low], axis=0)
    high, low = split_np(block(tail.conj()))
    back_tail_tab = np.concatenate([high, high, low], axis=0)
    high, low = split_np(np.concatenate([head.real, head.imag], axis=1))
    back_head_tab = np.block([[high, high], [low, np.zeros_like(low)]])
    twist_tab = np.concatenate([twist.real, twist.imag], axis=1).astype(np.float32)
    return head_tab, twist_tab, tail_tab, back_tail_tab, back_head_tab


def halves(values):
    high = values.astype(BF16)
    return high, (values - high.astype(F32)).astype(BF16)


def by_rows(values):
    high, low = halves(values)
    return jnp.concatenate([high, low, high], axis=0)


def by_lanes(values):
    high, low = halves(values)
    return jnp.concatenate([high, low, high], axis=1)


def mat(left, right):
    return jnp.dot(left, right, preferred_element_type=F32)


def head_stage(signals, head, twist):
    outer = signals[0].shape[0]
    mixed = mat(head, by_rows(jnp.concatenate(signals, axis=1)))
    cos, sin = twist[:, :LANES], twist[:, LANES:]
    rows = []
    for idx in range(len(signals)):
        real = mixed[:outer, idx * LANES : (idx + 1) * LANES]
        imag = mixed[outer:, idx * LANES : (idx + 1) * LANES]
        rows.append(jnp.concatenate([real * cos - imag * sin, real * sin + imag * cos], axis=1))
    return jnp.concatenate(rows, axis=0)


def product_stage(spec, outer, groups):
    pieces = [spec[idx * outer : (idx + 1) * outer] for idx in range(spec.shape[0] // outer)]
    own = len(pieces) // (groups + 1)
    prods = []
    for idx, mine in enumerate(pieces[own:]):
        other = pieces[idx // groups]
        f_re, f_im = other[:, :LANES], other[:, LANES:]
        d_re, d_im = mine[:, :LANES], mine[:, LANES:]
        prods.append(jnp.concatenate([d_re * f_re - d_im * f_im, d_re * f_im + d_im * f_re], axis=1))
    return jnp.concatenate(prods, axis=0)


def back_stage(back, cos, sin):
    outer = cos.shape[0]
    reals, imags = [], []
    for idx in range(back.shape[0] // outer):
        mine = back[idx * outer : (idx + 1) * outer]
        real, imag = mine[:, :LANES], mine[:, LANES:]
        reals.append(real * cos + imag * sin)
        imags.append(imag * cos - real * sin)
    return jnp.concatenate([jnp.concatenate(reals, axis=1), jnp.concatenate(imags, axis=1)], axis=0)


def pack_kernel(layout, staged, where_ref, key_ref, value_ref, filter_ref, bias_ref, out_ref, bias_out, key, value, taps, sems):
    rows, own, part, groups = layout
    count = out_ref.shape[0]
    blocks = count // groups
    homes = [(peer, peer * own) for peer in range(count)]
    if staged:
        near = where_ref[0] * 2 + where_ref[1]
        homes = [
            (((peer // blocks * 2 + peer % 2) ^ near) * (blocks // 2) + peer % blocks // 2, peer * own)
            for peer in range(count)
        ]
    first = where_ref[0] * (part * LANES if part < rows else 0)
    taken = filter_ref.at[pl.ds(pl.multiple_of(first, part * LANES), part * LANES)]
    cuts = 2 if rows % 2 == 0 else 1
    spans = [pl.ds(cut * rows // cuts * LANES, rows // cuts * LANES) for cut in range(cuts)]
    pairs = [(source.at[span], held.at[span]) for span in spans for source, held in ((key_ref, key), (value_ref, value))]
    pairs += [(taken, taps), (bias_ref, bias_out)]
    fetches = [pltpu.make_async_copy(*pair, sems.at[idx]) for idx, pair in enumerate(pairs)]
    for fetch in fetches:
        fetch.start()
    for row in range(rows):
        if row % (rows // cuts) == 0:
            for fetch in fetches[row // (rows // cuts) * 2 :][:2]:
                fetch.wait()
        span = pl.ds(row * LANES, LANES)
        turned = (key[span, :].astype(F32) * value[span, :].astype(F32)).T
        for place, chan in homes:
            out_ref[place, pl.ds(row, own, stride=rows), :] = turned[chan : chan + own]
    fetches[-2].wait()
    for row in range(part):
        turned = taps[pl.ds(row * LANES, LANES), :].T
        for place, chan in homes:
            out_ref[place, pl.ds(own * rows + row, own, stride=part), :] = turned[chan : chan + own]
    fetches[-1].wait()


def arrived(layout, staged, moved_ref, group, start, height):
    rows, own, part, groups = layout
    if staged:
        pair = [moved_ref[group * 2 + near, :, start : start + height] for near in range(2)]
        values = jnp.stack(pair, axis=1)
        return values.reshape(values.shape[0] * 2, height, LANES)
    blocks = moved_ref.shape[0] // groups
    return moved_ref[pl.ds(group * blocks, blocks), start : start + height]


def driver_signals(layout, staged, moved_ref, chans):
    rows, own, part, groups = layout
    parts = [
        arrived(layout, staged, moved_ref, group, chan * rows, rows) for chan in chans for group in range(groups)
    ]
    return [values.reshape(values.shape[0] * rows, LANES) for values in parts]


def filter_signals(layout, staged, moved_ref, chans):
    rows, own, part, groups = layout
    signals = []
    for chan in chans:
        pieces = [
            arrived(layout, staged, moved_ref, group, own * rows + chan * part, part)
            for group in range(groups if part < rows else 1)
        ]
        signals.append(jnp.concatenate(pieces, axis=1).reshape(pieces[0].shape[0] * rows, LANES))
    return signals


def conv_kernel(
    layout, staged, pieces, where_ref, moved_ref, head_ref, twist_ref, tail_ref, back_tail_ref, back_head_ref, out_ref, *held
):
    rows, own, part, groups = layout
    if staged:
        near = where_ref[0] * 2 + where_ref[1]
        height = own * (rows + part)
        for place in range(2 * groups):
            held[0][near ^ place] = moved_ref[:, place * height : (place + 1) * height]
        moved_ref = held[0]
    blocks = out_ref.shape[0] // groups
    outer = blocks * rows
    scale = 1.0 / (outer * LANES)
    cos, sin = twist_ref[:, :LANES] * scale, twist_ref[:, LANES:] * scale
    sets = [range(piece * own // pieces, (piece + 1) * own // pieces) for piece in range(pieces)]
    mixed = [
        head_stage(
            filter_signals(layout, staged, moved_ref, chans) + driver_signals(layout, staged, moved_ref, chans),
            head_ref[...],
            twist_ref[...],
        )
        for chans in sets
    ]
    specs = [mat(by_lanes(values), tail_ref[...]) for values in mixed]
    prods = [product_stage(spec, outer, groups) for spec in specs]
    backs = [mat(by_lanes(values), back_tail_ref[...]) for values in prods]
    turned = [back_stage(back, cos, sin) for back in backs]
    results = [mat(back_head_ref[...], jnp.concatenate(halves(values), axis=0)) for values in turned]
    for chans, result in zip(sets, results):
        result = result[:outer] + result[outer:]
        for idx in range(len(chans) * groups):
            chan, group = divmod(idx, groups)
            start = (chans[0] + chan) * rows
            out_ref[pl.ds(group * blocks, blocks), start : start + rows] = result[
                :, idx * LANES : (idx + 1) * LANES
            ].reshape(blocks, rows, LANES)


def gate_kernel(rows, conv_ref, query_ref, key_ref, value_ref, bias_ref, out_ref, gated, sems):
    bias = bias_ref[...]
    half = rows * LANES // 2
    stores = [
        pltpu.make_async_copy(gated.at[pl.ds(idx * half, half)], out_ref.at[pl.ds(idx * half, half)], sems.at[idx])
        for idx in range(2)
    ]
    for row in range(rows):
        span = pl.ds(row * LANES, LANES)
        driver = key_ref[span, :].astype(F32) * value_ref[span, :].astype(F32)
        convolved = conv_ref[pl.ds(row, LANES, stride=rows), :].T
        gated[span, :] = (query_ref[span, :].astype(F32) * (convolved + bias * driver)).astype(BF16)
        if (row + 1) * LANES == half:
            stores[0].start()
    if rows % 2:
        stores[0].start()
    stores[1].start()
    for store in stores:
        store.wait()


VMEM = pl.BlockSpec(memory_space=pltpu.VMEM)
HBM = pl.BlockSpec(memory_space=pltpu.HBM)
SMEM = pl.BlockSpec(memory_space=pltpu.SMEM)


def call(kernel, outs, specs, flops, moved, scratch=()):
    return pl.pallas_call(
        kernel,
        out_shape=[jax.ShapeDtypeStruct(*out) for out in outs],
        in_specs=specs,
        out_specs=[VMEM] * len(outs),
        scratch_shapes=scratch,
        compiler_params=pltpu.CompilerParams(vmem_limit_bytes=VMEM_LIMIT),
        cost_estimate=pl.CostEstimate(flops=flops, bytes_accessed=moved, transcendentals=0),
    )


def convolve(groups, blocks, staged, query_proj, key_proj, value_proj, long_filter, skip_bias):
    tokens, chans = key_proj.shape
    rows = tokens // LANES
    count, axes = groups * blocks, ("groups", "seq")
    own = chans // count
    outer = blocks * rows
    seq_len = blocks * tokens
    part = rows // groups
    if rows % groups or own * part % 8:
        part = rows
    layout = (rows, own, part, groups)
    head, twist, tail, back_tail, back_head = (jnp.asarray(table) for table in make_tables(seq_len))
    size = tokens * chans * 4
    macs = 2 * 3 * own * seq_len * (2 * outer + 4 * LANES)
    where = jnp.stack([lax.axis_index("groups"), lax.axis_index("seq") % 2]).astype(jnp.int32)

    def exchange(array):
        return lax.all_to_all(array, axes, 0, 0, tiled=True)

    sources = (key_proj, value_proj, long_filter, skip_bias.reshape(1, chans))
    packed, bias = call(
        functools.partial(pack_kernel, layout, staged),
        [((count, own * (rows + part), LANES), F32), ((1, chans), F32)],
        [SMEM] + [HBM] * 4, size // 4, size * 3,
        [pltpu.VMEM((tokens, chans), BF16), pltpu.VMEM((tokens, chans), BF16), pltpu.VMEM((part * LANES, chans), F32),
         pltpu.SemaphoreType.DMA((6,))],
    )(where, *(pltpu.with_memory_space_constraint(source, pltpu.HBM) for source in sources))
    if staged:
        far, height = blocks // 2, own * (rows + part)
        by_near = packed.reshape(4, far, height, LANES)
        places = [(group, block) for group in range(groups) for block in range(blocks)]
        held = [by_near[0]]
        for near in range(1, 4):
            pairs = [
                (group * blocks + block, (group ^ near // 2) * blocks + (block ^ near % 2)) for group, block in places
            ]
            held.append(lax.ppermute(by_near[near], axes, pairs))
        columns = [[2 * block + near for block in range(far)] for near in range(2)]
        moved = lax.all_to_all(
            jnp.concatenate(held, axis=1), "seq", 0, 0, axis_index_groups=columns, tiled=True
        )
    else:
        moved = exchange(packed)
    local = call(
        functools.partial(conv_kernel, layout, staged, min(own, 4)),
        [((count, own * rows, LANES), F32)], [SMEM] + [VMEM] * 6, 5 * macs, 3 * size,
        [pltpu.VMEM((2 * groups, blocks // 2, own * (rows + part), LANES), F32)] * staged,
    )(where, moved, head, twist, tail, back_tail, back_head)[0]
    convolved = exchange(local).reshape(chans * rows, LANES)
    return pl.pallas_call(
        functools.partial(gate_kernel, rows),
        out_shape=pltpu.HBM((tokens, chans), BF16),
        in_specs=[VMEM] * 5,
        out_specs=HBM,
        scratch_shapes=[pltpu.VMEM((tokens, chans), BF16), pltpu.SemaphoreType.DMA((2,))],
        compiler_params=pltpu.CompilerParams(vmem_limit_bytes=VMEM_LIMIT),
        cost_estimate=pl.CostEstimate(flops=size, bytes_accessed=3 * size, transcendentals=0),
    )(convolved, query_proj, key_proj, value_proj, bias)


def shards(groups, blocks, cores, *args):
    if cores == 1 or groups != 2 or blocks % 2:
        return convolve(groups, blocks, False, *args)
    return lax.cond(
        lax.axis_index("chan") % 2 == 1,
        functools.partial(convolve, groups, blocks, False),
        functools.partial(convolve, groups, blocks, True),
        *args,
    )


def solution(mesh):
    placed = (
        P(("groups", "seq"), "chan"),
        P(("groups", "seq"), "chan"),
        P(("groups", "seq"), "chan"),
        P("seq", "chan"),
        P("chan"),
    )
    body = functools.partial(shards, *(mesh.shape[axis] for axis in ("groups", "seq", "chan")))
    return jax.shard_map(
        body, mesh=mesh, in_specs=placed, out_specs=P(("groups", "seq"), "chan"), check_vma=False
    )
```

```python
import functools

import jax
import jax.numpy as jnp
import ml_dtypes
import numpy as np
from jax import lax
from jax.experimental import pallas as pl
from jax.experimental.pallas import tpu as pltpu
from jax.sharding import PartitionSpec as P

LANES = 128
BF16 = jnp.bfloat16
F32 = jnp.float32
VMEM_LIMIT = 48 * 2**20


def split_np(table):
    high = table.astype(np.float32).astype(ml_dtypes.bfloat16)
    low = (table - high.astype(np.float64)).astype(np.float32).astype(ml_dtypes.bfloat16)
    return high, low


def make_tables(seq_len):
    outer = seq_len // LANES
    n_out, k_out = np.meshgrid(np.arange(outer), np.arange(outer), indexing="ij")
    head = np.exp(-2j * np.pi * (n_out * (4 * k_out + 1) % (4 * outer)) / (4 * outer))
    n_in = np.arange(LANES)
    twist = np.exp(-2j * np.pi * np.outer(4 * np.arange(outer) + 1, n_in) / (4 * seq_len))
    tail = np.exp(-2j * np.pi * (np.outer(n_in, n_in) % LANES) / LANES)

    def block(mat):
        return np.block([[mat.real, mat.imag], [-mat.imag, mat.real]])

    fwd_head = np.concatenate([head.real.T, head.imag.T], axis=0)
    high, low = split_np(fwd_head)
    head_tab = np.concatenate([high, high, low], axis=1)
    high, low = split_np(block(tail))
    tail_tab = np.concatenate([high, high, low], axis=0)
    high, low = split_np(block(tail.conj()))
    back_tail_tab = np.concatenate([high, high, low], axis=0)
    high, low = split_np(np.concatenate([head.real, head.imag], axis=1))
    back_head_tab = np.block([[high, high], [low, np.zeros_like(low)]])
    twist_tab = np.concatenate([twist.real, twist.imag], axis=1).astype(np.float32)
    return head_tab, twist_tab, tail_tab, back_tail_tab, back_head_tab


def halves(values):
    high = values.astype(BF16)
    return high, (values - high.astype(F32)).astype(BF16)


def by_rows(values):
    high, low = halves(values)
    return jnp.concatenate([high, low, high], axis=0)


def by_lanes(values):
    high, low = halves(values)
    return jnp.concatenate([high, low, high], axis=1)


def mat(left, right):
    return jnp.dot(left, right, preferred_element_type=F32)


def head_stage(signals, head, twist):
    outer = signals[0].shape[0]
    mixed = mat(head, by_rows(jnp.concatenate(signals, axis=1)))
    cos, sin = twist[:, :LANES], twist[:, LANES:]
    rows = []
    for idx in range(len(signals)):
        real = mixed[:outer, idx * LANES : (idx + 1) * LANES]
        imag = mixed[outer:, idx * LANES : (idx + 1) * LANES]
        rows.append(jnp.concatenate([real * cos - imag * sin, real * sin + imag * cos], axis=1))
    return jnp.concatenate(rows, axis=0)


def product_stage(spec, outer, groups):
    pieces = [spec[idx * outer : (idx + 1) * outer] for idx in range(spec.shape[0] // outer)]
    own = len(pieces) // (groups + 1)
    prods = []
    for idx, mine in enumerate(pieces[own:]):
        other = pieces[idx // groups]
        f_re, f_im = other[:, :LANES], other[:, LANES:]
        d_re, d_im = mine[:, :LANES], mine[:, LANES:]
        prods.append(jnp.concatenate([d_re * f_re - d_im * f_im, d_re * f_im + d_im * f_re], axis=1))
    return jnp.concatenate(prods, axis=0)


def back_stage(back, cos, sin):
    outer = cos.shape[0]
    reals, imags = [], []
    for idx in range(back.shape[0] // outer):
        mine = back[idx * outer : (idx + 1) * outer]
        real, imag = mine[:, :LANES], mine[:, LANES:]
        reals.append(real * cos + imag * sin)
        imags.append(imag * cos - real * sin)
    return jnp.concatenate([jnp.concatenate(reals, axis=1), jnp.concatenate(imags, axis=1)], axis=0)


def pack_kernel(layout, where_ref, key_ref, value_ref, filter_ref, bias_ref, out_ref, bias_out, key, value, taps, sems):
    rows, own, part, groups = layout
    first = where_ref[0] * (part * LANES if part < rows else 0)
    taken = filter_ref.at[pl.ds(pl.multiple_of(first, part * LANES), part * LANES)]
    cuts = 2 if rows % 2 == 0 else 1
    spans = [pl.ds(cut * rows // cuts * LANES, rows // cuts * LANES) for cut in range(cuts)]
    pairs = [(source.at[span], held.at[span]) for span in spans for source, held in ((key_ref, key), (value_ref, value))]
    pairs += [(taken, taps), (bias_ref, bias_out)]
    fetches = [pltpu.make_async_copy(*pair, sems.at[idx]) for idx, pair in enumerate(pairs)]
    for fetch in fetches:
        fetch.start()
    for row in range(rows):
        if row % (rows // cuts) == 0:
            for fetch in fetches[row // (rows // cuts) * 2 :][:2]:
                fetch.wait()
        span = pl.ds(row * LANES, LANES)
        turned = (key[span, :].astype(F32) * value[span, :].astype(F32)).T
        for peer in range(out_ref.shape[0]):
            out_ref[peer, pl.ds(row, own, stride=rows), :] = turned[peer * own : (peer + 1) * own]
    fetches[-2].wait()
    for row in range(part):
        turned = taps[pl.ds(row * LANES, LANES), :].T
        for peer in range(out_ref.shape[0]):
            out_ref[peer, pl.ds(own * rows + row, own, stride=part), :] = turned[peer * own : (peer + 1) * own]
    fetches[-1].wait()


def arrived(layout, staged, moved_ref, group, start, height):
    rows, own, part, groups = layout
    if staged:
        start += group * own * (rows + part)
        return moved_ref[:, start : start + height]
    blocks = moved_ref.shape[0] // groups
    return moved_ref[pl.ds(group * blocks, blocks), start : start + height]


def driver_signals(layout, staged, moved_ref, chans):
    rows, own, part, groups = layout
    parts = [
        arrived(layout, staged, moved_ref, group, chan * rows, rows) for chan in chans for group in range(groups)
    ]
    return [values.reshape(values.shape[0] * rows, LANES) for values in parts]


def filter_signals(layout, staged, moved_ref, chans):
    rows, own, part, groups = layout
    signals = []
    for chan in chans:
        pieces = [
            arrived(layout, staged, moved_ref, group, own * rows + chan * part, part)
            for group in range(groups if part < rows else 1)
        ]
        signals.append(jnp.concatenate(pieces, axis=1).reshape(pieces[0].shape[0] * rows, LANES))
    return signals


def conv_kernel(layout, staged, pieces, moved_ref, head_ref, twist_ref, tail_ref, back_tail_ref, back_head_ref, out_ref):
    rows, own, part, groups = layout
    blocks = out_ref.shape[0] // groups
    outer = blocks * rows
    scale = 1.0 / (outer * LANES)
    cos, sin = twist_ref[:, :LANES] * scale, twist_ref[:, LANES:] * scale
    sets = [range(piece * own // pieces, (piece + 1) * own // pieces) for piece in range(pieces)]
    mixed = [
        head_stage(
            filter_signals(layout, staged, moved_ref, chans) + driver_signals(layout, staged, moved_ref, chans),
            head_ref[...],
            twist_ref[...],
        )
        for chans in sets
    ]
    specs = [mat(by_lanes(values), tail_ref[...]) for values in mixed]
    prods = [product_stage(spec, outer, groups) for spec in specs]
    backs = [mat(by_lanes(values), back_tail_ref[...]) for values in prods]
    turned = [back_stage(back, cos, sin) for back in backs]
    results = [mat(back_head_ref[...], jnp.concatenate(halves(values), axis=0)) for values in turned]
    for chans, result in zip(sets, results):
        result = result[:outer] + result[outer:]
        for idx in range(len(chans) * groups):
            chan, group = divmod(idx, groups)
            start = (chans[0] + chan) * rows
            out_ref[pl.ds(group * blocks, blocks), start : start + rows] = result[
                :, idx * LANES : (idx + 1) * LANES
            ].reshape(blocks, rows, LANES)


def gate_kernel(rows, conv_ref, query_ref, key_ref, value_ref, bias_ref, out_ref, gated, sems):
    bias = bias_ref[...]
    half = rows * LANES // 2
    stores = [
        pltpu.make_async_copy(gated.at[pl.ds(idx * half, half)], out_ref.at[pl.ds(idx * half, half)], sems.at[idx])
        for idx in range(2)
    ]
    for row in range(rows):
        span = pl.ds(row * LANES, LANES)
        driver = key_ref[span, :].astype(F32) * value_ref[span, :].astype(F32)
        convolved = conv_ref[pl.ds(row, LANES, stride=rows), :].T
        gated[span, :] = (query_ref[span, :].astype(F32) * (convolved + bias * driver)).astype(BF16)
        if (row + 1) * LANES == half:
            stores[0].start()
    if rows % 2:
        stores[0].start()
    stores[1].start()
    for store in stores:
        store.wait()


VMEM = pl.BlockSpec(memory_space=pltpu.VMEM)
HBM = pl.BlockSpec(memory_space=pltpu.HBM)
SMEM = pl.BlockSpec(memory_space=pltpu.SMEM)


def call(kernel, outs, specs, flops, moved, scratch=()):
    return pl.pallas_call(
        kernel,
        out_shape=[jax.ShapeDtypeStruct(*out) for out in outs],
        in_specs=specs,
        out_specs=[VMEM] * len(outs),
        scratch_shapes=scratch,
        compiler_params=pltpu.CompilerParams(vmem_limit_bytes=VMEM_LIMIT),
        cost_estimate=pl.CostEstimate(flops=flops, bytes_accessed=moved, transcendentals=0),
    )


def convolve(groups, blocks, staged, query_proj, key_proj, value_proj, long_filter, skip_bias):
    tokens, chans = key_proj.shape
    rows = tokens // LANES
    count, axes = groups * blocks, ("groups", "seq")
    own = chans // count
    outer = blocks * rows
    seq_len = blocks * tokens
    part = rows // groups
    if rows % groups or own * part % 8:
        part = rows
    layout = (rows, own, part, groups)
    head, twist, tail, back_tail, back_head = (jnp.asarray(table) for table in make_tables(seq_len))
    size = tokens * chans * 4
    macs = 2 * 3 * own * seq_len * (2 * outer + 4 * LANES)
    where = lax.axis_index("groups").reshape(1).astype(jnp.int32)

    def exchange(array):
        return lax.all_to_all(array, axes, 0, 0, tiled=True)

    sources = (key_proj, value_proj, long_filter, skip_bias.reshape(1, chans))
    packed, bias = call(
        functools.partial(pack_kernel, layout),
        [((count, own * (rows + part), LANES), F32), ((1, chans), F32)],
        [SMEM] + [HBM] * 4, size // 4, size * 3,
        [pltpu.VMEM((tokens, chans), BF16), pltpu.VMEM((tokens, chans), BF16), pltpu.VMEM((part * LANES, chans), F32),
         pltpu.SemaphoreType.DMA((6,))],
    )(where, *(pltpu.with_memory_space_constraint(source, pltpu.HBM) for source in sources))
    if staged:
        by_group = packed.reshape(groups, blocks, own * (rows + part), LANES)
        by_group = lax.all_to_all(by_group, "groups", 0, 0, tiled=True)
        pair = jnp.concatenate([by_group[group] for group in range(groups)], axis=1)
        moved = lax.all_to_all(pair, "seq", 0, 0, tiled=True)
    else:
        moved = exchange(packed)
    local = call(
        functools.partial(conv_kernel, layout, staged, min(own, 4)),
        [((count, own * rows, LANES), F32)], [VMEM] * 6, 5 * macs, 3 * size,
    )(moved, head, twist, tail, back_tail, back_head)[0]
    convolved = exchange(local).reshape(chans * rows, LANES)
    return pl.pallas_call(
        functools.partial(gate_kernel, rows),
        out_shape=pltpu.HBM((tokens, chans), BF16),
        in_specs=[VMEM] * 5,
        out_specs=HBM,
        scratch_shapes=[pltpu.VMEM((tokens, chans), BF16), pltpu.SemaphoreType.DMA((2,))],
        compiler_params=pltpu.CompilerParams(vmem_limit_bytes=VMEM_LIMIT),
        cost_estimate=pl.CostEstimate(flops=size, bytes_accessed=3 * size, transcendentals=0),
    )(convolved, query_proj, key_proj, value_proj, bias)


def shards(groups, blocks, cores, *args):
    if cores == 1 or groups == 1:
        return convolve(groups, blocks, False, *args)
    return lax.cond(
        lax.axis_index("chan") % 2 == 0,
        functools.partial(convolve, groups, blocks, False),
        functools.partial(convolve, groups, blocks, True),
        *args,
    )


def solution(mesh):
    placed = (
        P(("groups", "seq"), "chan"),
        P(("groups", "seq"), "chan"),
        P(("groups", "seq"), "chan"),
        P("seq", "chan"),
        P("chan"),
    )
    body = functools.partial(shards, *(mesh.shape[axis] for axis in ("groups", "seq", "chan")))
    return jax.shard_map(
        body, mesh=mesh, in_specs=placed, out_specs=P(("groups", "seq"), "chan"), check_vma=False
    )
```

```python
import functools

import jax
import jax.numpy as jnp
import ml_dtypes
import numpy as np
from jax import lax
from jax.experimental import pallas as pl
from jax.experimental.pallas import tpu as pltpu
from jax.sharding import PartitionSpec as P

LANES = 128
BF16 = jnp.bfloat16
F32 = jnp.float32
VMEM_LIMIT = 48 * 2**20


def split_np(table):
    high = table.astype(np.float32).astype(ml_dtypes.bfloat16)
    low = (table - high.astype(np.float64)).astype(np.float32).astype(ml_dtypes.bfloat16)
    return high, low


def make_tables(seq_len):
    outer = seq_len // LANES
    n_out, k_out = np.meshgrid(np.arange(outer), np.arange(outer), indexing="ij")
    head = np.exp(-2j * np.pi * (n_out * (4 * k_out + 1) % (4 * outer)) / (4 * outer))
    n_in = np.arange(LANES)
    twist = np.exp(-2j * np.pi * np.outer(4 * np.arange(outer) + 1, n_in) / (4 * seq_len))
    tail = np.exp(-2j * np.pi * (np.outer(n_in, n_in) % LANES) / LANES)

    def block(mat):
        return np.block([[mat.real, mat.imag], [-mat.imag, mat.real]])

    fwd_head = np.concatenate([head.real.T, head.imag.T], axis=0)
    high, low = split_np(fwd_head)
    head_tab = np.concatenate([high, high, low], axis=1)
    high, low = split_np(block(tail))
    tail_tab = np.concatenate([high, low], axis=0)
    high, low = split_np(block(tail.conj()))
    back_tail_tab = np.concatenate([high, low], axis=0)
    high, low = split_np(np.concatenate([head.real, head.imag], axis=1))
    back_head_tab = np.block([[high, high], [low, np.zeros_like(low)]])
    twist_tab = np.concatenate([twist.real, twist.imag], axis=1).astype(np.float32)
    return head_tab, twist_tab, tail_tab, back_tail_tab, back_head_tab


def halves(values):
    high = values.astype(BF16)
    return high, (values - high.astype(F32)).astype(BF16)


def by_rows(values):
    high, low = halves(values)
    return jnp.concatenate([high, low, high], axis=0)


def mat(left, right):
    return jnp.dot(left, right, preferred_element_type=F32)


def mat_split(values, table):
    high, low = halves(values)
    depth = values.shape[1]
    return mat(high, table[:depth]) + (mat(low, table[:depth]) + mat(high, table[depth:]))


def head_stage(signals, head, twist):
    outer = signals[0].shape[0]
    mixed = mat(head, by_rows(jnp.concatenate(signals, axis=1)))
    cos, sin = twist[:, :LANES], twist[:, LANES:]
    rows = []
    for idx in range(len(signals)):
        real = mixed[:outer, idx * LANES : (idx + 1) * LANES]
        imag = mixed[outer:, idx * LANES : (idx + 1) * LANES]
        rows.append(jnp.concatenate([real * cos - imag * sin, real * sin + imag * cos], axis=1))
    return jnp.concatenate(rows, axis=0)


def product_stage(spec, outer, groups):
    pieces = [spec[idx * outer : (idx + 1) * outer] for idx in range(spec.shape[0] // outer)]
    own = len(pieces) // (groups + 1)
    prods = []
    for idx, mine in enumerate(pieces[own:]):
        other = pieces[idx // groups]
        f_re, f_im = other[:, :LANES], other[:, LANES:]
        d_re, d_im = mine[:, :LANES], mine[:, LANES:]
        prods.append(jnp.concatenate([d_re * f_re - d_im * f_im, d_re * f_im + d_im * f_re], axis=1))
    return jnp.concatenate(prods, axis=0)


def back_stage(back, cos, sin):
    outer = cos.shape[0]
    reals, imags = [], []
    for idx in range(back.shape[0] // outer):
        mine = back[idx * outer : (idx + 1) * outer]
        real, imag = mine[:, :LANES], mine[:, LANES:]
        reals.append(real * cos + imag * sin)
        imags.append(imag * cos - real * sin)
    return jnp.concatenate([jnp.concatenate(reals, axis=1), jnp.concatenate(imags, axis=1)], axis=0)


def pack_kernel(layout, where_ref, key_ref, value_ref, filter_ref, bias_ref, out_ref, bias_out, key, value, taps, sems):
    rows, own, part, groups = layout
    first = where_ref[0] * (part * LANES if part < rows else 0)
    taken = filter_ref.at[pl.ds(pl.multiple_of(first, part * LANES), part * LANES)]
    cuts = 2 if rows % 2 == 0 else 1
    spans = [pl.ds(cut * rows // cuts * LANES, rows // cuts * LANES) for cut in range(cuts)]
    pairs = [(source.at[span], held.at[span]) for span in spans for source, held in ((key_ref, key), (value_ref, value))]
    pairs += [(taken, taps), (bias_ref, bias_out)]
    fetches = [pltpu.make_async_copy(*pair, sems.at[idx]) for idx, pair in enumerate(pairs)]
    for fetch in fetches:
        fetch.start()
    for row in range(rows):
        if row % (rows // cuts) == 0:
            for fetch in fetches[row // (rows // cuts) * 2 :][:2]:
                fetch.wait()
        span = pl.ds(row * LANES, LANES)
        turned = (key[span, :].astype(F32) * value[span, :].astype(F32)).T
        for peer in range(out_ref.shape[0]):
            out_ref[peer, pl.ds(row, own, stride=rows), :] = turned[peer * own : (peer + 1) * own]
    fetches[-2].wait()
    for row in range(part):
        turned = taps[pl.ds(row * LANES, LANES), :].T
        for peer in range(out_ref.shape[0]):
            out_ref[peer, pl.ds(own * rows + row, own, stride=part), :] = turned[peer * own : (peer + 1) * own]
    fetches[-1].wait()


def arrived(layout, staged, moved_ref, group, start, height):
    rows, own, part, groups = layout
    if staged:
        start += group * own * (rows + part)
        return moved_ref[:, start : start + height]
    blocks = moved_ref.shape[0] // groups
    return moved_ref[pl.ds(group * blocks, blocks), start : start + height]


def driver_signals(layout, staged, moved_ref, chans):
    rows, own, part, groups = layout
    parts = [
        arrived(layout, staged, moved_ref, group, chan * rows, rows) for chan in chans for group in range(groups)
    ]
    return [values.reshape(values.shape[0] * rows, LANES) for values in parts]


def filter_signals(layout, staged, moved_ref, chans):
    rows, own, part, groups = layout
    signals = []
    for chan in chans:
        pieces = [
            arrived(layout, staged, moved_ref, group, own * rows + chan * part, part)
            for group in range(groups if part < rows else 1)
        ]
        signals.append(jnp.concatenate(pieces, axis=1).reshape(pieces[0].shape[0] * rows, LANES))
    return signals


def conv_kernel(layout, staged, pieces, moved_ref, head_ref, twist_ref, tail_ref, back_tail_ref, back_head_ref, out_ref):
    rows, own, part, groups = layout
    blocks = out_ref.shape[0] // groups
    outer = blocks * rows
    scale = 1.0 / (outer * LANES)
    cos, sin = twist_ref[:, :LANES] * scale, twist_ref[:, LANES:] * scale
    sets = [range(piece * own // pieces, (piece + 1) * own // pieces) for piece in range(pieces)]
    mixed = [
        head_stage(
            filter_signals(layout, staged, moved_ref, chans) + driver_signals(layout, staged, moved_ref, chans),
            head_ref[...],
            twist_ref[...],
        )
        for chans in sets
    ]
    specs = [mat_split(values, tail_ref[...]) for values in mixed]
    prods = [product_stage(spec, outer, groups) for spec in specs]
    backs = [mat_split(values, back_tail_ref[...]) for values in prods]
    turned = [back_stage(back, cos, sin) for back in backs]
    results = [mat(back_head_ref[...], jnp.concatenate(halves(values), axis=0)) for values in turned]
    for chans, result in zip(sets, results):
        result = result[:outer] + result[outer:]
        for idx in range(len(chans) * groups):
            chan, group = divmod(idx, groups)
            start = (chans[0] + chan) * rows
            out_ref[pl.ds(group * blocks, blocks), start : start + rows] = result[
                :, idx * LANES : (idx + 1) * LANES
            ].reshape(blocks, rows, LANES)


def gate_kernel(rows, conv_ref, query_ref, key_ref, value_ref, bias_ref, out_ref, gated, sems):
    bias = bias_ref[...]
    half = rows * LANES // 2
    stores = [
        pltpu.make_async_copy(gated.at[pl.ds(idx * half, half)], out_ref.at[pl.ds(idx * half, half)], sems.at[idx])
        for idx in range(2)
    ]
    for row in range(rows):
        span = pl.ds(row * LANES, LANES)
        driver = key_ref[span, :].astype(F32) * value_ref[span, :].astype(F32)
        convolved = conv_ref[pl.ds(row, LANES, stride=rows), :].T
        gated[span, :] = (query_ref[span, :].astype(F32) * (convolved + bias * driver)).astype(BF16)
        if (row + 1) * LANES == half:
            stores[0].start()
    if rows % 2:
        stores[0].start()
    stores[1].start()
    for store in stores:
        store.wait()


VMEM = pl.BlockSpec(memory_space=pltpu.VMEM)
HBM = pl.BlockSpec(memory_space=pltpu.HBM)
SMEM = pl.BlockSpec(memory_space=pltpu.SMEM)


def call(kernel, outs, specs, flops, moved, scratch=()):
    return pl.pallas_call(
        kernel,
        out_shape=[jax.ShapeDtypeStruct(*out) for out in outs],
        in_specs=specs,
        out_specs=[VMEM] * len(outs),
        scratch_shapes=scratch,
        compiler_params=pltpu.CompilerParams(vmem_limit_bytes=VMEM_LIMIT),
        cost_estimate=pl.CostEstimate(flops=flops, bytes_accessed=moved, transcendentals=0),
    )


def convolve(groups, blocks, staged, query_proj, key_proj, value_proj, long_filter, skip_bias):
    tokens, chans = key_proj.shape
    rows = tokens // LANES
    count, axes = groups * blocks, ("groups", "seq")
    own = chans // count
    outer = blocks * rows
    seq_len = blocks * tokens
    part = rows // groups
    if rows % groups or own * part % 8:
        part = rows
    layout = (rows, own, part, groups)
    head, twist, tail, back_tail, back_head = (jnp.asarray(table) for table in make_tables(seq_len))
    size = tokens * chans * 4
    macs = 2 * 3 * own * seq_len * (2 * outer + 4 * LANES)
    where = lax.axis_index("groups").reshape(1).astype(jnp.int32)

    def exchange(array):
        return lax.all_to_all(array, axes, 0, 0, tiled=True)

    sources = (key_proj, value_proj, long_filter, skip_bias.reshape(1, chans))
    packed, bias = call(
        functools.partial(pack_kernel, layout),
        [((count, own * (rows + part), LANES), F32), ((1, chans), F32)],
        [SMEM] + [HBM] * 4, size // 4, size * 3,
        [pltpu.VMEM((tokens, chans), BF16), pltpu.VMEM((tokens, chans), BF16), pltpu.VMEM((part * LANES, chans), F32),
         pltpu.SemaphoreType.DMA((6,))],
    )(where, *(pltpu.with_memory_space_constraint(source, pltpu.HBM) for source in sources))
    if staged:
        mine = lax.axis_index("groups")
        height = own * (rows + part)
        by_group = packed.reshape(2, blocks, height, LANES)
        first = mine == 0
        kept = jnp.where(first, by_group[0], by_group[1])
        sent = jnp.where(first, by_group[1], by_group[0])
        cut = blocks // 2
        other = jnp.concatenate([lax.ppermute(piece, "groups", [(0, 1), (1, 0)]) for piece in (sent[:cut], sent[cut:])])
        pair = jnp.concatenate([jnp.where(first, kept, other), jnp.where(first, other, kept)], axis=1)
        moved = lax.all_to_all(pair, "seq", 0, 0, tiled=True)
    else:
        moved = exchange(packed)
    local = call(
        functools.partial(conv_kernel, layout, staged, min(own, 4)),
        [((count, own * rows, LANES), F32)], [VMEM] * 6, 5 * macs, 3 * size,
    )(moved, head, twist, tail, back_tail, back_head)[0]
    convolved = exchange(local).reshape(chans * rows, LANES)
    return pl.pallas_call(
        functools.partial(gate_kernel, rows),
        out_shape=pltpu.HBM((tokens, chans), BF16),
        in_specs=[VMEM] * 5,
        out_specs=HBM,
        scratch_shapes=[pltpu.VMEM((tokens, chans), BF16), pltpu.SemaphoreType.DMA((2,))],
        compiler_params=pltpu.CompilerParams(vmem_limit_bytes=VMEM_LIMIT),
        cost_estimate=pl.CostEstimate(flops=size, bytes_accessed=3 * size, transcendentals=0),
    )(convolved, query_proj, key_proj, value_proj, bias)


def shards(groups, blocks, cores, *args):
    if cores == 1 or groups != 2:
        return convolve(groups, blocks, False, *args)
    return lax.cond(
        lax.axis_index("chan") % 2 == 1,
        functools.partial(convolve, groups, blocks, False),
        functools.partial(convolve, groups, blocks, True),
        *args,
    )


def solution(mesh):
    placed = (
        P(("groups", "seq"), "chan"),
        P(("groups", "seq"), "chan"),
        P(("groups", "seq"), "chan"),
        P("seq", "chan"),
        P("chan"),
    )
    body = functools.partial(shards, *(mesh.shape[axis] for axis in ("groups", "seq", "chan")))
    return jax.shard_map(
        body, mesh=mesh, in_specs=placed, out_specs=P(("groups", "seq"), "chan"), check_vma=False
    )
```

```python
import functools

import jax
import jax.numpy as jnp
import ml_dtypes
import numpy as np
from jax import lax
from jax.experimental import pallas as pl
from jax.experimental.pallas import tpu as pltpu
from jax.sharding import PartitionSpec as P

LANES = 128
BF16 = jnp.bfloat16
F32 = jnp.float32
VMEM_LIMIT = 48 * 2**20


def split_np(table):
    high = table.astype(np.float32).astype(ml_dtypes.bfloat16)
    low = (table - high.astype(np.float64)).astype(np.float32).astype(ml_dtypes.bfloat16)
    return high, low


def make_tables(seq_len):
    outer = seq_len // LANES
    n_out, k_out = np.meshgrid(np.arange(outer), np.arange(outer), indexing="ij")
    head = np.exp(-2j * np.pi * (n_out * (4 * k_out + 1) % (4 * outer)) / (4 * outer))
    n_in = np.arange(LANES)
    twist = np.exp(-2j * np.pi * np.outer(4 * np.arange(outer) + 1, n_in) / (4 * seq_len))
    tail = np.exp(-2j * np.pi * (np.outer(n_in, n_in) % LANES) / LANES)

    def block(mat):
        return np.block([[mat.real, mat.imag], [-mat.imag, mat.real]])

    fwd_head = np.concatenate([head.real.T, head.imag.T], axis=0)
    high, low = split_np(fwd_head)
    head_tab = np.concatenate([high, high, low], axis=1)
    high, low = split_np(block(tail))
    tail_tab = np.concatenate([high, high, low], axis=0)
    high, low = split_np(block(tail.conj()))
    back_tail_tab = np.concatenate([high, high, low], axis=0)
    high, low = split_np(np.concatenate([head.real, head.imag], axis=1))
    back_head_tab = np.block([[high, high], [low, np.zeros_like(low)]])
    twist_tab = np.concatenate([twist.real, twist.imag], axis=1).astype(np.float32)
    return head_tab, twist_tab, tail_tab, back_tail_tab, back_head_tab


def halves(values):
    high = values.astype(BF16)
    return high, (values - high.astype(F32)).astype(BF16)


def by_rows(values):
    high, low = halves(values)
    return jnp.concatenate([high, low, high], axis=0)


def by_lanes(values):
    high, low = halves(values)
    return jnp.concatenate([high, low, high], axis=1)


def mat(left, right):
    return jnp.dot(left, right, preferred_element_type=F32)


def head_stage(signals, head, twist):
    outer = signals[0].shape[0]
    mixed = mat(head, by_rows(jnp.concatenate(signals, axis=1)))
    cos, sin = twist[:, :LANES], twist[:, LANES:]
    rows = []
    for idx in range(len(signals)):
        real = mixed[:outer, idx * LANES : (idx + 1) * LANES]
        imag = mixed[outer:, idx * LANES : (idx + 1) * LANES]
        rows.append(jnp.concatenate([real * cos - imag * sin, real * sin + imag * cos], axis=1))
    return jnp.concatenate(rows, axis=0)


def product_stage(spec, outer, groups):
    pieces = [spec[idx * outer : (idx + 1) * outer] for idx in range(spec.shape[0] // outer)]
    own = len(pieces) // (groups + 1)
    prods = []
    for idx, mine in enumerate(pieces[own:]):
        other = pieces[idx // groups]
        f_re, f_im = other[:, :LANES], other[:, LANES:]
        d_re, d_im = mine[:, :LANES], mine[:, LANES:]
        prods.append(jnp.concatenate([d_re * f_re - d_im * f_im, d_re * f_im + d_im * f_re], axis=1))
    return jnp.concatenate(prods, axis=0)


def back_stage(back, cos, sin):
    outer = cos.shape[0]
    reals, imags = [], []
    for idx in range(back.shape[0] // outer):
        mine = back[idx * outer : (idx + 1) * outer]
        real, imag = mine[:, :LANES], mine[:, LANES:]
        reals.append(real * cos + imag * sin)
        imags.append(imag * cos - real * sin)
    return jnp.concatenate([jnp.concatenate(reals, axis=1), jnp.concatenate(imags, axis=1)], axis=0)


def turn_exact(values):
    size = values.shape[1]
    rows = lax.broadcasted_iota(jnp.int32, (size, 2 * size), 0)
    unit = (lax.broadcasted_iota(jnp.int32, (size, 2 * size), 1) % size == rows).astype(BF16)
    parts = jnp.concatenate(halves(values), axis=1)
    return lax.dot_general(unit, parts, (((1,), (1,)), ((), ())), preferred_element_type=F32)


def pack_kernel(layout, where_ref, key_ref, value_ref, filter_ref, bias_ref, out_ref, bias_out, key, value, taps, sems):
    rows, own, part, groups = layout
    first = where_ref[0] * (part * LANES if part < rows else 0)
    taken = filter_ref.at[pl.ds(pl.multiple_of(first, part * LANES), part * LANES)]
    cuts = 2 if rows % 2 == 0 else 1
    spans = [pl.ds(cut * rows // cuts * LANES, rows // cuts * LANES) for cut in range(cuts)]
    pairs = [(source.at[span], held.at[span]) for span in spans for source, held in ((key_ref, key), (value_ref, value))]
    pairs += [(taken, taps), (bias_ref, bias_out)]
    fetches = [pltpu.make_async_copy(*pair, sems.at[idx]) for idx, pair in enumerate(pairs)]
    for fetch in fetches:
        fetch.start()
    for row in range(rows):
        if row % (rows // cuts) == 0:
            for fetch in fetches[row // (rows // cuts) * 2 :][:2]:
                fetch.wait()
        span = pl.ds(row * LANES, LANES)
        turned = turn_exact(key[span, :].astype(F32) * value[span, :].astype(F32))
        for peer in range(out_ref.shape[0]):
            out_ref[peer, pl.ds(row, own, stride=rows), :] = turned[peer * own : (peer + 1) * own]
    fetches[-2].wait()
    for row in range(part):
        turned = taps[pl.ds(row * LANES, LANES), :].T
        for peer in range(out_ref.shape[0]):
            out_ref[peer, pl.ds(own * rows + row, own, stride=part), :] = turned[peer * own : (peer + 1) * own]
    fetches[-1].wait()


def arrived(layout, staged, moved_ref, group, start, height):
    rows, own, part, groups = layout
    if staged:
        start += group * own * (rows + part)
        return moved_ref[:, start : start + height]
    blocks = moved_ref.shape[0] // groups
    return moved_ref[pl.ds(group * blocks, blocks), start : start + height]


def driver_signals(layout, staged, moved_ref, chans):
    rows, own, part, groups = layout
    parts = [
        arrived(layout, staged, moved_ref, group, chan * rows, rows) for chan in chans for group in range(groups)
    ]
    return [values.reshape(values.shape[0] * rows, LANES) for values in parts]


def filter_signals(layout, staged, moved_ref, chans):
    rows, own, part, groups = layout
    signals = []
    for chan in chans:
        pieces = [
            arrived(layout, staged, moved_ref, group, own * rows + chan * part, part)
            for group in range(groups if part < rows else 1)
        ]
        signals.append(jnp.concatenate(pieces, axis=1).reshape(pieces[0].shape[0] * rows, LANES))
    return signals


def conv_kernel(layout, staged, pieces, moved_ref, head_ref, twist_ref, tail_ref, back_tail_ref, back_head_ref, out_ref):
    rows, own, part, groups = layout
    blocks = out_ref.shape[0] // groups
    outer = blocks * rows
    scale = 1.0 / (outer * LANES)
    cos, sin = twist_ref[:, :LANES] * scale, twist_ref[:, LANES:] * scale
    sets = [range(piece * own // pieces, (piece + 1) * own // pieces) for piece in range(pieces)]
    mixed = [
        head_stage(
            filter_signals(layout, staged, moved_ref, chans) + driver_signals(layout, staged, moved_ref, chans),
            head_ref[...],
            twist_ref[...],
        )
        for chans in sets
    ]
    specs = [mat(by_lanes(values), tail_ref[...]) for values in mixed]
    prods = [product_stage(spec, outer, groups) for spec in specs]
    backs = [mat(by_lanes(values), back_tail_ref[...]) for values in prods]
    turned = [back_stage(back, cos, sin) for back in backs]
    results = [mat(back_head_ref[...], jnp.concatenate(halves(values), axis=0)) for values in turned]
    for chans, result in zip(sets, results):
        result = result[:outer] + result[outer:]
        for idx in range(len(chans) * groups):
            chan, group = divmod(idx, groups)
            start = (chans[0] + chan) * rows
            out_ref[pl.ds(group * blocks, blocks), start : start + rows] = result[
                :, idx * LANES : (idx + 1) * LANES
            ].reshape(blocks, rows, LANES)


def gate_kernel(rows, conv_ref, query_ref, key_ref, value_ref, bias_ref, out_ref, gated, sems):
    bias = bias_ref[...]
    half = rows * LANES // 2
    stores = [
        pltpu.make_async_copy(gated.at[pl.ds(idx * half, half)], out_ref.at[pl.ds(idx * half, half)], sems.at[idx])
        for idx in range(2)
    ]
    for row in range(rows):
        span = pl.ds(row * LANES, LANES)
        driver = key_ref[span, :].astype(F32) * value_ref[span, :].astype(F32)
        convolved = conv_ref[pl.ds(row, LANES, stride=rows), :].T
        gated[span, :] = (query_ref[span, :].astype(F32) * (convolved + bias * driver)).astype(BF16)
        if (row + 1) * LANES == half:
            stores[0].start()
    if rows % 2:
        stores[0].start()
    stores[1].start()
    for store in stores:
        store.wait()


VMEM = pl.BlockSpec(memory_space=pltpu.VMEM)
HBM = pl.BlockSpec(memory_space=pltpu.HBM)
SMEM = pl.BlockSpec(memory_space=pltpu.SMEM)


def call(kernel, outs, specs, flops, moved, scratch=()):
    return pl.pallas_call(
        kernel,
        out_shape=[jax.ShapeDtypeStruct(*out) for out in outs],
        in_specs=specs,
        out_specs=[VMEM] * len(outs),
        scratch_shapes=scratch,
        compiler_params=pltpu.CompilerParams(vmem_limit_bytes=VMEM_LIMIT),
        cost_estimate=pl.CostEstimate(flops=flops, bytes_accessed=moved, transcendentals=0),
    )


def convolve(groups, blocks, staged, query_proj, key_proj, value_proj, long_filter, skip_bias):
    tokens, chans = key_proj.shape
    rows = tokens // LANES
    count, axes = groups * blocks, ("groups", "seq")
    own = chans // count
    outer = blocks * rows
    seq_len = blocks * tokens
    part = rows // groups
    if rows % groups or own * part % 8:
        part = rows
    layout = (rows, own, part, groups)
    head, twist, tail, back_tail, back_head = (jnp.asarray(table) for table in make_tables(seq_len))
    size = tokens * chans * 4
    macs = 2 * 3 * own * seq_len * (2 * outer + 4 * LANES)
    where = lax.axis_index("groups").reshape(1).astype(jnp.int32)

    def exchange(array):
        return lax.all_to_all(array, axes, 0, 0, tiled=True)

    sources = (key_proj, value_proj, long_filter, skip_bias.reshape(1, chans))
    packed, bias = call(
        functools.partial(pack_kernel, layout),
        [((count, own * (rows + part), LANES), F32), ((1, chans), F32)],
        [SMEM] + [HBM] * 4, size // 4, size * 3,
        [pltpu.VMEM((tokens, chans), BF16), pltpu.VMEM((tokens, chans), BF16), pltpu.VMEM((part * LANES, chans), F32),
         pltpu.SemaphoreType.DMA((6,))],
    )(where, *(pltpu.with_memory_space_constraint(source, pltpu.HBM) for source in sources))
    if staged:
        mine = lax.axis_index("groups")
        height = own * (rows + part)
        by_group = packed.reshape(2, blocks, height, LANES)
        first = mine == 0
        kept = jnp.where(first, by_group[0], by_group[1])
        other = lax.ppermute(jnp.where(first, by_group[1], by_group[0]), "groups", [(0, 1), (1, 0)])
        pair = jnp.concatenate([jnp.where(first, kept, other), jnp.where(first, other, kept)], axis=1)
        moved = lax.all_to_all(pair, "seq", 0, 0, tiled=True)
    else:
        moved = exchange(packed)
    local = call(
        functools.partial(conv_kernel, layout, staged, min(own, 4)),
        [((count, own * rows, LANES), F32)], [VMEM] * 6, 5 * macs, 3 * size,
    )(moved, head, twist, tail, back_tail, back_head)[0]
    convolved = exchange(local).reshape(chans * rows, LANES)
    return pl.pallas_call(
        functools.partial(gate_kernel, rows),
        out_shape=pltpu.HBM((tokens, chans), BF16),
        in_specs=[VMEM] * 5,
        out_specs=HBM,
        scratch_shapes=[pltpu.VMEM((tokens, chans), BF16), pltpu.SemaphoreType.DMA((2,))],
        compiler_params=pltpu.CompilerParams(vmem_limit_bytes=VMEM_LIMIT),
        cost_estimate=pl.CostEstimate(flops=size, bytes_accessed=3 * size, transcendentals=0),
    )(convolved, query_proj, key_proj, value_proj, bias)


def shards(groups, blocks, cores, *args):
    if cores == 1 or groups != 2:
        return convolve(groups, blocks, False, *args)
    return lax.cond(
        lax.axis_index("chan") % 2 == 1,
        functools.partial(convolve, groups, blocks, False),
        functools.partial(convolve, groups, blocks, True),
        *args,
    )


def solution(mesh):
    placed = (
        P(("groups", "seq"), "chan"),
        P(("groups", "seq"), "chan"),
        P(("groups", "seq"), "chan"),
        P("seq", "chan"),
        P("chan"),
    )
    body = functools.partial(shards, *(mesh.shape[axis] for axis in ("groups", "seq", "chan")))
    return jax.shard_map(
        body, mesh=mesh, in_specs=placed, out_specs=P(("groups", "seq"), "chan"), check_vma=False
    )
```

```python
import functools

import jax
import jax.numpy as jnp
import ml_dtypes
import numpy as np
from jax import lax
from jax.experimental import pallas as pl
from jax.experimental.pallas import tpu as pltpu
from jax.sharding import PartitionSpec as P

LANES = 128
BF16 = jnp.bfloat16
F32 = jnp.float32
VMEM_LIMIT = 48 * 2**20


def split_np(table):
    high = table.astype(np.float32).astype(ml_dtypes.bfloat16)
    low = (table - high.astype(np.float64)).astype(np.float32).astype(ml_dtypes.bfloat16)
    return high, low


def make_tables(seq_len):
    outer = seq_len // LANES
    n_out, k_out = np.meshgrid(np.arange(outer), np.arange(outer), indexing="ij")
    head = np.exp(-2j * np.pi * (n_out * (4 * k_out + 1) % (4 * outer)) / (4 * outer))
    n_in = np.arange(LANES)
    twist = np.exp(-2j * np.pi * np.outer(4 * np.arange(outer) + 1, n_in) / (4 * seq_len))
    tail = np.exp(-2j * np.pi * (np.outer(n_in, n_in) % LANES) / LANES)

    def block(mat):
        return np.block([[mat.real, mat.imag], [-mat.imag, mat.real]])

    fwd_head = np.concatenate([head.real.T, head.imag.T], axis=0)
    high, low = split_np(fwd_head)
    head_tab = np.concatenate([high, high, low], axis=1)
    high, low = split_np(block(tail))
    tail_tab = np.concatenate([high, high, low], axis=0)
    high, low = split_np(block(tail.conj()))
    back_tail_tab = np.concatenate([high, high, low], axis=0)
    high, low = split_np(np.concatenate([head.real, head.imag], axis=1))
    back_head_tab = np.block([[high, high], [low, np.zeros_like(low)]])
    twist_tab = np.concatenate([twist.real, twist.imag], axis=1).astype(np.float32)
    return head_tab, twist_tab, tail_tab, back_tail_tab, back_head_tab


def halves(values):
    high = values.astype(BF16)
    return high, (values - high.astype(F32)).astype(BF16)


def by_rows(values):
    high, low = halves(values)
    return jnp.concatenate([high, low, high], axis=0)


def by_lanes(values):
    high, low = halves(values)
    return jnp.concatenate([high, low, high], axis=1)


def mat(left, right):
    return jnp.dot(left, right, preferred_element_type=F32)


def head_stage(signals, head, twist):
    outer = signals[0].shape[0]
    mixed = mat(head, by_rows(jnp.concatenate(signals, axis=1)))
    cos, sin = twist[:, :LANES], twist[:, LANES:]
    rows = []
    for idx in range(len(signals)):
        real = mixed[:outer, idx * LANES : (idx + 1) * LANES]
        imag = mixed[outer:, idx * LANES : (idx + 1) * LANES]
        rows.append(jnp.concatenate([real * cos - imag * sin, real * sin + imag * cos], axis=1))
    return jnp.concatenate(rows, axis=0)


def product_stage(spec, outer, groups):
    pieces = [spec[idx * outer : (idx + 1) * outer] for idx in range(spec.shape[0] // outer)]
    own = len(pieces) // (groups + 1)
    prods = []
    for idx, mine in enumerate(pieces[own:]):
        other = pieces[idx // groups]
        f_re, f_im = other[:, :LANES], other[:, LANES:]
        d_re, d_im = mine[:, :LANES], mine[:, LANES:]
        prods.append(jnp.concatenate([d_re * f_re - d_im * f_im, d_re * f_im + d_im * f_re], axis=1))
    return jnp.concatenate(prods, axis=0)


def back_stage(back, cos, sin):
    outer = cos.shape[0]
    reals, imags = [], []
    for idx in range(back.shape[0] // outer):
        mine = back[idx * outer : (idx + 1) * outer]
        real, imag = mine[:, :LANES], mine[:, LANES:]
        reals.append(real * cos + imag * sin)
        imags.append(imag * cos - real * sin)
    return jnp.concatenate([jnp.concatenate(reals, axis=1), jnp.concatenate(imags, axis=1)], axis=0)


def pack_kernel(layout, where_ref, key_ref, value_ref, filter_ref, bias_ref, out_ref, bias_out, key, value, taps, sems):
    rows, own, part, groups = layout
    first = where_ref[0] * (part * LANES if part < rows else 0)
    taken = filter_ref.at[pl.ds(pl.multiple_of(first, part * LANES), part * LANES)]
    cuts = 2 if rows % 2 == 0 else 1
    spans = [pl.ds(cut * rows // cuts * LANES, rows // cuts * LANES) for cut in range(cuts)]
    pairs = [(source.at[span], held.at[span]) for span in spans for source, held in ((key_ref, key), (value_ref, value))]
    pairs += [(taken, taps), (bias_ref, bias_out)]
    fetches = [pltpu.make_async_copy(*pair, sems.at[idx]) for idx, pair in enumerate(pairs)]
    for fetch in fetches:
        fetch.start()
    for row in range(rows):
        if row % (rows // cuts) == 0:
            for fetch in fetches[row // (rows // cuts) * 2 :][:2]:
                fetch.wait()
        span = pl.ds(row * LANES, LANES)
        turned = (key[span, :].astype(F32) * value[span, :].astype(F32)).T
        for peer in range(out_ref.shape[0]):
            out_ref[peer, pl.ds(row, own, stride=rows), :] = turned[peer * own : (peer + 1) * own]
    fetches[-2].wait()
    for row in range(part):
        turned = taps[pl.ds(row * LANES, LANES), :].T
        for peer in range(out_ref.shape[0]):
            out_ref[peer, pl.ds(own * rows + row, own, stride=part), :] = turned[peer * own : (peer + 1) * own]
    fetches[-1].wait()


def arrived(layout, staged, moved_ref, group, start, height):
    rows, own, part, groups = layout
    if staged:
        start += group * own * (rows + part)
        return moved_ref[:, start : start + height]
    blocks = moved_ref.shape[0] // groups
    return moved_ref[pl.ds(group * blocks, blocks), start : start + height]


def driver_signals(layout, staged, moved_ref, chans):
    rows, own, part, groups = layout
    parts = [
        arrived(layout, staged, moved_ref, group, chan * rows, rows) for chan in chans for group in range(groups)
    ]
    return [values.reshape(values.shape[0] * rows, LANES) for values in parts]


def filter_signals(layout, staged, moved_ref, chans):
    rows, own, part, groups = layout
    signals = []
    for chan in chans:
        pieces = [
            arrived(layout, staged, moved_ref, group, own * rows + chan * part, part)
            for group in range(groups if part < rows else 1)
        ]
        signals.append(jnp.concatenate(pieces, axis=1).reshape(pieces[0].shape[0] * rows, LANES))
    return signals


def conv_kernel(layout, staged, pieces, moved_ref, head_ref, twist_ref, tail_ref, back_tail_ref, back_head_ref, out_ref):
    rows, own, part, groups = layout
    blocks = out_ref.shape[0] // groups
    outer = blocks * rows
    scale = 1.0 / (outer * LANES)
    cos, sin = twist_ref[:, :LANES] * scale, twist_ref[:, LANES:] * scale
    sets = [range(piece * own // pieces, (piece + 1) * own // pieces) for piece in range(pieces)]
    mixed = [
        head_stage(
            filter_signals(layout, staged, moved_ref, chans) + driver_signals(layout, staged, moved_ref, chans),
            head_ref[...],
            twist_ref[...],
        )
        for chans in sets
    ]
    specs = [mat(by_lanes(values), tail_ref[...]) for values in mixed]
    prods = [product_stage(spec, outer, groups) for spec in specs]
    backs = [mat(by_lanes(values), back_tail_ref[...]) for values in prods]
    turned = [back_stage(back, cos, sin) for back in backs]
    results = [mat(back_head_ref[...], jnp.concatenate(halves(values), axis=0)) for values in turned]
    for chans, result in zip(sets, results):
        result = result[:outer] + result[outer:]
        for idx in range(len(chans) * groups):
            chan, group = divmod(idx, groups)
            start = (chans[0] + chan) * rows
            out_ref[pl.ds(group * blocks, blocks), start : start + rows] = result[
                :, idx * LANES : (idx + 1) * LANES
            ].reshape(blocks, rows, LANES)


def gate_kernel(rows, conv_ref, query_ref, key_ref, value_ref, bias_ref, out_ref, gated, sems):
    bias = bias_ref[...]
    half = rows * LANES // 2
    stores = [
        pltpu.make_async_copy(gated.at[pl.ds(idx * half, half)], out_ref.at[pl.ds(idx * half, half)], sems.at[idx])
        for idx in range(2)
    ]
    for row in range(rows):
        span = pl.ds(row * LANES, LANES)
        driver = key_ref[span, :].astype(F32) * value_ref[span, :].astype(F32)
        convolved = conv_ref[pl.ds(row, LANES, stride=rows), :].T
        gated[span, :] = (query_ref[span, :].astype(F32) * (convolved + bias * driver)).astype(BF16)
        if (row + 1) * LANES == half:
            stores[0].start()
    if rows % 2:
        stores[0].start()
    stores[1].start()
    for store in stores:
        store.wait()


VMEM = pl.BlockSpec(memory_space=pltpu.VMEM)
HBM = pl.BlockSpec(memory_space=pltpu.HBM)
SMEM = pl.BlockSpec(memory_space=pltpu.SMEM)


def call(kernel, outs, specs, flops, moved, scratch=()):
    return pl.pallas_call(
        kernel,
        out_shape=[jax.ShapeDtypeStruct(*out) for out in outs],
        in_specs=specs,
        out_specs=[VMEM] * len(outs),
        scratch_shapes=scratch,
        compiler_params=pltpu.CompilerParams(vmem_limit_bytes=VMEM_LIMIT),
        cost_estimate=pl.CostEstimate(flops=flops, bytes_accessed=moved, transcendentals=0),
    )


def convolve(groups, blocks, staged, query_proj, key_proj, value_proj, long_filter, skip_bias):
    tokens, chans = key_proj.shape
    rows = tokens // LANES
    count, axes = groups * blocks, ("groups", "seq")
    own = chans // count
    outer = blocks * rows
    seq_len = blocks * tokens
    part = rows // groups
    if rows % groups or own * part % 8:
        part = rows
    layout = (rows, own, part, groups)
    head, twist, tail, back_tail, back_head = (jnp.asarray(table) for table in make_tables(seq_len))
    size = tokens * chans * 4
    macs = 2 * 3 * own * seq_len * (2 * outer + 4 * LANES)
    where = lax.axis_index("groups").reshape(1).astype(jnp.int32)

    def exchange(array):
        return lax.all_to_all(array, axes, 0, 0, tiled=True)

    sources = (key_proj, value_proj, long_filter, skip_bias.reshape(1, chans))
    packed, bias = call(
        functools.partial(pack_kernel, layout),
        [((count, own * (rows + part), LANES), F32), ((1, chans), F32)],
        [SMEM] + [HBM] * 4, size // 4, size * 3,
        [pltpu.VMEM((tokens, chans), BF16), pltpu.VMEM((tokens, chans), BF16), pltpu.VMEM((part * LANES, chans), F32),
         pltpu.SemaphoreType.DMA((6,))],
    )(where, *(pltpu.with_memory_space_constraint(source, pltpu.HBM) for source in sources))
    if staged:
        by_group = packed.reshape(groups, blocks, own * (rows + part), LANES)
        by_group = lax.all_to_all(by_group, "groups", 0, 0, tiled=True)
        pair = jnp.concatenate([by_group[group] for group in range(groups)], axis=1)
        moved = lax.all_to_all(pair, "seq", 0, 0, tiled=True)
    else:
        moved = exchange(packed)
    local = call(
        functools.partial(conv_kernel, layout, staged, min(own, 4)),
        [((count, own * rows, LANES), F32)], [VMEM] * 6, 5 * macs, 3 * size,
    )(moved, head, twist, tail, back_tail, back_head)[0]
    convolved = exchange(local).reshape(chans * rows, LANES)
    return pl.pallas_call(
        functools.partial(gate_kernel, rows),
        out_shape=pltpu.HBM((tokens, chans), BF16),
        in_specs=[VMEM] * 5,
        out_specs=HBM,
        scratch_shapes=[pltpu.VMEM((tokens, chans), BF16), pltpu.SemaphoreType.DMA((2,))],
        compiler_params=pltpu.CompilerParams(vmem_limit_bytes=VMEM_LIMIT),
        cost_estimate=pl.CostEstimate(flops=size, bytes_accessed=3 * size, transcendentals=0),
    )(convolved, query_proj, key_proj, value_proj, bias)


def shards(groups, blocks, cores, *args):
    if cores == 1 or groups == 1:
        return convolve(groups, blocks, False, *args)
    return lax.cond(
        lax.axis_index("chan") % 2 == 1,
        functools.partial(convolve, groups, blocks, False),
        functools.partial(convolve, groups, blocks, True),
        *args,
    )


def solution(mesh):
    placed = (
        P(("groups", "seq"), "chan"),
        P(("groups", "seq"), "chan"),
        P(("groups", "seq"), "chan"),
        P("seq", "chan"),
        P("chan"),
    )
    body = functools.partial(shards, *(mesh.shape[axis] for axis in ("groups", "seq", "chan")))
    return jax.shard_map(
        body, mesh=mesh, in_specs=placed, out_specs=P(("groups", "seq"), "chan"), check_vma=False
    )
```

```python
import functools

import jax
import jax.numpy as jnp
import ml_dtypes
import numpy as np
from jax import lax
from jax.experimental import pallas as pl
from jax.experimental.pallas import tpu as pltpu
from jax.sharding import PartitionSpec as P

LANES = 128
BF16 = jnp.bfloat16
F32 = jnp.float32
VMEM_LIMIT = 48 * 2**20


def split_np(table):
    high = table.astype(np.float32).astype(ml_dtypes.bfloat16)
    low = (table - high.astype(np.float64)).astype(np.float32).astype(ml_dtypes.bfloat16)
    return high, low


def make_tables(seq_len):
    outer = seq_len // LANES
    n_out, k_out = np.meshgrid(np.arange(outer), np.arange(outer), indexing="ij")
    head = np.exp(-2j * np.pi * (n_out * (4 * k_out + 1) % (4 * outer)) / (4 * outer))
    n_in = np.arange(LANES)
    twist = np.exp(-2j * np.pi * np.outer(4 * np.arange(outer) + 1, n_in) / (4 * seq_len))
    tail = np.exp(-2j * np.pi * (np.outer(n_in, n_in) % LANES) / LANES)

    def block(mat):
        return np.block([[mat.real, mat.imag], [-mat.imag, mat.real]])

    fwd_head = np.concatenate([head.real.T, head.imag.T], axis=0)
    high, low = split_np(fwd_head)
    head_tab = np.concatenate([high, high, low], axis=1)
    high, low = split_np(block(tail))
    tail_tab = np.concatenate([high, high, low], axis=0)
    high, low = split_np(block(tail.conj()))
    back_tail_tab = np.concatenate([high, high, low], axis=0)
    high, low = split_np(np.concatenate([head.real, head.imag], axis=1))
    back_head_tab = np.block([[high, high], [low, np.zeros_like(low)]])
    twist_tab = np.concatenate([twist.real, twist.imag], axis=1).astype(np.float32)
    return head_tab, twist_tab, tail_tab, back_tail_tab, back_head_tab


def halves(values):
    high = values.astype(BF16)
    return high, (values - high.astype(F32)).astype(BF16)


def by_rows(values):
    high, low = halves(values)
    return jnp.concatenate([high, low, high], axis=0)


def by_lanes(values):
    high, low = halves(values)
    return jnp.concatenate([high, low, high], axis=1)


def mat(left, right):
    return jnp.dot(left, right, preferred_element_type=F32)


def head_stage(signals, head, twist):
    outer = signals[0].shape[0]
    mixed = mat(head, by_rows(jnp.concatenate(signals, axis=1)))
    cos, sin = twist[:, :LANES], twist[:, LANES:]
    rows = []
    for idx in range(len(signals)):
        real = mixed[:outer, idx * LANES : (idx + 1) * LANES]
        imag = mixed[outer:, idx * LANES : (idx + 1) * LANES]
        rows.append(jnp.concatenate([real * cos - imag * sin, real * sin + imag * cos], axis=1))
    return jnp.concatenate(rows, axis=0)


def product_stage(spec, outer, groups):
    pieces = [spec[idx * outer : (idx + 1) * outer] for idx in range(spec.shape[0] // outer)]
    own = len(pieces) // (groups + 1)
    prods = []
    for idx, mine in enumerate(pieces[own:]):
        other = pieces[idx // groups]
        f_re, f_im = other[:, :LANES], other[:, LANES:]
        d_re, d_im = mine[:, :LANES], mine[:, LANES:]
        prods.append(jnp.concatenate([d_re * f_re - d_im * f_im, d_re * f_im + d_im * f_re], axis=1))
    return jnp.concatenate(prods, axis=0)


def back_stage(back, cos, sin):
    outer = cos.shape[0]
    reals, imags = [], []
    for idx in range(back.shape[0] // outer):
        mine = back[idx * outer : (idx + 1) * outer]
        real, imag = mine[:, :LANES], mine[:, LANES:]
        reals.append(real * cos + imag * sin)
        imags.append(imag * cos - real * sin)
    return jnp.concatenate([jnp.concatenate(reals, axis=1), jnp.concatenate(imags, axis=1)], axis=0)


def pack_kernel(layout, where_ref, key_ref, value_ref, filter_ref, bias_ref, out_ref, bias_out, key, value, taps, sems):
    rows, own, part, groups = layout
    first = where_ref[0] * (part * LANES if part < rows else 0)
    taken = filter_ref.at[pl.ds(pl.multiple_of(first, part * LANES), part * LANES)]
    cuts = 2 if rows % 2 == 0 else 1
    spans = [pl.ds(cut * rows // cuts * LANES, rows // cuts * LANES) for cut in range(cuts)]
    pairs = [(source.at[span], held.at[span]) for span in spans for source, held in ((key_ref, key), (value_ref, value))]
    pairs += [(taken, taps), (bias_ref, bias_out)]
    fetches = [pltpu.make_async_copy(*pair, sems.at[idx]) for idx, pair in enumerate(pairs)]
    for fetch in fetches:
        fetch.start()
    for row in range(rows):
        if row % (rows // cuts) == 0:
            for fetch in fetches[row // (rows // cuts) * 2 :][:2]:
                fetch.wait()
        span = pl.ds(row * LANES, LANES)
        turned = (key[span, :].astype(F32) * value[span, :].astype(F32)).T
        for peer in range(out_ref.shape[0]):
            out_ref[peer, pl.ds(row, own, stride=rows), :] = turned[peer * own : (peer + 1) * own]
    fetches[-2].wait()
    for row in range(part):
        turned = taps[pl.ds(row * LANES, LANES), :].T
        for peer in range(out_ref.shape[0]):
            out_ref[peer, pl.ds(own * rows + row, own, stride=part), :] = turned[peer * own : (peer + 1) * own]
    fetches[-1].wait()


def arrived(layout, staged, moved_ref, group, start, height):
    rows, own, part, groups = layout
    if staged:
        start += group * own * (rows + part)
        return moved_ref[:, start : start + height]
    blocks = moved_ref.shape[0] // groups
    return moved_ref[pl.ds(group * blocks, blocks), start : start + height]


def driver_signals(layout, staged, moved_ref, chans):
    rows, own, part, groups = layout
    parts = [
        arrived(layout, staged, moved_ref, group, chan * rows, rows) for chan in chans for group in range(groups)
    ]
    return [values.reshape(values.shape[0] * rows, LANES) for values in parts]


def filter_signals(layout, staged, moved_ref, chans):
    rows, own, part, groups = layout
    signals = []
    for chan in chans:
        pieces = [
            arrived(layout, staged, moved_ref, group, own * rows + chan * part, part)
            for group in range(groups if part < rows else 1)
        ]
        signals.append(jnp.concatenate(pieces, axis=1).reshape(pieces[0].shape[0] * rows, LANES))
    return signals


def conv_kernel(
    layout, staged, pieces, moved_ref, head_ref, twist_ref, tail_ref, back_tail_ref, back_head_ref, result_ref, out_ref, sem
):
    rows, own, part, groups = layout
    blocks = out_ref.shape[0] // groups
    outer = blocks * rows
    scale = 1.0 / (outer * LANES)
    cos, sin = twist_ref[:, :LANES] * scale, twist_ref[:, LANES:] * scale
    sets = [range(piece * own // pieces, (piece + 1) * own // pieces) for piece in range(pieces)]
    mixed = [
        head_stage(
            filter_signals(layout, staged, moved_ref, chans) + driver_signals(layout, staged, moved_ref, chans),
            head_ref[...],
            twist_ref[...],
        )
        for chans in sets
    ]
    specs = [mat(by_lanes(values), tail_ref[...]) for values in mixed]
    prods = [product_stage(spec, outer, groups) for spec in specs]
    backs = [mat(by_lanes(values), back_tail_ref[...]) for values in prods]
    turned = [back_stage(back, cos, sin) for back in backs]
    results = [mat(back_head_ref[...], jnp.concatenate(halves(values), axis=0)) for values in turned]
    for chans, result in zip(sets, results):
        result = result[:outer] + result[outer:]
        for idx in range(len(chans) * groups):
            chan, group = divmod(idx, groups)
            start = (chans[0] + chan) * rows
            out_ref[pl.ds(group * blocks, blocks), start : start + rows] = result[
                :, idx * LANES : (idx + 1) * LANES
            ].reshape(blocks, rows, LANES)
    store = pltpu.make_async_copy(out_ref, result_ref, sem)
    store.start()
    store.wait()


def gate_kernel(rows, conv_ref, query_ref, key_ref, value_ref, bias_ref, out_ref, gated, sems):
    bias = bias_ref[...]
    half = rows * LANES // 2
    stores = [
        pltpu.make_async_copy(gated.at[pl.ds(idx * half, half)], out_ref.at[pl.ds(idx * half, half)], sems.at[idx])
        for idx in range(2)
    ]
    for row in range(rows):
        span = pl.ds(row * LANES, LANES)
        driver = key_ref[span, :].astype(F32) * value_ref[span, :].astype(F32)
        convolved = conv_ref[pl.ds(row, LANES, stride=rows), :].T
        gated[span, :] = (query_ref[span, :].astype(F32) * (convolved + bias * driver)).astype(BF16)
        if (row + 1) * LANES == half:
            stores[0].start()
    if rows % 2:
        stores[0].start()
    stores[1].start()
    for store in stores:
        store.wait()


VMEM = pl.BlockSpec(memory_space=pltpu.VMEM)
HBM = pl.BlockSpec(memory_space=pltpu.HBM)
SMEM = pl.BlockSpec(memory_space=pltpu.SMEM)


def call(kernel, outs, specs, flops, moved, scratch=()):
    return pl.pallas_call(
        kernel,
        out_shape=[jax.ShapeDtypeStruct(*out) for out in outs],
        in_specs=specs,
        out_specs=[VMEM] * len(outs),
        scratch_shapes=scratch,
        compiler_params=pltpu.CompilerParams(vmem_limit_bytes=VMEM_LIMIT),
        cost_estimate=pl.CostEstimate(flops=flops, bytes_accessed=moved, transcendentals=0),
    )


def convolve(groups, blocks, staged, query_proj, key_proj, value_proj, long_filter, skip_bias):
    tokens, chans = key_proj.shape
    rows = tokens // LANES
    count, axes = groups * blocks, ("groups", "seq")
    own = chans // count
    outer = blocks * rows
    seq_len = blocks * tokens
    part = rows // groups
    if rows % groups or own * part % 8:
        part = rows
    layout = (rows, own, part, groups)
    head, twist, tail, back_tail, back_head = (jnp.asarray(table) for table in make_tables(seq_len))
    size = tokens * chans * 4
    macs = 2 * 3 * own * seq_len * (2 * outer + 4 * LANES)
    where = lax.axis_index("groups").reshape(1).astype(jnp.int32)

    def exchange(array):
        return lax.all_to_all(array, axes, 0, 0, tiled=True)

    sources = (key_proj, value_proj, long_filter, skip_bias.reshape(1, chans))
    packed, bias = call(
        functools.partial(pack_kernel, layout),
        [((count, own * (rows + part), LANES), F32), ((1, chans), F32)],
        [SMEM] + [HBM] * 4, size // 4, size * 3,
        [pltpu.VMEM((tokens, chans), BF16), pltpu.VMEM((tokens, chans), BF16), pltpu.VMEM((part * LANES, chans), F32),
         pltpu.SemaphoreType.DMA((6,))],
    )(where, *(pltpu.with_memory_space_constraint(source, pltpu.HBM) for source in sources))
    if staged:
        mine = lax.axis_index("groups")
        height = own * (rows + part)
        by_group = packed.reshape(2, blocks, height, LANES)
        first = mine == 0
        kept = jnp.where(first, by_group[0], by_group[1])
        other = lax.ppermute(jnp.where(first, by_group[1], by_group[0]), "groups", [(0, 1), (1, 0)])
        pair = jnp.concatenate([jnp.where(first, kept, other), jnp.where(first, other, kept)], axis=1)
        moved = lax.all_to_all(pair, "seq", 0, 0, tiled=True)
    else:
        moved = exchange(packed)
    local = pl.pallas_call(
        functools.partial(conv_kernel, layout, staged, min(own, 4)),
        out_shape=pltpu.HBM((count, own * rows, LANES), F32),
        in_specs=[VMEM] * 6,
        out_specs=HBM,
        scratch_shapes=[pltpu.VMEM((count, own * rows, LANES), F32), pltpu.SemaphoreType.DMA],
        compiler_params=pltpu.CompilerParams(vmem_limit_bytes=VMEM_LIMIT),
        cost_estimate=pl.CostEstimate(flops=5 * macs, bytes_accessed=3 * size, transcendentals=0),
    )(moved, head, twist, tail, back_tail, back_head)
    convolved = exchange(local).reshape(chans * rows, LANES)
    return pl.pallas_call(
        functools.partial(gate_kernel, rows),
        out_shape=pltpu.HBM((tokens, chans), BF16),
        in_specs=[VMEM] * 5,
        out_specs=HBM,
        scratch_shapes=[pltpu.VMEM((tokens, chans), BF16), pltpu.SemaphoreType.DMA((2,))],
        compiler_params=pltpu.CompilerParams(vmem_limit_bytes=VMEM_LIMIT),
        cost_estimate=pl.CostEstimate(flops=size, bytes_accessed=3 * size, transcendentals=0),
    )(convolved, query_proj, key_proj, value_proj, bias)


def shards(groups, blocks, cores, *args):
    if cores == 1 or groups != 2:
        return convolve(groups, blocks, False, *args)
    return lax.cond(
        lax.axis_index("chan") % 2 == 1,
        functools.partial(convolve, groups, blocks, False),
        functools.partial(convolve, groups, blocks, True),
        *args,
    )


def solution(mesh):
    placed = (
        P(("groups", "seq"), "chan"),
        P(("groups", "seq"), "chan"),
        P(("groups", "seq"), "chan"),
        P("seq", "chan"),
        P("chan"),
    )
    body = functools.partial(shards, *(mesh.shape[axis] for axis in ("groups", "seq", "chan")))
    return jax.shard_map(
        body, mesh=mesh, in_specs=placed, out_specs=P(("groups", "seq"), "chan"), check_vma=False
    )
```

```python
import functools

import jax
import jax.numpy as jnp
import ml_dtypes
import numpy as np
from jax import lax
from jax.experimental import pallas as pl
from jax.experimental.pallas import tpu as pltpu
from jax.sharding import PartitionSpec as P

LANES = 128
BF16 = jnp.bfloat16
F32 = jnp.float32
VMEM_LIMIT = 48 * 2**20


def split_np(table):
    high = table.astype(np.float32).astype(ml_dtypes.bfloat16)
    low = (table - high.astype(np.float64)).astype(np.float32).astype(ml_dtypes.bfloat16)
    return high, low


def make_tables(seq_len):
    outer = seq_len // LANES
    n_out, k_out = np.meshgrid(np.arange(outer), np.arange(outer), indexing="ij")
    head = np.exp(-2j * np.pi * (n_out * (4 * k_out + 1) % (4 * outer)) / (4 * outer))
    n_in = np.arange(LANES)
    twist = np.exp(-2j * np.pi * np.outer(4 * np.arange(outer) + 1, n_in) / (4 * seq_len))
    tail = np.exp(-2j * np.pi * (np.outer(n_in, n_in) % LANES) / LANES)

    def block(mat):
        return np.block([[mat.real, mat.imag], [-mat.imag, mat.real]])

    fwd_head = np.concatenate([head.real.T, head.imag.T], axis=0)
    high, low = split_np(fwd_head)
    head_tab = np.concatenate([high, high, low], axis=1)
    high, low = split_np(block(tail))
    tail_tab = np.concatenate([high, high, low], axis=0)
    high, low = split_np(block(tail.conj()))
    back_tail_tab = np.concatenate([high, high, low], axis=0)
    high, low = split_np(np.concatenate([head.real, head.imag], axis=1))
    back_head_tab = np.block([[high, high], [low, np.zeros_like(low)]])
    twist_tab = np.concatenate([twist.real, twist.imag], axis=1).astype(np.float32)
    return head_tab, twist_tab, tail_tab, back_tail_tab, back_head_tab


def halves(values):
    high = values.astype(BF16)
    return high, (values - high.astype(F32)).astype(BF16)


def by_rows(values):
    high, low = halves(values)
    return jnp.concatenate([high, low, high], axis=0)


def by_lanes(values):
    high, low = halves(values)
    return jnp.concatenate([high, low, high], axis=1)


def mat(left, right):
    return jnp.dot(left, right, preferred_element_type=F32)


def head_stage(signals, head, twist):
    outer = signals[0].shape[0]
    mixed = mat(head, by_rows(jnp.concatenate(signals, axis=1)))
    cos, sin = twist[:, :LANES], twist[:, LANES:]
    rows = []
    for idx in range(len(signals)):
        real = mixed[:outer, idx * LANES : (idx + 1) * LANES]
        imag = mixed[outer:, idx * LANES : (idx + 1) * LANES]
        rows.append(jnp.concatenate([real * cos - imag * sin, real * sin + imag * cos], axis=1))
    return jnp.concatenate(rows, axis=0)


def product_stage(spec, outer, groups):
    pieces = [spec[idx * outer : (idx + 1) * outer] for idx in range(spec.shape[0] // outer)]
    own = len(pieces) // (groups + 1)
    prods = []
    for idx, mine in enumerate(pieces[own:]):
        other = pieces[idx // groups]
        f_re, f_im = other[:, :LANES], other[:, LANES:]
        d_re, d_im = mine[:, :LANES], mine[:, LANES:]
        prods.append(jnp.concatenate([d_re * f_re - d_im * f_im, d_re * f_im + d_im * f_re], axis=1))
    return jnp.concatenate(prods, axis=0)


def back_stage(back, cos, sin):
    outer = cos.shape[0]
    reals, imags = [], []
    for idx in range(back.shape[0] // outer):
        mine = back[idx * outer : (idx + 1) * outer]
        real, imag = mine[:, :LANES], mine[:, LANES:]
        reals.append(real * cos + imag * sin)
        imags.append(imag * cos - real * sin)
    return jnp.concatenate([jnp.concatenate(reals, axis=1), jnp.concatenate(imags, axis=1)], axis=0)


def pack_kernel(layout, staged, where_ref, key_ref, value_ref, filter_ref, bias_ref, out_ref, bias_out, key, value, taps, sems):
    rows, own, part, groups = layout
    count = out_ref.shape[0]
    blocks = count // groups
    homes = [
        ((peer // blocks ^ where_ref[0]) * blocks + peer % blocks if staged else peer, peer * own)
        for peer in range(count)
    ]
    first = where_ref[0] * (part * LANES if part < rows else 0)
    taken = filter_ref.at[pl.ds(pl.multiple_of(first, part * LANES), part * LANES)]
    cuts = 2 if rows % 2 == 0 else 1
    spans = [pl.ds(cut * rows // cuts * LANES, rows // cuts * LANES) for cut in range(cuts)]
    pairs = [(source.at[span], held.at[span]) for span in spans for source, held in ((key_ref, key), (value_ref, value))]
    pairs += [(taken, taps), (bias_ref, bias_out)]
    fetches = [pltpu.make_async_copy(*pair, sems.at[idx]) for idx, pair in enumerate(pairs)]
    for fetch in fetches:
        fetch.start()
    for row in range(rows):
        if row % (rows // cuts) == 0:
            for fetch in fetches[row // (rows // cuts) * 2 :][:2]:
                fetch.wait()
        span = pl.ds(row * LANES, LANES)
        turned = (key[span, :].astype(F32) * value[span, :].astype(F32)).T
        for place, chan in homes:
            out_ref[place, pl.ds(row, own, stride=rows), :] = turned[chan : chan + own]
    fetches[-2].wait()
    for row in range(part):
        turned = taps[pl.ds(row * LANES, LANES), :].T
        for place, chan in homes:
            out_ref[place, pl.ds(own * rows + row, own, stride=part), :] = turned[chan : chan + own]
    fetches[-1].wait()


def arrived(layout, staged, moved_ref, group, start, height):
    rows, own, part, groups = layout
    if staged:
        start += group * own * (rows + part)
        return moved_ref[:, start : start + height]
    blocks = moved_ref.shape[0] // groups
    return moved_ref[pl.ds(group * blocks, blocks), start : start + height]


def driver_signals(layout, staged, moved_ref, chans):
    rows, own, part, groups = layout
    parts = [
        arrived(layout, staged, moved_ref, group, chan * rows, rows) for chan in chans for group in range(groups)
    ]
    return [values.reshape(values.shape[0] * rows, LANES) for values in parts]


def filter_signals(layout, staged, mine, moved_ref, chans):
    rows, own, part, groups = layout
    signals = []
    for chan in chans:
        pieces = [
            arrived(layout, staged, moved_ref, group, own * rows + chan * part, part)
            for group in range(groups if part < rows else 1)
        ]
        if staged and len(pieces) == 2:
            pieces = [jnp.where(mine == 0, pieces[0], pieces[1]), jnp.where(mine == 0, pieces[1], pieces[0])]
        signals.append(jnp.concatenate(pieces, axis=1).reshape(pieces[0].shape[0] * rows, LANES))
    return signals


def conv_kernel(
    layout, staged, pieces, where_ref, moved_ref, head_ref, twist_ref, tail_ref, back_tail_ref, back_head_ref, out_ref
):
    rows, own, part, groups = layout
    mine = where_ref[0]
    blocks = out_ref.shape[0] // groups
    outer = blocks * rows
    scale = 1.0 / (outer * LANES)
    cos, sin = twist_ref[:, :LANES] * scale, twist_ref[:, LANES:] * scale
    sets = [range(piece * own // pieces, (piece + 1) * own // pieces) for piece in range(pieces)]
    mixed = [
        head_stage(
            filter_signals(layout, staged, mine, moved_ref, chans) + driver_signals(layout, staged, moved_ref, chans),
            head_ref[...],
            twist_ref[...],
        )
        for chans in sets
    ]
    specs = [mat(by_lanes(values), tail_ref[...]) for values in mixed]
    prods = [product_stage(spec, outer, groups) for spec in specs]
    backs = [mat(by_lanes(values), back_tail_ref[...]) for values in prods]
    turned = [back_stage(back, cos, sin) for back in backs]
    results = [mat(back_head_ref[...], jnp.concatenate(halves(values), axis=0)) for values in turned]
    for chans, result in zip(sets, results):
        result = result[:outer] + result[outer:]
        for idx in range(len(chans) * groups):
            chan, group = divmod(idx, groups)
            start = (chans[0] + chan) * rows
            group = group ^ mine if staged else group
            out_ref[pl.ds(group * blocks, blocks), start : start + rows] = result[
                :, idx * LANES : (idx + 1) * LANES
            ].reshape(blocks, rows, LANES)


def gate_kernel(rows, conv_ref, query_ref, key_ref, value_ref, bias_ref, out_ref, gated, sems):
    bias = bias_ref[...]
    half = rows * LANES // 2
    stores = [
        pltpu.make_async_copy(gated.at[pl.ds(idx * half, half)], out_ref.at[pl.ds(idx * half, half)], sems.at[idx])
        for idx in range(2)
    ]
    for row in range(rows):
        span = pl.ds(row * LANES, LANES)
        driver = key_ref[span, :].astype(F32) * value_ref[span, :].astype(F32)
        convolved = conv_ref[pl.ds(row, LANES, stride=rows), :].T
        gated[span, :] = (query_ref[span, :].astype(F32) * (convolved + bias * driver)).astype(BF16)
        if (row + 1) * LANES == half:
            stores[0].start()
    if rows % 2:
        stores[0].start()
    stores[1].start()
    for store in stores:
        store.wait()


VMEM = pl.BlockSpec(memory_space=pltpu.VMEM)
HBM = pl.BlockSpec(memory_space=pltpu.HBM)
SMEM = pl.BlockSpec(memory_space=pltpu.SMEM)


def call(kernel, outs, specs, flops, moved, scratch=()):
    return pl.pallas_call(
        kernel,
        out_shape=[jax.ShapeDtypeStruct(*out) for out in outs],
        in_specs=specs,
        out_specs=[VMEM] * len(outs),
        scratch_shapes=scratch,
        compiler_params=pltpu.CompilerParams(vmem_limit_bytes=VMEM_LIMIT),
        cost_estimate=pl.CostEstimate(flops=flops, bytes_accessed=moved, transcendentals=0),
    )


def convolve(groups, blocks, staged, query_proj, key_proj, value_proj, long_filter, skip_bias):
    tokens, chans = key_proj.shape
    rows = tokens // LANES
    count, axes = groups * blocks, ("groups", "seq")
    own = chans // count
    outer = blocks * rows
    seq_len = blocks * tokens
    part = rows // groups
    if rows % groups or own * part % 8:
        part = rows
    layout = (rows, own, part, groups)
    head, twist, tail, back_tail, back_head = (jnp.asarray(table) for table in make_tables(seq_len))
    size = tokens * chans * 4
    macs = 2 * 3 * own * seq_len * (2 * outer + 4 * LANES)
    where = lax.axis_index("groups").reshape(1).astype(jnp.int32)

    def exchange(array):
        return lax.all_to_all(array, axes, 0, 0, tiled=True)

    sources = (key_proj, value_proj, long_filter, skip_bias.reshape(1, chans))
    packed, bias = call(
        functools.partial(pack_kernel, layout, staged),
        [((count, own * (rows + part), LANES), F32), ((1, chans), F32)],
        [SMEM] + [HBM] * 4, size // 4, size * 3,
        [pltpu.VMEM((tokens, chans), BF16), pltpu.VMEM((tokens, chans), BF16), pltpu.VMEM((part * LANES, chans), F32),
         pltpu.SemaphoreType.DMA((6,))],
    )(where, *(pltpu.with_memory_space_constraint(source, pltpu.HBM) for source in sources))
    if staged:
        kept, sent = packed[:blocks], packed[blocks:]
        pair = jnp.concatenate([kept, lax.ppermute(sent, "groups", [(0, 1), (1, 0)])], axis=1)
        moved = lax.all_to_all(pair, "seq", 0, 0, tiled=True)
    else:
        moved = exchange(packed)
    local = call(
        functools.partial(conv_kernel, layout, staged, min(own, 4)),
        [((count, own * rows, LANES), F32)], [SMEM] + [VMEM] * 6, 5 * macs, 3 * size,
    )(where, moved, head, twist, tail, back_tail, back_head)[0]
    convolved = exchange(local).reshape(chans * rows, LANES)
    return pl.pallas_call(
        functools.partial(gate_kernel, rows),
        out_shape=pltpu.HBM((tokens, chans), BF16),
        in_specs=[VMEM] * 5,
        out_specs=HBM,
        scratch_shapes=[pltpu.VMEM((tokens, chans), BF16), pltpu.SemaphoreType.DMA((2,))],
        compiler_params=pltpu.CompilerParams(vmem_limit_bytes=VMEM_LIMIT),
        cost_estimate=pl.CostEstimate(flops=size, bytes_accessed=3 * size, transcendentals=0),
    )(convolved, query_proj, key_proj, value_proj, bias)


def shards(groups, blocks, cores, *args):
    if cores == 1 or groups != 2:
        return convolve(groups, blocks, False, *args)
    return lax.cond(
        lax.axis_index("chan") % 2 == 1,
        functools.partial(convolve, groups, blocks, False),
        functools.partial(convolve, groups, blocks, True),
        *args,
    )


def solution(mesh):
    placed = (
        P(("groups", "seq"), "chan"),
        P(("groups", "seq"), "chan"),
        P(("groups", "seq"), "chan"),
        P("seq", "chan"),
        P("chan"),
    )
    body = functools.partial(shards, *(mesh.shape[axis] for axis in ("groups", "seq", "chan")))
    return jax.shard_map(
        body, mesh=mesh, in_specs=placed, out_specs=P(("groups", "seq"), "chan"), check_vma=False
    )
```

```python
import functools

import jax
import jax.numpy as jnp
import ml_dtypes
import numpy as np
from jax import lax
from jax.experimental import pallas as pl
from jax.experimental.pallas import tpu as pltpu
from jax.sharding import PartitionSpec as P

LANES = 128
BF16 = jnp.bfloat16
F32 = jnp.float32
VMEM_LIMIT = 48 * 2**20


def split_np(table):
    high = table.astype(np.float32).astype(ml_dtypes.bfloat16)
    low = (table - high.astype(np.float64)).astype(np.float32).astype(ml_dtypes.bfloat16)
    return high, low


def make_tables(seq_len):
    outer = seq_len // LANES
    n_out, k_out = np.meshgrid(np.arange(outer), np.arange(outer), indexing="ij")
    head = np.exp(-2j * np.pi * (n_out * (4 * k_out + 1) % (4 * outer)) / (4 * outer))
    n_in = np.arange(LANES)
    twist = np.exp(-2j * np.pi * np.outer(4 * np.arange(outer) + 1, n_in) / (4 * seq_len))
    tail = np.exp(-2j * np.pi * (np.outer(n_in, n_in) % LANES) / LANES)

    def block(mat):
        return np.block([[mat.real, mat.imag], [-mat.imag, mat.real]])

    fwd_head = np.concatenate([head.real.T, head.imag.T], axis=0)
    high, low = split_np(fwd_head)
    head_tab = np.concatenate([high, high, low], axis=1)
    high, low = split_np(block(tail))
    tail_tab = np.concatenate([high, high, low], axis=0)
    high, low = split_np(block(tail.conj()))
    back_tail_tab = np.concatenate([high, high, low], axis=0)
    high, low = split_np(np.concatenate([head.real, head.imag], axis=1))
    back_head_tab = np.block([[high, high], [low, np.zeros_like(low)]])
    twist_tab = np.concatenate([twist.real, twist.imag], axis=1).astype(np.float32)
    return head_tab, twist_tab, tail_tab, back_tail_tab, back_head_tab


def halves(values):
    high = values.astype(BF16)
    return high, (values - high.astype(F32)).astype(BF16)


def by_rows(values):
    high, low = halves(values)
    return jnp.concatenate([high, low, high], axis=0)


def by_lanes(values):
    high, low = halves(values)
    return jnp.concatenate([high, low, high], axis=1)


def mat(left, right):
    return jnp.dot(left, right, preferred_element_type=F32)


def head_stage(signals, head, twist):
    outer = signals[0].shape[0]
    mixed = mat(head, by_rows(jnp.concatenate(signals, axis=1)))
    cos, sin = twist[:, :LANES], twist[:, LANES:]
    rows = []
    for idx in range(len(signals)):
        real = mixed[:outer, idx * LANES : (idx + 1) * LANES]
        imag = mixed[outer:, idx * LANES : (idx + 1) * LANES]
        rows.append(jnp.concatenate([real * cos - imag * sin, real * sin + imag * cos], axis=1))
    return jnp.concatenate(rows, axis=0)


def product_stage(spec, outer, groups):
    pieces = [spec[idx * outer : (idx + 1) * outer] for idx in range(spec.shape[0] // outer)]
    own = len(pieces) // (groups + 1)
    prods = []
    for idx, mine in enumerate(pieces[own:]):
        other = pieces[idx // groups]
        f_re, f_im = other[:, :LANES], other[:, LANES:]
        d_re, d_im = mine[:, :LANES], mine[:, LANES:]
        prods.append(jnp.concatenate([d_re * f_re - d_im * f_im, d_re * f_im + d_im * f_re], axis=1))
    return jnp.concatenate(prods, axis=0)


def back_stage(back, cos, sin):
    outer = cos.shape[0]
    reals, imags = [], []
    for idx in range(back.shape[0] // outer):
        mine = back[idx * outer : (idx + 1) * outer]
        real, imag = mine[:, :LANES], mine[:, LANES:]
        reals.append(real * cos + imag * sin)
        imags.append(imag * cos - real * sin)
    return jnp.concatenate([jnp.concatenate(reals, axis=1), jnp.concatenate(imags, axis=1)], axis=0)


def pack_kernel(layout, staged, where_ref, key_ref, value_ref, filter_ref, bias_ref, out_ref, bias_out, key, value, taps, sems):
    rows, own, part, groups = layout
    count = out_ref.shape[0]
    blocks = count // groups
    homes = [
        ((peer // blocks ^ where_ref[0]) * blocks + peer % blocks if staged else peer, peer * own)
        for peer in range(count)
    ]
    first = where_ref[0] * (part * LANES if part < rows else 0)
    taken = filter_ref.at[pl.ds(pl.multiple_of(first, part * LANES), part * LANES)]
    cuts = 2 if rows % 2 == 0 else 1
    spans = [pl.ds(cut * rows // cuts * LANES, rows // cuts * LANES) for cut in range(cuts)]
    pairs = [(source.at[span], held.at[span]) for span in spans for source, held in ((key_ref, key), (value_ref, value))]
    pairs += [(taken, taps), (bias_ref, bias_out)]
    fetches = [pltpu.make_async_copy(*pair, sems.at[idx]) for idx, pair in enumerate(pairs)]
    for idx, fetch in enumerate(fetches):
        fetch.start(priority=idx % 2)
    for row in range(rows):
        if row % (rows // cuts) == 0:
            for fetch in fetches[row // (rows // cuts) * 2 :][:2]:
                fetch.wait()
        span = pl.ds(row * LANES, LANES)
        turned = (key[span, :].astype(F32) * value[span, :].astype(F32)).T
        for place, chan in homes:
            out_ref[place, pl.ds(row, own, stride=rows), :] = turned[chan : chan + own]
    fetches[-2].wait()
    for row in range(part):
        turned = taps[pl.ds(row * LANES, LANES), :].T
        for place, chan in homes:
            out_ref[place, pl.ds(own * rows + row, own, stride=part), :] = turned[chan : chan + own]
    fetches[-1].wait()


def arrived(layout, staged, moved_ref, group, start, height):
    rows, own, part, groups = layout
    if staged:
        start += group * own * (rows + part)
        return moved_ref[:, start : start + height]
    blocks = moved_ref.shape[0] // groups
    return moved_ref[pl.ds(group * blocks, blocks), start : start + height]


def driver_signals(layout, staged, moved_ref, chans):
    rows, own, part, groups = layout
    parts = [
        arrived(layout, staged, moved_ref, group, chan * rows, rows) for chan in chans for group in range(groups)
    ]
    return [values.reshape(values.shape[0] * rows, LANES) for values in parts]


def filter_signals(layout, staged, mine, moved_ref, chans):
    rows, own, part, groups = layout
    signals = []
    for chan in chans:
        pieces = [
            arrived(layout, staged, moved_ref, group, own * rows + chan * part, part)
            for group in range(groups if part < rows else 1)
        ]
        if staged and len(pieces) == 2:
            pieces = [jnp.where(mine == 0, pieces[0], pieces[1]), jnp.where(mine == 0, pieces[1], pieces[0])]
        signals.append(jnp.concatenate(pieces, axis=1).reshape(pieces[0].shape[0] * rows, LANES))
    return signals


def conv_kernel(
    layout, staged, pieces, where_ref, moved_ref, head_ref, twist_ref, tail_ref, back_tail_ref, back_head_ref, out_ref
):
    rows, own, part, groups = layout
    mine = where_ref[0]
    blocks = out_ref.shape[0] // groups
    outer = blocks * rows
    scale = 1.0 / (outer * LANES)
    cos, sin = twist_ref[:, :LANES] * scale, twist_ref[:, LANES:] * scale
    sets = [range(piece * own // pieces, (piece + 1) * own // pieces) for piece in range(pieces)]
    mixed = [
        head_stage(
            filter_signals(layout, staged, mine, moved_ref, chans) + driver_signals(layout, staged, moved_ref, chans),
            head_ref[...],
            twist_ref[...],
        )
        for chans in sets
    ]
    specs = [mat(by_lanes(values), tail_ref[...]) for values in mixed]
    prods = [product_stage(spec, outer, groups) for spec in specs]
    backs = [mat(by_lanes(values), back_tail_ref[...]) for values in prods]
    turned = [back_stage(back, cos, sin) for back in backs]
    results = [mat(back_head_ref[...], jnp.concatenate(halves(values), axis=0)) for values in turned]
    for chans, result in zip(sets, results):
        result = result[:outer] + result[outer:]
        for idx in range(len(chans) * groups):
            chan, group = divmod(idx, groups)
            start = (chans[0] + chan) * rows
            group = group ^ mine if staged else group
            out_ref[pl.ds(group * blocks, blocks), start : start + rows] = result[
                :, idx * LANES : (idx + 1) * LANES
            ].reshape(blocks, rows, LANES)


def gate_kernel(rows, conv_ref, query_ref, key_ref, value_ref, bias_ref, out_ref, gated, sems):
    bias = bias_ref[...]
    cuts = 4 if rows % 4 == 0 else 1
    size = rows // cuts * LANES
    stores = [
        pltpu.make_async_copy(gated.at[pl.ds(cut * size, size)], out_ref.at[pl.ds(cut * size, size)], sems.at[cut])
        for cut in range(cuts)
    ]
    for row in range(rows):
        span = pl.ds(row * LANES, LANES)
        driver = key_ref[span, :].astype(F32) * value_ref[span, :].astype(F32)
        convolved = conv_ref[pl.ds(row, LANES, stride=rows), :].T
        gated[span, :] = (query_ref[span, :].astype(F32) * (convolved + bias * driver)).astype(BF16)
        if (row + 1) * LANES % size == 0:
            cut = row * LANES // size
            stores[cut].start(priority=cut % 2)
    for store in stores:
        store.wait()


VMEM = pl.BlockSpec(memory_space=pltpu.VMEM)
HBM = pl.BlockSpec(memory_space=pltpu.HBM)
SMEM = pl.BlockSpec(memory_space=pltpu.SMEM)


def call(kernel, outs, specs, flops, moved, scratch=()):
    return pl.pallas_call(
        kernel,
        out_shape=[jax.ShapeDtypeStruct(*out) for out in outs],
        in_specs=specs,
        out_specs=[VMEM] * len(outs),
        scratch_shapes=scratch,
        compiler_params=pltpu.CompilerParams(vmem_limit_bytes=VMEM_LIMIT),
        cost_estimate=pl.CostEstimate(flops=flops, bytes_accessed=moved, transcendentals=0),
    )


def convolve(groups, blocks, staged, query_proj, key_proj, value_proj, long_filter, skip_bias):
    tokens, chans = key_proj.shape
    rows = tokens // LANES
    count, axes = groups * blocks, ("groups", "seq")
    own = chans // count
    outer = blocks * rows
    seq_len = blocks * tokens
    part = rows // groups
    if rows % groups or own * part % 8:
        part = rows
    layout = (rows, own, part, groups)
    head, twist, tail, back_tail, back_head = (jnp.asarray(table) for table in make_tables(seq_len))
    size = tokens * chans * 4
    macs = 2 * 3 * own * seq_len * (2 * outer + 4 * LANES)
    where = lax.axis_index("groups").reshape(1).astype(jnp.int32)

    def exchange(array):
        return lax.all_to_all(array, axes, 0, 0, tiled=True)

    sources = (key_proj, value_proj, long_filter, skip_bias.reshape(1, chans))
    packed, bias = call(
        functools.partial(pack_kernel, layout, staged),
        [((count, own * (rows + part), LANES), F32), ((1, chans), F32)],
        [SMEM] + [HBM] * 4, size // 4, size * 3,
        [pltpu.VMEM((tokens, chans), BF16), pltpu.VMEM((tokens, chans), BF16), pltpu.VMEM((part * LANES, chans), F32),
         pltpu.SemaphoreType.DMA((6,))],
    )(where, *(pltpu.with_memory_space_constraint(source, pltpu.HBM) for source in sources))
    if staged:
        kept, sent = packed[:blocks], packed[blocks:]
        pair = jnp.concatenate([kept, lax.ppermute(sent, "groups", [(0, 1), (1, 0)])], axis=1)
        moved = lax.all_to_all(pair, "seq", 0, 0, tiled=True)
    else:
        moved = exchange(packed)
    local = call(
        functools.partial(conv_kernel, layout, staged, min(own, 4)),
        [((count, own * rows, LANES), F32)], [SMEM] + [VMEM] * 6, 5 * macs, 3 * size,
    )(where, moved, head, twist, tail, back_tail, back_head)[0]
    convolved = exchange(local).reshape(chans * rows, LANES)
    return pl.pallas_call(
        functools.partial(gate_kernel, rows),
        out_shape=pltpu.HBM((tokens, chans), BF16),
        in_specs=[VMEM] * 5,
        out_specs=HBM,
        scratch_shapes=[pltpu.VMEM((tokens, chans), BF16), pltpu.SemaphoreType.DMA((4,))],
        compiler_params=pltpu.CompilerParams(vmem_limit_bytes=VMEM_LIMIT),
        cost_estimate=pl.CostEstimate(flops=size, bytes_accessed=3 * size, transcendentals=0),
    )(convolved, query_proj, key_proj, value_proj, bias)


def shards(groups, blocks, cores, *args):
    if cores == 1 or groups != 2:
        return convolve(groups, blocks, False, *args)
    return lax.cond(
        lax.axis_index("chan") % 2 == 1,
        functools.partial(convolve, groups, blocks, False),
        functools.partial(convolve, groups, blocks, True),
        *args,
    )


def solution(mesh):
    placed = (
        P(("groups", "seq"), "chan"),
        P(("groups", "seq"), "chan"),
        P(("groups", "seq"), "chan"),
        P("seq", "chan"),
        P("chan"),
    )
    body = functools.partial(shards, *(mesh.shape[axis] for axis in ("groups", "seq", "chan")))
    return jax.shard_map(
        body, mesh=mesh, in_specs=placed, out_specs=P(("groups", "seq"), "chan"), check_vma=False
    )
```

```python
import functools

import jax
import jax.numpy as jnp
import ml_dtypes
import numpy as np
from jax import lax
from jax.experimental import pallas as pl
from jax.experimental.pallas import tpu as pltpu
from jax.sharding import PartitionSpec as P

LANES = 128
BF16 = jnp.bfloat16
F32 = jnp.float32
VMEM_LIMIT = 48 * 2**20


def split_np(table):
    high = table.astype(np.float32).astype(ml_dtypes.bfloat16)
    low = (table - high.astype(np.float64)).astype(np.float32).astype(ml_dtypes.bfloat16)
    return high, low


def make_tables(seq_len):
    outer = seq_len // LANES
    n_out, k_out = np.meshgrid(np.arange(outer), np.arange(outer), indexing="ij")
    head = np.exp(-2j * np.pi * (n_out * (4 * k_out + 1) % (4 * outer)) / (4 * outer))
    n_in = np.arange(LANES)
    twist = np.exp(-2j * np.pi * np.outer(4 * np.arange(outer) + 1, n_in) / (4 * seq_len))
    tail = np.exp(-2j * np.pi * (np.outer(n_in, n_in) % LANES) / LANES)

    def block(mat):
        return np.block([[mat.real, mat.imag], [-mat.imag, mat.real]])

    fwd_head = np.concatenate([head.real.T, head.imag.T], axis=0)
    high, low = split_np(fwd_head)
    head_tab = np.concatenate([high, high, low], axis=1)
    high, low = split_np(block(tail))
    tail_tab = np.concatenate([high, high, low], axis=0)
    high, low = split_np(block(tail.conj()))
    back_tail_tab = np.concatenate([high, high, low], axis=0)
    high, low = split_np(np.concatenate([head.real, head.imag], axis=1))
    back_head_tab = np.block([[high, high], [low, np.zeros_like(low)]])
    twist_tab = np.concatenate([twist.real, twist.imag], axis=1).astype(np.float32)
    return head_tab, twist_tab, tail_tab, back_tail_tab, back_head_tab


def halves(values):
    high = values.astype(BF16)
    return high, (values - high.astype(F32)).astype(BF16)


def by_rows(values):
    high, low = halves(values)
    return jnp.concatenate([high, low, high], axis=0)


def by_lanes(values):
    high, low = halves(values)
    return jnp.concatenate([high, low, high], axis=1)


def mat(left, right):
    return jnp.dot(left, right, preferred_element_type=F32)


def head_stage(signals, head, twist):
    outer = signals[0].shape[0]
    mixed = mat(head, by_rows(jnp.concatenate(signals, axis=1)))
    cos, sin = twist[:, :LANES], twist[:, LANES:]
    rows = []
    for idx in range(len(signals)):
        real = mixed[:outer, idx * LANES : (idx + 1) * LANES]
        imag = mixed[outer:, idx * LANES : (idx + 1) * LANES]
        rows.append(jnp.concatenate([real * cos - imag * sin, real * sin + imag * cos], axis=1))
    return jnp.concatenate(rows, axis=0)


def product_stage(spec, outer, groups):
    pieces = [spec[idx * outer : (idx + 1) * outer] for idx in range(spec.shape[0] // outer)]
    own = len(pieces) // (groups + 1)
    prods = []
    for idx, mine in enumerate(pieces[own:]):
        other = pieces[idx // groups]
        f_re, f_im = other[:, :LANES], other[:, LANES:]
        d_re, d_im = mine[:, :LANES], mine[:, LANES:]
        prods.append(jnp.concatenate([d_re * f_re - d_im * f_im, d_re * f_im + d_im * f_re], axis=1))
    return jnp.concatenate(prods, axis=0)


def back_stage(back, cos, sin):
    outer = cos.shape[0]
    reals, imags = [], []
    for idx in range(back.shape[0] // outer):
        mine = back[idx * outer : (idx + 1) * outer]
        real, imag = mine[:, :LANES], mine[:, LANES:]
        reals.append(real * cos + imag * sin)
        imags.append(imag * cos - real * sin)
    return jnp.concatenate([jnp.concatenate(reals, axis=1), jnp.concatenate(imags, axis=1)], axis=0)


def pack_kernel(layout, staged, where_ref, key_ref, value_ref, filter_ref, bias_ref, out_ref, bias_out, key, value, taps, sems):
    rows, own, part, groups = layout
    count = out_ref.shape[0]
    blocks = count // groups
    homes = [
        ((peer // blocks ^ where_ref[0]) * blocks + peer % blocks if staged else peer, peer * own)
        for peer in range(count)
    ]
    first = where_ref[0] * (part * LANES if part < rows else 0)
    taken = filter_ref.at[pl.ds(pl.multiple_of(first, part * LANES), part * LANES)]
    pairs = ((key_ref, key), (value_ref, value), (taken, taps), (bias_ref, bias_out))
    fetches = [pltpu.make_async_copy(*pair, sems.at[idx]) for idx, pair in enumerate(pairs)]
    for fetch in fetches:
        fetch.start()
    fetches[0].wait()
    fetches[1].wait()
    for row in range(rows):
        span = pl.ds(row * LANES, LANES)
        turned = (key[span, :].astype(F32) * value[span, :].astype(F32)).T
        for place, chan in homes:
            out_ref[place, pl.ds(row, own, stride=rows), :] = turned[chan : chan + own]
    fetches[-2].wait()
    for row in range(part):
        turned = taps[pl.ds(row * LANES, LANES), :].T
        for place, chan in homes:
            out_ref[place, pl.ds(own * rows + row, own, stride=part), :] = turned[chan : chan + own]
    fetches[-1].wait()


def arrived(layout, staged, moved_ref, group, start, height):
    rows, own, part, groups = layout
    if staged:
        start += group * own * (rows + part)
        return moved_ref[:, start : start + height]
    blocks = moved_ref.shape[0] // groups
    return moved_ref[pl.ds(group * blocks, blocks), start : start + height]


def driver_signals(layout, staged, moved_ref, chans):
    rows, own, part, groups = layout
    parts = [
        arrived(layout, staged, moved_ref, group, chan * rows, rows) for chan in chans for group in range(groups)
    ]
    return [values.reshape(values.shape[0] * rows, LANES) for values in parts]


def filter_signals(layout, staged, mine, moved_ref, chans):
    rows, own, part, groups = layout
    signals = []
    for chan in chans:
        pieces = [
            arrived(layout, staged, moved_ref, group, own * rows + chan * part, part)
            for group in range(groups if part < rows else 1)
        ]
        if staged and len(pieces) == 2:
            pieces = [jnp.where(mine == 0, pieces[0], pieces[1]), jnp.where(mine == 0, pieces[1], pieces[0])]
        signals.append(jnp.concatenate(pieces, axis=1).reshape(pieces[0].shape[0] * rows, LANES))
    return signals


def conv_kernel(
    layout, staged, pieces, where_ref, moved_ref, head_ref, twist_ref, tail_ref, back_tail_ref, back_head_ref, out_ref
):
    rows, own, part, groups = layout
    mine = where_ref[0]
    blocks = out_ref.shape[0] // groups
    outer = blocks * rows
    scale = 1.0 / (outer * LANES)
    cos, sin = twist_ref[:, :LANES] * scale, twist_ref[:, LANES:] * scale
    sets = [range(piece * own // pieces, (piece + 1) * own // pieces) for piece in range(pieces)]
    mixed = [
        head_stage(
            filter_signals(layout, staged, mine, moved_ref, chans) + driver_signals(layout, staged, moved_ref, chans),
            head_ref[...],
            twist_ref[...],
        )
        for chans in sets
    ]
    specs = [mat(by_lanes(values), tail_ref[...]) for values in mixed]
    prods = [product_stage(spec, outer, groups) for spec in specs]
    backs = [mat(by_lanes(values), back_tail_ref[...]) for values in prods]
    turned = [back_stage(back, cos, sin) for back in backs]
    results = [mat(back_head_ref[...], jnp.concatenate(halves(values), axis=0)) for values in turned]
    for chans, result in zip(sets, results):
        result = result[:outer] + result[outer:]
        for idx in range(len(chans) * groups):
            chan, group = divmod(idx, groups)
            start = (chans[0] + chan) * rows
            group = group ^ mine if staged else group
            out_ref[pl.ds(group * blocks, blocks), start : start + rows] = result[
                :, idx * LANES : (idx + 1) * LANES
            ].reshape(blocks, rows, LANES)


def gate_kernel(rows, conv_ref, query_ref, key_ref, value_ref, bias_ref, out_ref, gated, sems):
    bias = bias_ref[...]
    half = rows * LANES // 2
    stores = [
        pltpu.make_async_copy(gated.at[pl.ds(idx * half, half)], out_ref.at[pl.ds(idx * half, half)], sems.at[idx])
        for idx in range(2)
    ]
    for row in range(rows):
        span = pl.ds(row * LANES, LANES)
        driver = key_ref[span, :].astype(F32) * value_ref[span, :].astype(F32)
        convolved = conv_ref[pl.ds(row, LANES, stride=rows), :].T
        gated[span, :] = (query_ref[span, :].astype(F32) * (convolved + bias * driver)).astype(BF16)
        if (row + 1) * LANES == half:
            stores[0].start()
    if rows % 2:
        stores[0].start()
    stores[1].start()
    for store in stores:
        store.wait()


VMEM = pl.BlockSpec(memory_space=pltpu.VMEM)
HBM = pl.BlockSpec(memory_space=pltpu.HBM)
SMEM = pl.BlockSpec(memory_space=pltpu.SMEM)


def call(kernel, outs, specs, flops, moved, scratch=()):
    return pl.pallas_call(
        kernel,
        out_shape=[jax.ShapeDtypeStruct(*out) for out in outs],
        in_specs=specs,
        out_specs=[VMEM] * len(outs),
        scratch_shapes=scratch,
        compiler_params=pltpu.CompilerParams(vmem_limit_bytes=VMEM_LIMIT),
        cost_estimate=pl.CostEstimate(flops=flops, bytes_accessed=moved, transcendentals=0),
    )


def convolve(groups, blocks, staged, query_proj, key_proj, value_proj, long_filter, skip_bias):
    tokens, chans = key_proj.shape
    rows = tokens // LANES
    count, axes = groups * blocks, ("groups", "seq")
    own = chans // count
    outer = blocks * rows
    seq_len = blocks * tokens
    part = rows // groups
    if rows % groups or own * part % 8:
        part = rows
    layout = (rows, own, part, groups)
    head, twist, tail, back_tail, back_head = (jnp.asarray(table) for table in make_tables(seq_len))
    size = tokens * chans * 4
    macs = 2 * 3 * own * seq_len * (2 * outer + 4 * LANES)
    where = lax.axis_index("groups").reshape(1).astype(jnp.int32)

    def exchange(array):
        return lax.all_to_all(array, axes, 0, 0, tiled=True)

    sources = (key_proj, value_proj, long_filter, skip_bias.reshape(1, chans))
    packed, bias = call(
        functools.partial(pack_kernel, layout, staged),
        [((count, own * (rows + part), LANES), F32), ((1, chans), F32)],
        [SMEM] + [HBM] * 4, size // 4, size * 3,
        [pltpu.VMEM((tokens, chans), BF16), pltpu.VMEM((tokens, chans), BF16), pltpu.VMEM((part * LANES, chans), F32),
         pltpu.SemaphoreType.DMA((4,))],
    )(where, *(pltpu.with_memory_space_constraint(source, pltpu.HBM) for source in sources))
    if staged:
        kept, sent = packed[:blocks], packed[blocks:]
        pair = jnp.concatenate([kept, lax.ppermute(sent, "groups", [(0, 1), (1, 0)])], axis=1)
        moved = lax.all_to_all(pair, "seq", 0, 0, tiled=True)
    else:
        moved = exchange(packed)
    local = call(
        functools.partial(conv_kernel, layout, staged, own),
        [((count, own * rows, LANES), F32)], [SMEM] + [VMEM] * 6, 5 * macs, 3 * size,
    )(where, moved, head, twist, tail, back_tail, back_head)[0]
    convolved = exchange(local).reshape(chans * rows, LANES)
    return pl.pallas_call(
        functools.partial(gate_kernel, rows),
        out_shape=pltpu.HBM((tokens, chans), BF16),
        in_specs=[VMEM] * 5,
        out_specs=HBM,
        scratch_shapes=[pltpu.VMEM((tokens, chans), BF16), pltpu.SemaphoreType.DMA((2,))],
        compiler_params=pltpu.CompilerParams(vmem_limit_bytes=VMEM_LIMIT),
        cost_estimate=pl.CostEstimate(flops=size, bytes_accessed=3 * size, transcendentals=0),
    )(convolved, query_proj, key_proj, value_proj, bias)


def shards(groups, blocks, cores, *args):
    if cores == 1 or groups != 2:
        return convolve(groups, blocks, False, *args)
    return lax.cond(
        lax.axis_index("chan") % 2 == 1,
        functools.partial(convolve, groups, blocks, False),
        functools.partial(convolve, groups, blocks, True),
        *args,
    )


def solution(mesh):
    placed = (
        P(("groups", "seq"), "chan"),
        P(("groups", "seq"), "chan"),
        P(("groups", "seq"), "chan"),
        P("seq", "chan"),
        P("chan"),
    )
    body = functools.partial(shards, *(mesh.shape[axis] for axis in ("groups", "seq", "chan")))
    return jax.shard_map(
        body, mesh=mesh, in_specs=placed, out_specs=P(("groups", "seq"), "chan"), check_vma=False
    )
```

```python
import functools

import jax
import jax.numpy as jnp
import ml_dtypes
import numpy as np
from jax import lax
from jax.experimental import pallas as pl
from jax.experimental.pallas import tpu as pltpu
from jax.sharding import PartitionSpec as P

LANES = 128
BF16 = jnp.bfloat16
F32 = jnp.float32
VMEM_LIMIT = 48 * 2**20


def split_np(table):
    high = table.astype(np.float32).astype(ml_dtypes.bfloat16)
    low = (table - high.astype(np.float64)).astype(np.float32).astype(ml_dtypes.bfloat16)
    return high, low


def make_tables(seq_len):
    outer = seq_len // LANES
    n_out, k_out = np.meshgrid(np.arange(outer), np.arange(outer), indexing="ij")
    head = np.exp(-2j * np.pi * (n_out * (4 * k_out + 1) % (4 * outer)) / (4 * outer))
    n_in = np.arange(LANES)
    twist = np.exp(-2j * np.pi * np.outer(4 * np.arange(outer) + 1, n_in) / (4 * seq_len))
    tail = np.exp(-2j * np.pi * (np.outer(n_in, n_in) % LANES) / LANES)

    def block(mat):
        return np.block([[mat.real, mat.imag], [-mat.imag, mat.real]])

    fwd_head = np.concatenate([head.real.T, head.imag.T], axis=0)
    high, low = split_np(fwd_head)
    head_tab = np.concatenate([high, high, low], axis=1)
    high, low = split_np(block(tail))
    tail_tab = np.concatenate([high, high, low], axis=0)
    high, low = split_np(block(tail.conj()))
    back_tail_tab = np.concatenate([high, high, low], axis=0)
    high, low = split_np(np.concatenate([head.real, head.imag], axis=1))
    back_head_tab = np.block([[high, high], [low, np.zeros_like(low)]])
    twist_tab = np.concatenate([twist.real, twist.imag], axis=1).astype(np.float32)
    return head_tab, twist_tab, tail_tab, back_tail_tab, back_head_tab


def halves(values):
    high = values.astype(BF16)
    return high, (values - high.astype(F32)).astype(BF16)


def by_rows(values):
    high, low = halves(values)
    return jnp.concatenate([high, low, high], axis=0)


def by_lanes(values):
    high, low = halves(values)
    return jnp.concatenate([high, low, high], axis=1)


def mat(left, right):
    return jnp.dot(left, right, preferred_element_type=F32)


def head_stage(signals, head, twist):
    outer = signals[0].shape[0]
    mixed = mat(head, by_rows(jnp.concatenate(signals, axis=1)))
    cos, sin = twist[:, :LANES], twist[:, LANES:]
    rows = []
    for idx in range(len(signals)):
        real = mixed[:outer, idx * LANES : (idx + 1) * LANES]
        imag = mixed[outer:, idx * LANES : (idx + 1) * LANES]
        rows.append(jnp.concatenate([real * cos - imag * sin, real * sin + imag * cos], axis=1))
    return jnp.concatenate(rows, axis=0)


def product_stage(spec, outer, groups):
    pieces = [spec[idx * outer : (idx + 1) * outer] for idx in range(spec.shape[0] // outer)]
    own = len(pieces) // (groups + 1)
    prods = []
    for idx, mine in enumerate(pieces[own:]):
        other = pieces[idx // groups]
        f_re, f_im = other[:, :LANES], other[:, LANES:]
        d_re, d_im = mine[:, :LANES], mine[:, LANES:]
        prods.append(jnp.concatenate([d_re * f_re - d_im * f_im, d_re * f_im + d_im * f_re], axis=1))
    return jnp.concatenate(prods, axis=0)


def back_stage(back, cos, sin):
    outer = cos.shape[0]
    reals, imags = [], []
    for idx in range(back.shape[0] // outer):
        mine = back[idx * outer : (idx + 1) * outer]
        real, imag = mine[:, :LANES], mine[:, LANES:]
        reals.append(real * cos + imag * sin)
        imags.append(imag * cos - real * sin)
    return jnp.concatenate([jnp.concatenate(reals, axis=1), jnp.concatenate(imags, axis=1)], axis=0)


def pack_kernel(layout, staged, where_ref, near_ref, key_ref, value_ref, filter_ref, bias_ref, out_ref, bias_out, key, value, taps, sems):
    rows, own, part, groups = layout
    count = out_ref.shape[0]
    blocks = count // groups
    homes = [
        ((peer % 2 ^ near_ref[0]) * (count // 2) + peer // 2 if staged else peer, peer * own)
        for peer in range(count)
    ]
    first = where_ref[0] * (part * LANES if part < rows else 0)
    taken = filter_ref.at[pl.ds(pl.multiple_of(first, part * LANES), part * LANES)]
    cuts = 2 if rows % 2 == 0 else 1
    spans = [pl.ds(cut * rows // cuts * LANES, rows // cuts * LANES) for cut in range(cuts)]
    pairs = [(source.at[span], held.at[span]) for span in spans for source, held in ((key_ref, key), (value_ref, value))]
    pairs += [(taken, taps), (bias_ref, bias_out)]
    fetches = [pltpu.make_async_copy(*pair, sems.at[idx]) for idx, pair in enumerate(pairs)]
    for fetch in fetches:
        fetch.start()
    for row in range(rows):
        if row % (rows // cuts) == 0:
            for fetch in fetches[row // (rows // cuts) * 2 :][:2]:
                fetch.wait()
        span = pl.ds(row * LANES, LANES)
        turned = (key[span, :].astype(F32) * value[span, :].astype(F32)).T
        for place, chan in homes:
            out_ref[place, pl.ds(row, own, stride=rows), :] = turned[chan : chan + own]
    fetches[-2].wait()
    for row in range(part):
        turned = taps[pl.ds(row * LANES, LANES), :].T
        for place, chan in homes:
            out_ref[place, pl.ds(own * rows + row, own, stride=part), :] = turned[chan : chan + own]
    fetches[-1].wait()


def arrived(layout, staged, near, moved_ref, group, start, height):
    rows, own, part, groups = layout
    if staged:
        far, second = moved_ref.shape[0] // groups, start + own * (rows + part)
        span = pl.ds(group * far, far)
        ours, other = moved_ref[span, start : start + height], moved_ref[span, second : second + height]
        pair = [jnp.where(near == 0, ours, other), jnp.where(near == 0, other, ours)]
        return jnp.stack(pair, axis=1).reshape(2 * far, height, LANES)
    blocks = moved_ref.shape[0] // groups
    return moved_ref[pl.ds(group * blocks, blocks), start : start + height]


def driver_signals(layout, staged, near, moved_ref, chans):
    rows, own, part, groups = layout
    parts = [
        arrived(layout, staged, near, moved_ref, group, chan * rows, rows) for chan in chans for group in range(groups)
    ]
    return [values.reshape(values.shape[0] * rows, LANES) for values in parts]


def filter_signals(layout, staged, near, moved_ref, chans):
    rows, own, part, groups = layout
    signals = []
    for chan in chans:
        pieces = [
            arrived(layout, staged, near, moved_ref, group, own * rows + chan * part, part)
            for group in range(groups if part < rows else 1)
        ]
        signals.append(jnp.concatenate(pieces, axis=1).reshape(pieces[0].shape[0] * rows, LANES))
    return signals


def conv_kernel(
    layout, staged, pieces, near_ref, moved_ref, head_ref, twist_ref, tail_ref, back_tail_ref, back_head_ref, out_ref
):
    rows, own, part, groups = layout
    near = near_ref[0]
    blocks = out_ref.shape[0] // groups
    outer = blocks * rows
    scale = 1.0 / (outer * LANES)
    cos, sin = twist_ref[:, :LANES] * scale, twist_ref[:, LANES:] * scale
    sets = [range(piece * own // pieces, (piece + 1) * own // pieces) for piece in range(pieces)]
    mixed = [
        head_stage(
            filter_signals(layout, staged, near, moved_ref, chans) + driver_signals(layout, staged, near, moved_ref, chans),
            head_ref[...],
            twist_ref[...],
        )
        for chans in sets
    ]
    specs = [mat(by_lanes(values), tail_ref[...]) for values in mixed]
    prods = [product_stage(spec, outer, groups) for spec in specs]
    backs = [mat(by_lanes(values), back_tail_ref[...]) for values in prods]
    turned = [back_stage(back, cos, sin) for back in backs]
    results = [mat(back_head_ref[...], jnp.concatenate(halves(values), axis=0)) for values in turned]
    for chans, result in zip(sets, results):
        result = result[:outer] + result[outer:]
        for idx in range(len(chans) * groups):
            chan, group = divmod(idx, groups)
            start = (chans[0] + chan) * rows
            out_ref[pl.ds(group * blocks, blocks), start : start + rows] = result[
                :, idx * LANES : (idx + 1) * LANES
            ].reshape(blocks, rows, LANES)


def gate_kernel(rows, conv_ref, query_ref, key_ref, value_ref, bias_ref, out_ref, gated, sems):
    bias = bias_ref[...]
    half = rows * LANES // 2
    stores = [
        pltpu.make_async_copy(gated.at[pl.ds(idx * half, half)], out_ref.at[pl.ds(idx * half, half)], sems.at[idx])
        for idx in range(2)
    ]
    for row in range(rows):
        span = pl.ds(row * LANES, LANES)
        driver = key_ref[span, :].astype(F32) * value_ref[span, :].astype(F32)
        convolved = conv_ref[pl.ds(row, LANES, stride=rows), :].T
        gated[span, :] = (query_ref[span, :].astype(F32) * (convolved + bias * driver)).astype(BF16)
        if (row + 1) * LANES == half:
            stores[0].start()
    if rows % 2:
        stores[0].start()
    stores[1].start()
    for store in stores:
        store.wait()


VMEM = pl.BlockSpec(memory_space=pltpu.VMEM)
HBM = pl.BlockSpec(memory_space=pltpu.HBM)
SMEM = pl.BlockSpec(memory_space=pltpu.SMEM)


def call(kernel, outs, specs, flops, moved, scratch=()):
    return pl.pallas_call(
        kernel,
        out_shape=[jax.ShapeDtypeStruct(*out) for out in outs],
        in_specs=specs,
        out_specs=[VMEM] * len(outs),
        scratch_shapes=scratch,
        compiler_params=pltpu.CompilerParams(vmem_limit_bytes=VMEM_LIMIT),
        cost_estimate=pl.CostEstimate(flops=flops, bytes_accessed=moved, transcendentals=0),
    )


def convolve(groups, blocks, staged, query_proj, key_proj, value_proj, long_filter, skip_bias):
    tokens, chans = key_proj.shape
    rows = tokens // LANES
    count, axes = groups * blocks, ("groups", "seq")
    own = chans // count
    outer = blocks * rows
    seq_len = blocks * tokens
    part = rows // groups
    if rows % groups or own * part % 8:
        part = rows
    layout = (rows, own, part, groups)
    head, twist, tail, back_tail, back_head = (jnp.asarray(table) for table in make_tables(seq_len))
    size = tokens * chans * 4
    macs = 2 * 3 * own * seq_len * (2 * outer + 4 * LANES)
    where = lax.axis_index("groups").reshape(1).astype(jnp.int32)
    near = (lax.axis_index("seq") % 2).reshape(1).astype(jnp.int32)

    def exchange(array):
        return lax.all_to_all(array, axes, 0, 0, tiled=True)

    sources = (key_proj, value_proj, long_filter, skip_bias.reshape(1, chans))
    packed, bias = call(
        functools.partial(pack_kernel, layout, staged),
        [((count, own * (rows + part), LANES), F32), ((1, chans), F32)],
        [SMEM] * 2 + [HBM] * 4, size // 4, size * 3,
        [pltpu.VMEM((tokens, chans), BF16), pltpu.VMEM((tokens, chans), BF16), pltpu.VMEM((part * LANES, chans), F32),
         pltpu.SemaphoreType.DMA((6,))],
    )(where, near, *(pltpu.with_memory_space_constraint(source, pltpu.HBM) for source in sources))
    if staged:
        kept, sent = packed[: count // 2], packed[count // 2 :]
        swap = [(block, block ^ 1) for block in range(blocks)]
        pair = jnp.concatenate([kept, lax.ppermute(sent, "seq", swap)], axis=1)
        sides = [list(range(side, count, 2)) for side in range(2)]
        moved = lax.all_to_all(pair, axes, 0, 0, axis_index_groups=sides, tiled=True)
    else:
        moved = exchange(packed)
    local = call(
        functools.partial(conv_kernel, layout, staged, min(own, 4)),
        [((count, own * rows, LANES), F32)], [SMEM] + [VMEM] * 6, 5 * macs, 3 * size,
    )(near, moved, head, twist, tail, back_tail, back_head)[0]
    convolved = exchange(local).reshape(chans * rows, LANES)
    return pl.pallas_call(
        functools.partial(gate_kernel, rows),
        out_shape=pltpu.HBM((tokens, chans), BF16),
        in_specs=[VMEM] * 5,
        out_specs=HBM,
        scratch_shapes=[pltpu.VMEM((tokens, chans), BF16), pltpu.SemaphoreType.DMA((2,))],
        compiler_params=pltpu.CompilerParams(vmem_limit_bytes=VMEM_LIMIT),
        cost_estimate=pl.CostEstimate(flops=size, bytes_accessed=3 * size, transcendentals=0),
    )(convolved, query_proj, key_proj, value_proj, bias)


def shards(groups, blocks, cores, *args):
    if cores == 1 or blocks % 2:
        return convolve(groups, blocks, False, *args)
    return lax.cond(
        lax.axis_index("chan") % 2 == 1,
        functools.partial(convolve, groups, blocks, False),
        functools.partial(convolve, groups, blocks, True),
        *args,
    )


def solution(mesh):
    placed = (
        P(("groups", "seq"), "chan"),
        P(("groups", "seq"), "chan"),
        P(("groups", "seq"), "chan"),
        P("seq", "chan"),
        P("chan"),
    )
    body = functools.partial(shards, *(mesh.shape[axis] for axis in ("groups", "seq", "chan")))
    return jax.shard_map(
        body, mesh=mesh, in_specs=placed, out_specs=P(("groups", "seq"), "chan"), check_vma=False
    )
```

```python
import functools

import jax
import jax.numpy as jnp
import ml_dtypes
import numpy as np
from jax import lax
from jax.experimental import pallas as pl
from jax.experimental.pallas import tpu as pltpu
from jax.sharding import PartitionSpec as P

LANES = 128
BF16 = jnp.bfloat16
F32 = jnp.float32
VMEM_LIMIT = 48 * 2**20


def split_np(table):
    high = table.astype(np.float32).astype(ml_dtypes.bfloat16)
    low = (table - high.astype(np.float64)).astype(np.float32).astype(ml_dtypes.bfloat16)
    return high, low


def make_tables(seq_len):
    outer = seq_len // LANES
    n_out, k_out = np.meshgrid(np.arange(outer), np.arange(outer), indexing="ij")
    head = np.exp(-2j * np.pi * (n_out * (4 * k_out + 1) % (4 * outer)) / (4 * outer))
    n_in = np.arange(LANES)
    twist = np.exp(-2j * np.pi * np.outer(4 * np.arange(outer) + 1, n_in) / (4 * seq_len))
    tail = np.exp(-2j * np.pi * (np.outer(n_in, n_in) % LANES) / LANES)

    def block(mat):
        return np.block([[mat.real, mat.imag], [-mat.imag, mat.real]])

    fwd_head = np.concatenate([head.real.T, head.imag.T], axis=0)
    high, low = split_np(fwd_head)
    head_tab = np.concatenate([high, high, low], axis=1)
    high, low = split_np(block(tail))
    tail_tab = np.concatenate([high, high, low], axis=0)
    high, low = split_np(block(tail.conj()))
    back_tail_tab = np.concatenate([high, high, low], axis=0)
    high, low = split_np(np.concatenate([head.real, head.imag], axis=1))
    back_head_tab = np.block([[high, high], [low, np.zeros_like(low)]])
    twist_tab = np.concatenate([twist.real, twist.imag], axis=1).astype(np.float32)
    return head_tab, twist_tab, tail_tab, back_tail_tab, back_head_tab


def halves(values):
    high = values.astype(BF16)
    return high, (values - high.astype(F32)).astype(BF16)


def by_rows(values):
    high, low = halves(values)
    return jnp.concatenate([high, low, high], axis=0)


def by_lanes(values):
    high, low = halves(values)
    return jnp.concatenate([high, low, high], axis=1)


def mat(left, right):
    return jnp.dot(left, right, preferred_element_type=F32)


def head_stage(signals, head, twist):
    outer = signals[0].shape[0]
    mixed = mat(head, by_rows(jnp.concatenate(signals, axis=1)))
    cos, sin = twist[:, :LANES], twist[:, LANES:]
    rows = []
    for idx in range(len(signals)):
        real = mixed[:outer, idx * LANES : (idx + 1) * LANES]
        imag = mixed[outer:, idx * LANES : (idx + 1) * LANES]
        rows.append(jnp.concatenate([real * cos - imag * sin, real * sin + imag * cos], axis=1))
    return jnp.concatenate(rows, axis=0)


def product_stage(spec, outer, groups):
    pieces = [spec[idx * outer : (idx + 1) * outer] for idx in range(spec.shape[0] // outer)]
    own = len(pieces) // (groups + 1)
    prods = []
    for idx, mine in enumerate(pieces[own:]):
        other = pieces[idx // groups]
        f_re, f_im = other[:, :LANES], other[:, LANES:]
        d_re, d_im = mine[:, :LANES], mine[:, LANES:]
        prods.append(jnp.concatenate([d_re * f_re - d_im * f_im, d_re * f_im + d_im * f_re], axis=1))
    return jnp.concatenate(prods, axis=0)


def back_stage(back, cos, sin):
    outer = cos.shape[0]
    reals, imags = [], []
    for idx in range(back.shape[0] // outer):
        mine = back[idx * outer : (idx + 1) * outer]
        real, imag = mine[:, :LANES], mine[:, LANES:]
        reals.append(real * cos + imag * sin)
        imags.append(imag * cos - real * sin)
    return jnp.concatenate([jnp.concatenate(reals, axis=1), jnp.concatenate(imags, axis=1)], axis=0)


def pack_kernel(layout, staged, with_driver, with_filter, where_ref, near_ref, *refs):
    rows, own, part, groups = layout
    refs = list(refs)
    sources = [refs.pop(0) for _ in range(3 * with_driver + with_filter)]
    out_ref = refs.pop(0)
    held = ([refs.pop(0)] if with_driver else []) + refs[:-1]
    sems = refs[-1]
    if with_driver:
        held = held[1:3] + held[:1] + held[3:]
    if with_filter:
        first = where_ref[0] * (part * LANES if part < rows else 0)
        sources[-1] = sources[-1].at[pl.ds(pl.multiple_of(first, part * LANES), part * LANES)]
    fetches = [pltpu.make_async_copy(*pair, sems.at[idx]) for idx, pair in enumerate(zip(sources, held))]
    for fetch in fetches:
        fetch.start()
    count = out_ref.shape[0]
    homes = [
        ((peer % 2 ^ near_ref[0]) * (count // 2) + peer // 2 if staged else peer, peer * own)
        for peer in range(count)
    ]
    if with_driver:
        fetches[0].wait()
        fetches[1].wait()
        for row in range(rows):
            span = pl.ds(row * LANES, LANES)
            turned = (held[0][span, :].astype(F32) * held[1][span, :].astype(F32)).T
            for place, chan in homes:
                out_ref[place, pl.ds(row, own, stride=rows), :] = turned[chan : chan + own]
    if with_filter:
        fetches[-1].wait()
        base = own * rows * with_driver
        for row in range(part):
            turned = held[-1][pl.ds(row * LANES, LANES), :].T
            for place, chan in homes:
                out_ref[place, pl.ds(base + row, own, stride=part), :] = turned[chan : chan + own]
    if with_driver:
        fetches[2].wait()


def arrived(layout, staged, near, moved_ref, group, start, height):
    rows, own, part, groups = layout
    if staged:
        far, second = moved_ref.shape[0] // groups, start + own * (rows + part)
        span = pl.ds(group * far, far)
        ours, other = moved_ref[span, start : start + height], moved_ref[span, second : second + height]
        pair = [jnp.where(near == 0, ours, other), jnp.where(near == 0, other, ours)]
        return jnp.stack(pair, axis=1).reshape(2 * far, height, LANES)
    blocks = moved_ref.shape[0] // groups
    return moved_ref[pl.ds(group * blocks, blocks), start : start + height]


def driver_signals(layout, staged, near, moved_ref, chans):
    rows, own, part, groups = layout
    parts = [
        arrived(layout, staged, near, moved_ref, group, chan * rows, rows) for chan in chans for group in range(groups)
    ]
    return [values.reshape(values.shape[0] * rows, LANES) for values in parts]


def filter_signals(layout, staged, near, moved_ref, chans):
    rows, own, part, groups = layout
    signals = []
    for chan in chans:
        pieces = [
            arrived(layout, staged, near, moved_ref, group, own * rows + chan * part, part)
            for group in range(groups if part < rows else 1)
        ]
        signals.append(jnp.concatenate(pieces, axis=1).reshape(pieces[0].shape[0] * rows, LANES))
    return signals


def conv_kernel(
    layout, staged, pieces, near_ref, moved_ref, head_ref, twist_ref, tail_ref, back_tail_ref, back_head_ref, out_ref
):
    rows, own, part, groups = layout
    near = near_ref[0]
    blocks = out_ref.shape[0] // groups
    outer = blocks * rows
    scale = 1.0 / (outer * LANES)
    cos, sin = twist_ref[:, :LANES] * scale, twist_ref[:, LANES:] * scale
    sets = [range(piece * own // pieces, (piece + 1) * own // pieces) for piece in range(pieces)]
    mixed = [
        head_stage(
            filter_signals(layout, staged, near, moved_ref, chans) + driver_signals(layout, staged, near, moved_ref, chans),
            head_ref[...],
            twist_ref[...],
        )
        for chans in sets
    ]
    specs = [mat(by_lanes(values), tail_ref[...]) for values in mixed]
    prods = [product_stage(spec, outer, groups) for spec in specs]
    backs = [mat(by_lanes(values), back_tail_ref[...]) for values in prods]
    turned = [back_stage(back, cos, sin) for back in backs]
    results = [mat(back_head_ref[...], jnp.concatenate(halves(values), axis=0)) for values in turned]
    for chans, result in zip(sets, results):
        result = result[:outer] + result[outer:]
        for idx in range(len(chans) * groups):
            chan, group = divmod(idx, groups)
            start = (chans[0] + chan) * rows
            out_ref[pl.ds(group * blocks, blocks), start : start + rows] = result[
                :, idx * LANES : (idx + 1) * LANES
            ].reshape(blocks, rows, LANES)


def gate_kernel(rows, conv_ref, query_ref, key_ref, value_ref, bias_ref, out_ref, gated, sems):
    bias = bias_ref[...]
    half = rows * LANES // 2
    stores = [
        pltpu.make_async_copy(gated.at[pl.ds(idx * half, half)], out_ref.at[pl.ds(idx * half, half)], sems.at[idx])
        for idx in range(2)
    ]
    for row in range(rows):
        span = pl.ds(row * LANES, LANES)
        driver = key_ref[span, :].astype(F32) * value_ref[span, :].astype(F32)
        convolved = conv_ref[pl.ds(row, LANES, stride=rows), :].T
        gated[span, :] = (query_ref[span, :].astype(F32) * (convolved + bias * driver)).astype(BF16)
        if (row + 1) * LANES == half:
            stores[0].start()
    if rows % 2:
        stores[0].start()
    stores[1].start()
    for store in stores:
        store.wait()


VMEM = pl.BlockSpec(memory_space=pltpu.VMEM)
HBM = pl.BlockSpec(memory_space=pltpu.HBM)
SMEM = pl.BlockSpec(memory_space=pltpu.SMEM)


def call(kernel, outs, specs, flops, moved, scratch=()):
    return pl.pallas_call(
        kernel,
        out_shape=[jax.ShapeDtypeStruct(*out) for out in outs],
        in_specs=specs,
        out_specs=[VMEM] * len(outs),
        scratch_shapes=scratch,
        compiler_params=pltpu.CompilerParams(vmem_limit_bytes=VMEM_LIMIT),
        cost_estimate=pl.CostEstimate(flops=flops, bytes_accessed=moved, transcendentals=0),
    )


def convolve(groups, blocks, staged, query_proj, key_proj, value_proj, long_filter, skip_bias):
    tokens, chans = key_proj.shape
    rows = tokens // LANES
    count, axes = groups * blocks, ("groups", "seq")
    own = chans // count
    outer = blocks * rows
    seq_len = blocks * tokens
    part = rows // groups
    if rows % groups or own * part % 8:
        part = rows
    layout = (rows, own, part, groups)
    head, twist, tail, back_tail, back_head = (jnp.asarray(table) for table in make_tables(seq_len))
    size = tokens * chans * 4
    macs = 2 * 3 * own * seq_len * (2 * outer + 4 * LANES)
    where = lax.axis_index("groups").reshape(1).astype(jnp.int32)
    near = (lax.axis_index("seq") % 2).reshape(1).astype(jnp.int32)

    def exchange(array):
        return lax.all_to_all(array, axes, 0, 0, tiled=True)

    def pack(with_driver, with_filter):
        sources = [key_proj, value_proj, skip_bias.reshape(1, chans)] * with_driver + [long_filter] * with_filter
        tall = [(tokens, BF16), (tokens, BF16)] * with_driver + [(part * LANES, F32)] * with_filter
        height = own * (rows * with_driver + part * with_filter)
        return call(
            functools.partial(pack_kernel, layout, staged, with_driver, with_filter),
            [((count, height, LANES), F32)] + [((1, chans), F32)] * with_driver,
            [SMEM] * 2 + [HBM] * len(sources), size // 4, size * 3,
            [pltpu.VMEM((rows_held, chans), kind) for rows_held, kind in tall]
            + [pltpu.SemaphoreType.DMA((len(sources),))],
        )(where, near, *(pltpu.with_memory_space_constraint(source, pltpu.HBM) for source in sources))

    if staged:
        swap = [(block, block ^ 1) for block in range(blocks)]
        packed, bias = pack(1, 0)
        half = count // 2
        driver_blocks = [packed[:half], lax.ppermute(packed[half:], "seq", swap)]
        packed = pack(0, 1)[0]
        filter_blocks = [packed[:half], lax.ppermute(packed[half:], "seq", swap)]
        pair = jnp.concatenate([driver_blocks[0], filter_blocks[0], driver_blocks[1], filter_blocks[1]], axis=1)
        sides = [list(range(side, count, 2)) for side in range(2)]
        moved = lax.all_to_all(pair, axes, 0, 0, axis_index_groups=sides, tiled=True)
    else:
        packed, bias = pack(1, 1)
        moved = exchange(packed)
    local = call(
        functools.partial(conv_kernel, layout, staged, min(own, 4)),
        [((count, own * rows, LANES), F32)], [SMEM] + [VMEM] * 6, 5 * macs, 3 * size,
    )(near, moved, head, twist, tail, back_tail, back_head)[0]
    convolved = exchange(local).reshape(chans * rows, LANES)
    return pl.pallas_call(
        functools.partial(gate_kernel, rows),
        out_shape=pltpu.HBM((tokens, chans), BF16),
        in_specs=[VMEM] * 5,
        out_specs=HBM,
        scratch_shapes=[pltpu.VMEM((tokens, chans), BF16), pltpu.SemaphoreType.DMA((2,))],
        compiler_params=pltpu.CompilerParams(vmem_limit_bytes=VMEM_LIMIT),
        cost_estimate=pl.CostEstimate(flops=size, bytes_accessed=3 * size, transcendentals=0),
    )(convolved, query_proj, key_proj, value_proj, bias)


def shards(groups, blocks, cores, *args):
    if cores == 1 or blocks % 2:
        return convolve(groups, blocks, False, *args)
    return lax.cond(
        lax.axis_index("chan") % 2 == 1,
        functools.partial(convolve, groups, blocks, False),
        functools.partial(convolve, groups, blocks, True),
        *args,
    )


def solution(mesh):
    placed = (
        P(("groups", "seq"), "chan"),
        P(("groups", "seq"), "chan"),
        P(("groups", "seq"), "chan"),
        P("seq", "chan"),
        P("chan"),
    )
    body = functools.partial(shards, *(mesh.shape[axis] for axis in ("groups", "seq", "chan")))
    return jax.shard_map(
        body, mesh=mesh, in_specs=placed, out_specs=P(("groups", "seq"), "chan"), check_vma=False
    )
```

```python
import functools

import jax
import jax.numpy as jnp
import ml_dtypes
import numpy as np
from jax import lax
from jax.experimental import pallas as pl
from jax.experimental.pallas import tpu as pltpu
from jax.sharding import PartitionSpec as P

LANES = 128
BF16 = jnp.bfloat16
F32 = jnp.float32
VMEM_LIMIT = 48 * 2**20


def split_np(table):
    high = table.astype(np.float32).astype(ml_dtypes.bfloat16)
    low = (table - high.astype(np.float64)).astype(np.float32).astype(ml_dtypes.bfloat16)
    return high, low


def make_tables(seq_len):
    outer = seq_len // LANES
    n_out, k_out = np.meshgrid(np.arange(outer), np.arange(outer), indexing="ij")
    head = np.exp(-2j * np.pi * (n_out * (4 * k_out + 1) % (4 * outer)) / (4 * outer))
    n_in = np.arange(LANES)
    twist = np.exp(-2j * np.pi * np.outer(4 * np.arange(outer) + 1, n_in) / (4 * seq_len))
    tail = np.exp(-2j * np.pi * (np.outer(n_in, n_in) % LANES) / LANES)

    def block(mat):
        return np.block([[mat.real, mat.imag], [-mat.imag, mat.real]])

    fwd_head = np.concatenate([head.real.T, head.imag.T], axis=0)
    high, low = split_np(fwd_head)
    head_tab = np.concatenate([high, high, low], axis=1)
    high, low = split_np(block(tail))
    tail_tab = np.concatenate([high, high, low], axis=0)
    high, low = split_np(block(tail.conj()))
    back_tail_tab = np.concatenate([high, high, low], axis=0)
    high, low = split_np(np.concatenate([head.real, head.imag], axis=1))
    back_head_tab = np.block([[high, high], [low, np.zeros_like(low)]])
    twist_tab = np.concatenate([twist.real, twist.imag], axis=1).astype(np.float32)
    return head_tab, twist_tab, tail_tab, back_tail_tab, back_head_tab


def halves(values):
    high = values.astype(BF16)
    return high, (values - high.astype(F32)).astype(BF16)


def by_rows(values):
    high, low = halves(values)
    return jnp.concatenate([high, low, high], axis=0)


def by_lanes(values):
    high, low = halves(values)
    return jnp.concatenate([high, low, high], axis=1)


def mat(left, right):
    return jnp.dot(left, right, preferred_element_type=F32)


def head_stage(signals, head, twist):
    outer = signals[0].shape[0]
    mixed = mat(head, by_rows(jnp.concatenate(signals, axis=1)))
    cos, sin = twist[:, :LANES], twist[:, LANES:]
    rows = []
    for idx in range(len(signals)):
        real = mixed[:outer, idx * LANES : (idx + 1) * LANES]
        imag = mixed[outer:, idx * LANES : (idx + 1) * LANES]
        rows.append(jnp.concatenate([real * cos - imag * sin, real * sin + imag * cos], axis=1))
    return jnp.concatenate(rows, axis=0)


def product_stage(spec, outer, groups):
    pieces = [spec[idx * outer : (idx + 1) * outer] for idx in range(spec.shape[0] // outer)]
    own = len(pieces) // (groups + 1)
    prods = []
    for idx, mine in enumerate(pieces[own:]):
        other = pieces[idx // groups]
        f_re, f_im = other[:, :LANES], other[:, LANES:]
        d_re, d_im = mine[:, :LANES], mine[:, LANES:]
        prods.append(jnp.concatenate([d_re * f_re - d_im * f_im, d_re * f_im + d_im * f_re], axis=1))
    return jnp.concatenate(prods, axis=0)


def back_stage(back, cos, sin):
    outer = cos.shape[0]
    reals, imags = [], []
    for idx in range(back.shape[0] // outer):
        mine = back[idx * outer : (idx + 1) * outer]
        real, imag = mine[:, :LANES], mine[:, LANES:]
        reals.append(real * cos + imag * sin)
        imags.append(imag * cos - real * sin)
    return jnp.concatenate([jnp.concatenate(reals, axis=1), jnp.concatenate(imags, axis=1)], axis=0)


def pack_kernel(layout, staged, where_ref, near_ref, key_ref, value_ref, filter_ref, bias_ref, out_ref, bias_out, key, value, taps, sems):
    rows, own, part, groups = layout
    count = out_ref.shape[0]
    blocks = count // groups
    homes = [
        (((peer // blocks + peer) % 2 ^ near_ref[0]) * (count // 2) + peer // 2 if staged else peer, peer * own)
        for peer in range(count)
    ]
    first = where_ref[0] * (part * LANES if part < rows else 0)
    taken = filter_ref.at[pl.ds(pl.multiple_of(first, part * LANES), part * LANES)]
    cuts = 2 if rows % 2 == 0 else 1
    spans = [pl.ds(cut * rows // cuts * LANES, rows // cuts * LANES) for cut in range(cuts)]
    pairs = [(source.at[span], held.at[span]) for span in spans for source, held in ((key_ref, key), (value_ref, value))]
    pairs += [(taken, taps), (bias_ref, bias_out)]
    fetches = [pltpu.make_async_copy(*pair, sems.at[idx]) for idx, pair in enumerate(pairs)]
    for fetch in fetches:
        fetch.start()
    for row in range(rows):
        if row % (rows // cuts) == 0:
            for fetch in fetches[row // (rows // cuts) * 2 :][:2]:
                fetch.wait()
        span = pl.ds(row * LANES, LANES)
        turned = (key[span, :].astype(F32) * value[span, :].astype(F32)).T
        for place, chan in homes:
            out_ref[place, pl.ds(row, own, stride=rows), :] = turned[chan : chan + own]
    fetches[-2].wait()
    for row in range(part):
        turned = taps[pl.ds(row * LANES, LANES), :].T
        for place, chan in homes:
            out_ref[place, pl.ds(own * rows + row, own, stride=part), :] = turned[chan : chan + own]
    fetches[-1].wait()


def arrived(layout, staged, near, moved_ref, group, start, height):
    rows, own, part, groups = layout
    if staged:
        far, second = moved_ref.shape[0] // groups, start + own * (rows + part)
        span = pl.ds(group * far, far)
        ours, other = moved_ref[span, start : start + height], moved_ref[span, second : second + height]
        near = near ^ group % 2
        pair = [jnp.where(near == 0, ours, other), jnp.where(near == 0, other, ours)]
        return jnp.stack(pair, axis=1).reshape(2 * far, height, LANES)
    blocks = moved_ref.shape[0] // groups
    return moved_ref[pl.ds(group * blocks, blocks), start : start + height]


def driver_signals(layout, staged, near, moved_ref, chans):
    rows, own, part, groups = layout
    parts = [
        arrived(layout, staged, near, moved_ref, group, chan * rows, rows) for chan in chans for group in range(groups)
    ]
    return [values.reshape(values.shape[0] * rows, LANES) for values in parts]


def filter_signals(layout, staged, near, moved_ref, chans):
    rows, own, part, groups = layout
    signals = []
    for chan in chans:
        pieces = [
            arrived(layout, staged, near, moved_ref, group, own * rows + chan * part, part)
            for group in range(groups if part < rows else 1)
        ]
        signals.append(jnp.concatenate(pieces, axis=1).reshape(pieces[0].shape[0] * rows, LANES))
    return signals


def conv_kernel(
    layout, staged, pieces, near_ref, moved_ref, head_ref, twist_ref, tail_ref, back_tail_ref, back_head_ref, out_ref
):
    rows, own, part, groups = layout
    near = near_ref[0]
    blocks = out_ref.shape[0] // groups
    outer = blocks * rows
    scale = 1.0 / (outer * LANES)
    cos, sin = twist_ref[:, :LANES] * scale, twist_ref[:, LANES:] * scale
    sets = [range(piece * own // pieces, (piece + 1) * own // pieces) for piece in range(pieces)]
    mixed = [
        head_stage(
            filter_signals(layout, staged, near, moved_ref, chans) + driver_signals(layout, staged, near, moved_ref, chans),
            head_ref[...],
            twist_ref[...],
        )
        for chans in sets
    ]
    specs = [mat(by_lanes(values), tail_ref[...]) for values in mixed]
    prods = [product_stage(spec, outer, groups) for spec in specs]
    backs = [mat(by_lanes(values), back_tail_ref[...]) for values in prods]
    turned = [back_stage(back, cos, sin) for back in backs]
    results = [mat(back_head_ref[...], jnp.concatenate(halves(values), axis=0)) for values in turned]
    for chans, result in zip(sets, results):
        result = result[:outer] + result[outer:]
        for idx in range(len(chans) * groups):
            chan, group = divmod(idx, groups)
            start = (chans[0] + chan) * rows
            out_ref[pl.ds(group * blocks, blocks), start : start + rows] = result[
                :, idx * LANES : (idx + 1) * LANES
            ].reshape(blocks, rows, LANES)


def gate_kernel(rows, conv_ref, query_ref, key_ref, value_ref, bias_ref, out_ref, gated, sems):
    bias = bias_ref[...]
    half = rows * LANES // 2
    stores = [
        pltpu.make_async_copy(gated.at[pl.ds(idx * half, half)], out_ref.at[pl.ds(idx * half, half)], sems.at[idx])
        for idx in range(2)
    ]
    for row in range(rows):
        span = pl.ds(row * LANES, LANES)
        driver = key_ref[span, :].astype(F32) * value_ref[span, :].astype(F32)
        convolved = conv_ref[pl.ds(row, LANES, stride=rows), :].T
        gated[span, :] = (query_ref[span, :].astype(F32) * (convolved + bias * driver)).astype(BF16)
        if (row + 1) * LANES == half:
            stores[0].start()
    if rows % 2:
        stores[0].start()
    stores[1].start()
    for store in stores:
        store.wait()


VMEM = pl.BlockSpec(memory_space=pltpu.VMEM)
HBM = pl.BlockSpec(memory_space=pltpu.HBM)
SMEM = pl.BlockSpec(memory_space=pltpu.SMEM)


def call(kernel, outs, specs, flops, moved, scratch=()):
    return pl.pallas_call(
        kernel,
        out_shape=[jax.ShapeDtypeStruct(*out) for out in outs],
        in_specs=specs,
        out_specs=[VMEM] * len(outs),
        scratch_shapes=scratch,
        compiler_params=pltpu.CompilerParams(vmem_limit_bytes=VMEM_LIMIT),
        cost_estimate=pl.CostEstimate(flops=flops, bytes_accessed=moved, transcendentals=0),
    )


def convolve(groups, blocks, staged, query_proj, key_proj, value_proj, long_filter, skip_bias):
    tokens, chans = key_proj.shape
    rows = tokens // LANES
    count, axes = groups * blocks, ("groups", "seq")
    own = chans // count
    outer = blocks * rows
    seq_len = blocks * tokens
    part = rows // groups
    if rows % groups or own * part % 8:
        part = rows
    layout = (rows, own, part, groups)
    head, twist, tail, back_tail, back_head = (jnp.asarray(table) for table in make_tables(seq_len))
    size = tokens * chans * 4
    macs = 2 * 3 * own * seq_len * (2 * outer + 4 * LANES)
    where = lax.axis_index("groups").reshape(1).astype(jnp.int32)
    near = ((lax.axis_index("groups") + lax.axis_index("seq")) % 2).reshape(1).astype(jnp.int32)

    def exchange(array):
        return lax.all_to_all(array, axes, 0, 0, tiled=True)

    sources = (key_proj, value_proj, long_filter, skip_bias.reshape(1, chans))
    packed, bias = call(
        functools.partial(pack_kernel, layout, staged),
        [((count, own * (rows + part), LANES), F32), ((1, chans), F32)],
        [SMEM] * 2 + [HBM] * 4, size // 4, size * 3,
        [pltpu.VMEM((tokens, chans), BF16), pltpu.VMEM((tokens, chans), BF16), pltpu.VMEM((part * LANES, chans), F32),
         pltpu.SemaphoreType.DMA((6,))],
    )(where, near, *(pltpu.with_memory_space_constraint(source, pltpu.HBM) for source in sources))
    if staged:
        kept, sent = packed[: count // 2], packed[count // 2 :]
        swap = [(block, block ^ 1) for block in range(blocks)]
        pair = jnp.concatenate([kept, lax.ppermute(sent, "seq", swap)], axis=1)
        sides = [[peer for peer in range(count) if (peer // blocks + peer) % 2 == side] for side in range(2)]
        moved = lax.all_to_all(pair, axes, 0, 0, axis_index_groups=sides, tiled=True)
    else:
        moved = exchange(packed)
    local = call(
        functools.partial(conv_kernel, layout, staged, min(own, 4)),
        [((count, own * rows, LANES), F32)], [SMEM] + [VMEM] * 6, 5 * macs, 3 * size,
    )(near, moved, head, twist, tail, back_tail, back_head)[0]
    convolved = exchange(local).reshape(chans * rows, LANES)
    return pl.pallas_call(
        functools.partial(gate_kernel, rows),
        out_shape=pltpu.HBM((tokens, chans), BF16),
        in_specs=[VMEM] * 5,
        out_specs=HBM,
        scratch_shapes=[pltpu.VMEM((tokens, chans), BF16), pltpu.SemaphoreType.DMA((2,))],
        compiler_params=pltpu.CompilerParams(vmem_limit_bytes=VMEM_LIMIT),
        cost_estimate=pl.CostEstimate(flops=size, bytes_accessed=3 * size, transcendentals=0),
    )(convolved, query_proj, key_proj, value_proj, bias)


def shards(groups, blocks, cores, *args):
    if cores == 1 or blocks % 2:
        return convolve(groups, blocks, False, *args)
    return lax.cond(
        lax.axis_index("chan") % 2 == 1,
        functools.partial(convolve, groups, blocks, False),
        functools.partial(convolve, groups, blocks, True),
        *args,
    )


def solution(mesh):
    placed = (
        P(("groups", "seq"), "chan"),
        P(("groups", "seq"), "chan"),
        P(("groups", "seq"), "chan"),
        P("seq", "chan"),
        P("chan"),
    )
    body = functools.partial(shards, *(mesh.shape[axis] for axis in ("groups", "seq", "chan")))
    return jax.shard_map(
        body, mesh=mesh, in_specs=placed, out_specs=P(("groups", "seq"), "chan"), check_vma=False
    )
```

```python
import functools

import jax
import jax.numpy as jnp
import ml_dtypes
import numpy as np
from jax import lax
from jax.experimental import pallas as pl
from jax.experimental.pallas import tpu as pltpu
from jax.sharding import PartitionSpec as P

LANES = 128
BF16 = jnp.bfloat16
F32 = jnp.float32
VMEM_LIMIT = 48 * 2**20


def split_np(table):
    high = table.astype(np.float32).astype(ml_dtypes.bfloat16)
    low = (table - high.astype(np.float64)).astype(np.float32).astype(ml_dtypes.bfloat16)
    return high, low


def make_tables(seq_len):
    outer = seq_len // LANES
    n_out, k_out = np.meshgrid(np.arange(outer), np.arange(outer), indexing="ij")
    head = np.exp(-2j * np.pi * (n_out * (4 * k_out + 1) % (4 * outer)) / (4 * outer))
    n_in = np.arange(LANES)
    twist = np.exp(-2j * np.pi * np.outer(4 * np.arange(outer) + 1, n_in) / (4 * seq_len))
    tail = np.exp(-2j * np.pi * (np.outer(n_in, n_in) % LANES) / LANES)

    def block(mat):
        return np.block([[mat.real, mat.imag], [-mat.imag, mat.real]])

    fwd_head = np.concatenate([head.real.T, head.imag.T], axis=0)
    high, low = split_np(fwd_head)
    head_tab = np.concatenate([high, high, low], axis=1)
    high, low = split_np(block(tail))
    tail_tab = np.concatenate([high, high, low], axis=0)
    high, low = split_np(block(tail.conj()))
    back_tail_tab = np.concatenate([high, high, low], axis=0)
    high, low = split_np(np.concatenate([head.real, head.imag], axis=1))
    back_head_tab = np.block([[high, high], [low, np.zeros_like(low)]])
    twist_tab = np.concatenate([twist.real, twist.imag], axis=1).astype(np.float32)
    return head_tab, twist_tab, tail_tab, back_tail_tab, back_head_tab


def halves(values):
    high = values.astype(BF16)
    return high, (values - high.astype(F32)).astype(BF16)


def by_rows(values):
    high, low = halves(values)
    return jnp.concatenate([high, low, high], axis=0)


def by_lanes(values):
    high, low = halves(values)
    return jnp.concatenate([high, low, high], axis=1)


def mat(left, right):
    return jnp.dot(left, right, preferred_element_type=F32)


def head_stage(signals, head, twist):
    outer = signals[0].shape[0]
    mixed = mat(head, by_rows(jnp.concatenate(signals, axis=1)))
    cos, sin = twist[:, :LANES], twist[:, LANES:]
    rows = []
    for idx in range(len(signals)):
        real = mixed[:outer, idx * LANES : (idx + 1) * LANES]
        imag = mixed[outer:, idx * LANES : (idx + 1) * LANES]
        rows.append(jnp.concatenate([real * cos - imag * sin, real * sin + imag * cos], axis=1))
    return jnp.concatenate(rows, axis=0)


def product_stage(spec, outer, groups):
    pieces = [spec[idx * outer : (idx + 1) * outer] for idx in range(spec.shape[0] // outer)]
    own = len(pieces) // (groups + 1)
    prods = []
    for idx, mine in enumerate(pieces[own:]):
        other = pieces[idx // groups]
        f_re, f_im = other[:, :LANES], other[:, LANES:]
        d_re, d_im = mine[:, :LANES], mine[:, LANES:]
        prods.append(jnp.concatenate([d_re * f_re - d_im * f_im, d_re * f_im + d_im * f_re], axis=1))
    return jnp.concatenate(prods, axis=0)


def back_stage(back, cos, sin):
    outer = cos.shape[0]
    reals, imags = [], []
    for idx in range(back.shape[0] // outer):
        mine = back[idx * outer : (idx + 1) * outer]
        real, imag = mine[:, :LANES], mine[:, LANES:]
        reals.append(real * cos + imag * sin)
        imags.append(imag * cos - real * sin)
    return jnp.concatenate([jnp.concatenate(reals, axis=1), jnp.concatenate(imags, axis=1)], axis=0)


def pack_kernel(layout, staged, where_ref, near_ref, key_ref, value_ref, filter_ref, bias_ref, out_ref, bias_out, key, value, taps, sems):
    rows, own, part, groups = layout
    count = out_ref.shape[0]
    blocks = count // groups
    homes = [
        ((peer % 2 ^ near_ref[0]) * (count // 2) + peer // 2 if staged else peer, peer * own)
        for peer in range(count)
    ]
    first = where_ref[0] * (part * LANES if part < rows else 0)
    taken = filter_ref.at[pl.ds(pl.multiple_of(first, part * LANES), part * LANES)]
    cuts = 1
    spans = [pl.ds(cut * rows // cuts * LANES, rows // cuts * LANES) for cut in range(cuts)]
    pairs = [(source.at[span], held.at[span]) for span in spans for source, held in ((key_ref, key), (value_ref, value))]
    pairs += [(taken, taps), (bias_ref, bias_out)]
    fetches = [pltpu.make_async_copy(*pair, sems.at[idx]) for idx, pair in enumerate(pairs)]
    for fetch in fetches:
        fetch.start()
    for row in range(rows):
        if row % (rows // cuts) == 0:
            for fetch in fetches[row // (rows // cuts) * 2 :][:2]:
                fetch.wait()
        span = pl.ds(row * LANES, LANES)
        turned = (key[span, :].astype(F32) * value[span, :].astype(F32)).T
        for place, chan in homes:
            out_ref[place, pl.ds(row, own, stride=rows), :] = turned[chan : chan + own]
    fetches[-2].wait()
    for row in range(part):
        turned = taps[pl.ds(row * LANES, LANES), :].T
        for place, chan in homes:
            out_ref[place, pl.ds(own * rows + row, own, stride=part), :] = turned[chan : chan + own]
    fetches[-1].wait()


def arrived(layout, staged, near, moved_ref, group, start, height):
    rows, own, part, groups = layout
    if staged:
        far, second = moved_ref.shape[0] // groups, start + own * (rows + part)
        span = pl.ds(group * far, far)
        ours, other = moved_ref[span, start : start + height], moved_ref[span, second : second + height]
        pair = [jnp.where(near == 0, ours, other), jnp.where(near == 0, other, ours)]
        return jnp.stack(pair, axis=1).reshape(2 * far, height, LANES)
    blocks = moved_ref.shape[0] // groups
    return moved_ref[pl.ds(group * blocks, blocks), start : start + height]


def driver_signals(layout, staged, near, moved_ref, chans):
    rows, own, part, groups = layout
    parts = [
        arrived(layout, staged, near, moved_ref, group, chan * rows, rows) for chan in chans for group in range(groups)
    ]
    return [values.reshape(values.shape[0] * rows, LANES) for values in parts]


def filter_signals(layout, staged, near, moved_ref, chans):
    rows, own, part, groups = layout
    signals = []
    for chan in chans:
        pieces = [
            arrived(layout, staged, near, moved_ref, group, own * rows + chan * part, part)
            for group in range(groups if part < rows else 1)
        ]
        signals.append(jnp.concatenate(pieces, axis=1).reshape(pieces[0].shape[0] * rows, LANES))
    return signals


def conv_kernel(
    layout, staged, pieces, near_ref, moved_ref, head_ref, twist_ref, tail_ref, back_tail_ref, back_head_ref, out_ref
):
    rows, own, part, groups = layout
    near = near_ref[0]
    blocks = out_ref.shape[0] // groups
    outer = blocks * rows
    scale = 1.0 / (outer * LANES)
    cos, sin = twist_ref[:, :LANES] * scale, twist_ref[:, LANES:] * scale
    sets = [range(piece * own // pieces, (piece + 1) * own // pieces) for piece in range(pieces)]
    mixed = [
        head_stage(
            filter_signals(layout, staged, near, moved_ref, chans) + driver_signals(layout, staged, near, moved_ref, chans),
            head_ref[...],
            twist_ref[...],
        )
        for chans in sets
    ]
    specs = [mat(by_lanes(values), tail_ref[...]) for values in mixed]
    prods = [product_stage(spec, outer, groups) for spec in specs]
    backs = [mat(by_lanes(values), back_tail_ref[...]) for values in prods]
    turned = [back_stage(back, cos, sin) for back in backs]
    results = [mat(back_head_ref[...], jnp.concatenate(halves(values), axis=0)) for values in turned]
    for chans, result in zip(sets, results):
        result = result[:outer] + result[outer:]
        for idx in range(len(chans) * groups):
            chan, group = divmod(idx, groups)
            start = (chans[0] + chan) * rows
            out_ref[pl.ds(group * blocks, blocks), start : start + rows] = result[
                :, idx * LANES : (idx + 1) * LANES
            ].reshape(blocks, rows, LANES)


def gate_kernel(rows, conv_ref, query_ref, key_ref, value_ref, bias_ref, out_ref, gated, sems):
    bias = bias_ref[...]
    half = rows * LANES // 2
    stores = [
        pltpu.make_async_copy(gated.at[pl.ds(idx * half, half)], out_ref.at[pl.ds(idx * half, half)], sems.at[idx])
        for idx in range(2)
    ]
    for row in range(rows):
        span = pl.ds(row * LANES, LANES)
        driver = key_ref[span, :].astype(F32) * value_ref[span, :].astype(F32)
        convolved = conv_ref[pl.ds(row, LANES, stride=rows), :].T
        gated[span, :] = (query_ref[span, :].astype(F32) * (convolved + bias * driver)).astype(BF16)
        if (row + 1) * LANES == half:
            stores[0].start()
    if rows % 2:
        stores[0].start()
    stores[1].start()
    for store in stores:
        store.wait()


VMEM = pl.BlockSpec(memory_space=pltpu.VMEM)
HBM = pl.BlockSpec(memory_space=pltpu.HBM)
SMEM = pl.BlockSpec(memory_space=pltpu.SMEM)


def call(kernel, outs, specs, flops, moved, scratch=()):
    return pl.pallas_call(
        kernel,
        out_shape=[jax.ShapeDtypeStruct(*out) for out in outs],
        in_specs=specs,
        out_specs=[VMEM] * len(outs),
        scratch_shapes=scratch,
        compiler_params=pltpu.CompilerParams(vmem_limit_bytes=VMEM_LIMIT),
        cost_estimate=pl.CostEstimate(flops=flops, bytes_accessed=moved, transcendentals=0),
    )


def convolve(groups, blocks, staged, query_proj, key_proj, value_proj, long_filter, skip_bias):
    tokens, chans = key_proj.shape
    rows = tokens // LANES
    count, axes = groups * blocks, ("groups", "seq")
    own = chans // count
    outer = blocks * rows
    seq_len = blocks * tokens
    part = rows // groups
    if rows % groups or own * part % 8:
        part = rows
    layout = (rows, own, part, groups)
    head, twist, tail, back_tail, back_head = (jnp.asarray(table) for table in make_tables(seq_len))
    size = tokens * chans * 4
    macs = 2 * 3 * own * seq_len * (2 * outer + 4 * LANES)
    where = lax.axis_index("groups").reshape(1).astype(jnp.int32)
    near = (lax.axis_index("seq") % 2).reshape(1).astype(jnp.int32)

    def exchange(array):
        return lax.all_to_all(array, axes, 0, 0, tiled=True)

    sources = (key_proj, value_proj, long_filter, skip_bias.reshape(1, chans))
    packed, bias = call(
        functools.partial(pack_kernel, layout, staged),
        [((count, own * (rows + part), LANES), F32), ((1, chans), F32)],
        [SMEM] * 2 + [HBM] * 4, size // 4, size * 3,
        [pltpu.VMEM((tokens, chans), BF16), pltpu.VMEM((tokens, chans), BF16), pltpu.VMEM((part * LANES, chans), F32),
         pltpu.SemaphoreType.DMA((6,))],
    )(where, near, *(pltpu.with_memory_space_constraint(source, pltpu.HBM) for source in sources))
    if staged:
        kept, sent = packed[: count // 2], packed[count // 2 :]
        swap = [(block, block ^ 1) for block in range(blocks)]
        pair = jnp.concatenate([kept, lax.ppermute(sent, "seq", swap)], axis=1)
        sides = [list(range(side, count, 2)) for side in range(2)]
        moved = lax.all_to_all(pair, axes, 0, 0, axis_index_groups=sides, tiled=True)
    else:
        moved = exchange(packed)
    local = call(
        functools.partial(conv_kernel, layout, staged, min(own, 2)),
        [((count, own * rows, LANES), F32)], [SMEM] + [VMEM] * 6, 5 * macs, 3 * size,
    )(near, moved, head, twist, tail, back_tail, back_head)[0]
    convolved = exchange(local).reshape(chans * rows, LANES)
    return pl.pallas_call(
        functools.partial(gate_kernel, rows),
        out_shape=pltpu.HBM((tokens, chans), BF16),
        in_specs=[VMEM] * 5,
        out_specs=HBM,
        scratch_shapes=[pltpu.VMEM((tokens, chans), BF16), pltpu.SemaphoreType.DMA((2,))],
        compiler_params=pltpu.CompilerParams(vmem_limit_bytes=VMEM_LIMIT),
        cost_estimate=pl.CostEstimate(flops=size, bytes_accessed=3 * size, transcendentals=0),
    )(convolved, query_proj, key_proj, value_proj, bias)


def shards(groups, blocks, cores, *args):
    if cores == 1 or blocks % 2:
        return convolve(groups, blocks, False, *args)
    return lax.cond(
        lax.axis_index("chan") % 2 == 1,
        functools.partial(convolve, groups, blocks, False),
        functools.partial(convolve, groups, blocks, True),
        *args,
    )


def solution(mesh):
    placed = (
        P(("groups", "seq"), "chan"),
        P(("groups", "seq"), "chan"),
        P(("groups", "seq"), "chan"),
        P("seq", "chan"),
        P("chan"),
    )
    body = functools.partial(shards, *(mesh.shape[axis] for axis in ("groups", "seq", "chan")))
    return jax.shard_map(
        body, mesh=mesh, in_specs=placed, out_specs=P(("groups", "seq"), "chan"), check_vma=False
    )
```

```python
import functools

import jax
import jax.numpy as jnp
import ml_dtypes
import numpy as np
from jax import lax
from jax.experimental import pallas as pl
from jax.experimental.pallas import tpu as pltpu
from jax.sharding import PartitionSpec as P

LANES = 128
BF16 = jnp.bfloat16
F32 = jnp.float32
VMEM_LIMIT = 48 * 2**20


def split_np(table):
    high = table.astype(np.float32).astype(ml_dtypes.bfloat16)
    low = (table - high.astype(np.float64)).astype(np.float32).astype(ml_dtypes.bfloat16)
    return high, low


def make_tables(seq_len):
    outer = seq_len // LANES
    n_out, k_out = np.meshgrid(np.arange(outer), np.arange(outer), indexing="ij")
    head = np.exp(-2j * np.pi * (n_out * (4 * k_out + 1) % (4 * outer)) / (4 * outer))
    n_in = np.arange(LANES)
    twist = np.exp(-2j * np.pi * np.outer(4 * np.arange(outer) + 1, n_in) / (4 * seq_len))
    tail = np.exp(-2j * np.pi * (np.outer(n_in, n_in) % LANES) / LANES)

    def block(mat):
        return np.block([[mat.real, mat.imag], [-mat.imag, mat.real]])

    fwd_head = np.concatenate([head.real.T, head.imag.T], axis=0)
    high, low = split_np(fwd_head)
    head_tab = np.concatenate([high, high, low], axis=1)
    high, low = split_np(block(tail))
    tail_tab = np.concatenate([high, high, low], axis=0)
    high, low = split_np(block(tail.conj()))
    back_tail_tab = np.concatenate([high, high, low], axis=0)
    high, low = split_np(np.concatenate([head.real, head.imag], axis=1))
    back_head_tab = np.block([[high, high], [low, np.zeros_like(low)]])
    twist_tab = np.concatenate([twist.real, twist.imag], axis=1).astype(np.float32)
    return head_tab, twist_tab, tail_tab, back_tail_tab, back_head_tab


def halves(values):
    high = values.astype(BF16)
    return high, (values - high.astype(F32)).astype(BF16)


def by_rows(values):
    high, low = halves(values)
    return jnp.concatenate([high, low, high], axis=0)


def by_lanes(values):
    high, low = halves(values)
    return jnp.concatenate([high, low, high], axis=1)


def mat(left, right):
    return jnp.dot(left, right, preferred_element_type=F32)


def head_stage(signals, head, twist):
    outer = signals[0].shape[0]
    mixed = mat(head, by_rows(jnp.concatenate(signals, axis=1)))
    cos, sin = twist[:, :LANES], twist[:, LANES:]
    rows = []
    for idx in range(len(signals)):
        real = mixed[:outer, idx * LANES : (idx + 1) * LANES]
        imag = mixed[outer:, idx * LANES : (idx + 1) * LANES]
        rows.append(jnp.concatenate([real * cos - imag * sin, real * sin + imag * cos], axis=1))
    return jnp.concatenate(rows, axis=0)


def product_stage(spec, outer, groups):
    pieces = [spec[idx * outer : (idx + 1) * outer] for idx in range(spec.shape[0] // outer)]
    own = len(pieces) // (groups + 1)
    prods = []
    for idx, mine in enumerate(pieces[own:]):
        other = pieces[idx // groups]
        f_re, f_im = other[:, :LANES], other[:, LANES:]
        d_re, d_im = mine[:, :LANES], mine[:, LANES:]
        prods.append(jnp.concatenate([d_re * f_re - d_im * f_im, d_re * f_im + d_im * f_re], axis=1))
    return jnp.concatenate(prods, axis=0)


def back_stage(back, cos, sin):
    outer = cos.shape[0]
    reals, imags = [], []
    for idx in range(back.shape[0] // outer):
        mine = back[idx * outer : (idx + 1) * outer]
        real, imag = mine[:, :LANES], mine[:, LANES:]
        reals.append(real * cos + imag * sin)
        imags.append(imag * cos - real * sin)
    return jnp.concatenate([jnp.concatenate(reals, axis=1), jnp.concatenate(imags, axis=1)], axis=0)


def pack_kernel(layout, staged, where_ref, near_ref, key_ref, value_ref, filter_ref, bias_ref, out_ref, bias_out, key, value, taps, sems):
    rows, own, part, groups = layout
    count = out_ref.shape[0]
    blocks = count // groups
    homes = [
        ((peer % 2 ^ near_ref[0]) * (count // 2) + peer // 2 if staged else peer, peer * own)
        for peer in range(count)
    ]
    first = where_ref[0] * (part * LANES if part < rows else 0)
    taken = filter_ref.at[pl.ds(pl.multiple_of(first, part * LANES), part * LANES)]
    cuts = 2 if rows % 2 == 0 else 1
    spans = [pl.ds(cut * rows // cuts * LANES, rows // cuts * LANES) for cut in range(cuts)]
    pairs = [(source.at[span], held.at[span]) for span in spans for source, held in ((key_ref, key), (value_ref, value))]
    pairs = [(taken, taps)] + pairs + [(bias_ref, bias_out)]
    fetches = [pltpu.make_async_copy(*pair, sems.at[idx]) for idx, pair in enumerate(pairs)]
    for fetch in fetches:
        fetch.start()
    fetches[0].wait()
    for row in range(part):
        turned = taps[pl.ds(row * LANES, LANES), :].T
        for place, chan in homes:
            out_ref[place, pl.ds(own * rows + row, own, stride=part), :] = turned[chan : chan + own]
    for row in range(rows):
        if row % (rows // cuts) == 0:
            for fetch in fetches[1 + row // (rows // cuts) * 2 :][:2]:
                fetch.wait()
        span = pl.ds(row * LANES, LANES)
        turned = (key[span, :].astype(F32) * value[span, :].astype(F32)).T
        for place, chan in homes:
            out_ref[place, pl.ds(row, own, stride=rows), :] = turned[chan : chan + own]
    fetches[-1].wait()


def arrived(layout, staged, near, moved_ref, group, start, height):
    rows, own, part, groups = layout
    if staged:
        far, second = moved_ref.shape[0] // groups, start + own * (rows + part)
        span = pl.ds(group * far, far)
        ours, other = moved_ref[span, start : start + height], moved_ref[span, second : second + height]
        pair = [jnp.where(near == 0, ours, other), jnp.where(near == 0, other, ours)]
        return jnp.stack(pair, axis=1).reshape(2 * far, height, LANES)
    blocks = moved_ref.shape[0] // groups
    return moved_ref[pl.ds(group * blocks, blocks), start : start + height]


def driver_signals(layout, staged, near, moved_ref, chans):
    rows, own, part, groups = layout
    parts = [
        arrived(layout, staged, near, moved_ref, group, chan * rows, rows) for chan in chans for group in range(groups)
    ]
    return [values.reshape(values.shape[0] * rows, LANES) for values in parts]


def filter_signals(layout, staged, near, moved_ref, chans):
    rows, own, part, groups = layout
    signals = []
    for chan in chans:
        pieces = [
            arrived(layout, staged, near, moved_ref, group, own * rows + chan * part, part)
            for group in range(groups if part < rows else 1)
        ]
        signals.append(jnp.concatenate(pieces, axis=1).reshape(pieces[0].shape[0] * rows, LANES))
    return signals


def conv_kernel(
    layout, staged, pieces, near_ref, moved_ref, head_ref, twist_ref, tail_ref, back_tail_ref, back_head_ref, out_ref
):
    rows, own, part, groups = layout
    near = near_ref[0]
    blocks = out_ref.shape[0] // groups
    outer = blocks * rows
    scale = 1.0 / (outer * LANES)
    cos, sin = twist_ref[:, :LANES] * scale, twist_ref[:, LANES:] * scale
    sets = [range(piece * own // pieces, (piece + 1) * own // pieces) for piece in range(pieces)]
    mixed = [
        head_stage(
            filter_signals(layout, staged, near, moved_ref, chans) + driver_signals(layout, staged, near, moved_ref, chans),
            head_ref[...],
            twist_ref[...],
        )
        for chans in sets
    ]
    specs = [mat(by_lanes(values), tail_ref[...]) for values in mixed]
    prods = [product_stage(spec, outer, groups) for spec in specs]
    backs = [mat(by_lanes(values), back_tail_ref[...]) for values in prods]
    turned = [back_stage(back, cos, sin) for back in backs]
    results = [mat(back_head_ref[...], jnp.concatenate(halves(values), axis=0)) for values in turned]
    for chans, result in zip(sets, results):
        result = result[:outer] + result[outer:]
        for idx in range(len(chans) * groups):
            chan, group = divmod(idx, groups)
            start = (chans[0] + chan) * rows
            out_ref[pl.ds(group * blocks, blocks), start : start + rows] = result[
                :, idx * LANES : (idx + 1) * LANES
            ].reshape(blocks, rows, LANES)


def gate_kernel(rows, conv_ref, query_ref, key_ref, value_ref, bias_ref, out_ref, gated, sems):
    bias = bias_ref[...]
    half = rows * LANES // 2
    stores = [
        pltpu.make_async_copy(gated.at[pl.ds(idx * half, half)], out_ref.at[pl.ds(idx * half, half)], sems.at[idx])
        for idx in range(2)
    ]
    for row in range(rows):
        span = pl.ds(row * LANES, LANES)
        driver = key_ref[span, :].astype(F32) * value_ref[span, :].astype(F32)
        convolved = conv_ref[pl.ds(row, LANES, stride=rows), :].T
        gated[span, :] = (query_ref[span, :].astype(F32) * (convolved + bias * driver)).astype(BF16)
        if (row + 1) * LANES == half:
            stores[0].start()
    if rows % 2:
        stores[0].start()
    stores[1].start()
    for store in stores:
        store.wait()


VMEM = pl.BlockSpec(memory_space=pltpu.VMEM)
HBM = pl.BlockSpec(memory_space=pltpu.HBM)
SMEM = pl.BlockSpec(memory_space=pltpu.SMEM)


def call(kernel, outs, specs, flops, moved, scratch=()):
    return pl.pallas_call(
        kernel,
        out_shape=[jax.ShapeDtypeStruct(*out) for out in outs],
        in_specs=specs,
        out_specs=[VMEM] * len(outs),
        scratch_shapes=scratch,
        compiler_params=pltpu.CompilerParams(vmem_limit_bytes=VMEM_LIMIT),
        cost_estimate=pl.CostEstimate(flops=flops, bytes_accessed=moved, transcendentals=0),
    )


def convolve(groups, blocks, staged, query_proj, key_proj, value_proj, long_filter, skip_bias):
    tokens, chans = key_proj.shape
    rows = tokens // LANES
    count, axes = groups * blocks, ("groups", "seq")
    own = chans // count
    outer = blocks * rows
    seq_len = blocks * tokens
    part = rows // groups
    if rows % groups or own * part % 8:
        part = rows
    layout = (rows, own, part, groups)
    head, twist, tail, back_tail, back_head = (jnp.asarray(table) for table in make_tables(seq_len))
    size = tokens * chans * 4
    macs = 2 * 3 * own * seq_len * (2 * outer + 4 * LANES)
    where = lax.axis_index("groups").reshape(1).astype(jnp.int32)
    near = (lax.axis_index("seq") % 2).reshape(1).astype(jnp.int32)

    def exchange(array):
        return lax.all_to_all(array, axes, 0, 0, tiled=True)

    sources = (key_proj, value_proj, long_filter, skip_bias.reshape(1, chans))
    packed, bias = call(
        functools.partial(pack_kernel, layout, staged),
        [((count, own * (rows + part), LANES), F32), ((1, chans), F32)],
        [SMEM] * 2 + [HBM] * 4, size // 4, size * 3,
        [pltpu.VMEM((tokens, chans), BF16), pltpu.VMEM((tokens, chans), BF16), pltpu.VMEM((part * LANES, chans), F32),
         pltpu.SemaphoreType.DMA((6,))],
    )(where, near, *(pltpu.with_memory_space_constraint(source, pltpu.HBM) for source in sources))
    if staged:
        kept, sent = packed[: count // 2], packed[count // 2 :]
        swap = [(block, block ^ 1) for block in range(blocks)]
        pair = jnp.concatenate([kept, lax.ppermute(sent, "seq", swap)], axis=1)
        sides = [list(range(side, count, 2)) for side in range(2)]
        moved = lax.all_to_all(pair, axes, 0, 0, axis_index_groups=sides, tiled=True)
    else:
        moved = exchange(packed)
    local = call(
        functools.partial(conv_kernel, layout, staged, min(own, 4)),
        [((count, own * rows, LANES), F32)], [SMEM] + [VMEM] * 6, 5 * macs, 3 * size,
    )(near, moved, head, twist, tail, back_tail, back_head)[0]
    convolved = exchange(local).reshape(chans * rows, LANES)
    return pl.pallas_call(
        functools.partial(gate_kernel, rows),
        out_shape=pltpu.HBM((tokens, chans), BF16),
        in_specs=[VMEM] * 5,
        out_specs=HBM,
        scratch_shapes=[pltpu.VMEM((tokens, chans), BF16), pltpu.SemaphoreType.DMA((2,))],
        compiler_params=pltpu.CompilerParams(vmem_limit_bytes=VMEM_LIMIT),
        cost_estimate=pl.CostEstimate(flops=size, bytes_accessed=3 * size, transcendentals=0),
    )(convolved, query_proj, key_proj, value_proj, bias)


def shards(groups, blocks, cores, *args):
    if cores == 1 or blocks % 2:
        return convolve(groups, blocks, False, *args)
    return lax.cond(
        lax.axis_index("chan") % 2 == 1,
        functools.partial(convolve, groups, blocks, False),
        functools.partial(convolve, groups, blocks, True),
        *args,
    )


def solution(mesh):
    placed = (
        P(("groups", "seq"), "chan"),
        P(("groups", "seq"), "chan"),
        P(("groups", "seq"), "chan"),
        P("seq", "chan"),
        P("chan"),
    )
    body = functools.partial(shards, *(mesh.shape[axis] for axis in ("groups", "seq", "chan")))
    return jax.shard_map(
        body, mesh=mesh, in_specs=placed, out_specs=P(("groups", "seq"), "chan"), check_vma=False
    )
```
